32 devices in a mesh: wide: 8 (over z, core), narrow: 4 (over y, x).
Axes of the slice: x: 2, y: 2, z: 4, core: 2. Of those that a mesh axis runs over, the one named last changes fastest.
Arguments:
- density: float32 [2, 1, 4096, 4096], P(None, None, 'narrow', 'wide'), may hold values from -6 to 6
- plane_wave: int32 [1], replicated, may hold values from 1 to 4
Outputs:
- potential: float32 [2, 1, 4096, 4096], P(None, None, 'narrow', 'wide')
The draws below stay inside these ranges and needn't reach their ends.
All inputs are finite; a program needn't handle non-finite values.
Results may differ from the reference program's by a relative error of at most 0.000073.
Values sent between devices are 32-bit elements; how exact they have to be, the bound alone decides.
No kernel may reach another device: no remote copies, remote signals or barrier semaphores. Data moves between devices by JAX's collectives and lax.ppermute only.
A program may use at most 128 MiB of HBM per device.

```python
import jax
import jax.numpy as jnp

NX = 4096
NZ = 4096
YP = 1
SCREEN = 1024
AMP = 2048


def level_of(key, shape, shards, smallest, largest):
    loudness, own = 1.0, jax.random.fold_in(key, 6)
    for dim, parts in shards:
        steps = jnp.exp(jax.random.uniform(jax.random.fold_in(own, dim), (parts,), jnp.float32, smallest / len(shards), largest / len(shards)))
        loudness = loudness * jnp.repeat(steps, shape[dim] // parts).reshape([-1 if axis == dim else 1 for axis in range(len(shape))])
    return loudness


def centred(own_key, shape, scale, limit, shards=(), held_as=jnp.bfloat16):
    factor_of = level_of(own_key, shape, shards, -0.22, 0.18) if shards else 1.0
    array = jax.random.normal(own_key, shape, jnp.float32) * scale * factor_of
    return jnp.minimum(jnp.maximum(array, -limit), limit).astype(held_as)


def setup_inputs(seed: int = 0) -> dict:
    key_of = jax.random.split(jax.random.key(seed), 3)
    return {
        "density": centred(key_of[0], (2, YP, NZ, NX), 1.0, 6.0, ((2, 4), (3, 8)), jnp.float32),
        "plane_wave": jax.random.randint(key_of[1], (YP,), 1, 5).astype(jnp.int32),
    }


def reference(density, plane_wave):
    field = density[0] + 1j * density[1]
    spectrum = jnp.fft.fft2(field, axes=(1, 2))
    wave_z = jnp.arange(NZ, dtype=jnp.int32)
    wave_z = jnp.where(wave_z < NZ // 2, wave_z, wave_z - NZ)
    wave_x = jnp.arange(NX, dtype=jnp.int32)
    wave_x = jnp.where(wave_x < NX // 2, wave_x, wave_x - NX)
    square = wave_z[None, :, None] ** 2 + plane_wave[:, None, None] ** 2 + wave_x[None, None, :] ** 2
    square = square.astype(jnp.float32)
    green = 1.0 / (1.0 + square / float(SCREEN * SCREEN)) + float(AMP) / (square + 1.0)
    result = jnp.fft.ifft2(spectrum * green, axes=(1, 2))
    return jnp.stack([jnp.real(result), jnp.imag(result)]).astype(jnp.float32)
```

```python
import functools
import math

import jax
import jax.numpy as jnp
import numpy as np
from jax import lax
from jax.experimental import pallas as pl
from jax.experimental.pallas import tpu as pltpu
from jax.sharding import PartitionSpec as P

SCREEN = 1024
AMP = 2048
LANES = 128
VMEM_LIMIT = 48 * 1024 * 1024


def split_bf16(value):
    high = np.asarray(value, np.float64).astype(np.float32).astype(jnp.bfloat16)
    low = (value - high.astype(np.float64)).astype(np.float32).astype(jnp.bfloat16)
    return high, low


def dft_matrix(length, orient, left):
    index = np.arange(length)
    angle = 2.0 * np.pi * ((index[:, None] * index[None, :]) % length) / length
    cosine, sine = np.cos(angle), orient * np.sin(angle)
    if left:
        whole = np.block([[cosine, -sine], [sine, cosine]])
    else:
        whole = np.block([[cosine, sine], [-sine, cosine]])
    high, low = split_bf16(whole)
    return np.stack([high, low])


def turn(numerator, length):
    angle = (numerator % length).astype(jnp.float32) * (2.0 * math.pi / length)
    return jnp.cos(angle), -jnp.sin(angle)


def c_add(a, b):
    return (a[0] + b[0], a[1] + b[1])


def c_sub(a, b):
    return (a[0] - b[0], a[1] - b[1])


def c_mul(a, b):
    return (a[0] * b[0] - a[1] * b[1], a[0] * b[1] + a[1] * b[0])


def c_const(a, numerator, length, orient):
    numerator = (orient * numerator) % length
    if numerator == 0:
        return a
    if 2 * numerator == length:
        return (-a[0], -a[1])
    if 4 * numerator == length:
        return (-a[1], a[0])
    if 4 * numerator == 3 * length:
        return (a[1], -a[0])
    angle = 2.0 * math.pi * numerator / length
    cosine, sine = math.cos(angle), math.sin(angle)
    if 8 * numerator % length == 0:
        root = math.sqrt(0.5)
        total, differ = (a[0] + a[1]) * root, (a[0] - a[1]) * root
        if cosine > 0 and sine > 0:
            return (differ, total)
        if cosine > 0:
            return (total, -differ)
        if sine > 0:
            return (-total, differ)
        return (-differ, -total)
    return (a[0] * cosine - a[1] * sine, a[0] * sine + a[1] * cosine)


def small_dft(values, orient):
    count = len(values)
    if count == 1:
        return values
    half = count // 2
    upper = [c_add(values[i], values[i + half]) for i in range(half)]
    lower = [
        c_const(c_sub(values[i], values[i + half]), i, count, orient) for i in range(half)
    ]
    even, odd = small_dft(upper, orient), small_dft(lower, orient)
    result = []
    for i in range(half):
        result += [even[i], odd[i]]
    return result


def dot3(high, low, value, left):
    value_high = value.astype(jnp.bfloat16)
    value_low = (value - value_high.astype(jnp.float32)).astype(jnp.bfloat16)
    dot = functools.partial(jnp.dot, preferred_element_type=jnp.float32)
    if left:
        return dot(high, value_high) + (dot(high, value_low) + dot(low, value_high))
    return dot(value_high, high) + (dot(value_low, high) + dot(value_high, low))


def z_forward_kernel(terms, parts, slots, rows, coef_ref, matrix_ref, turn_ref, *refs):
    inputs = refs[: terms * parts]
    outputs = refs[terms * parts : terms * parts + slots]
    held = refs[-1]
    per_part = slots // parts
    tile = min(rows, 8)

    def step(index, carry):
        row = pl.multiple_of(index * tile, tile)
        values = []
        for h in range(slots):
            part, inner = divmod(h, per_part)
            total = None
            for term in range(terms):
                ref = inputs[part * terms + term]
                place = pl.ds(inner * rows + row, tile)
                value = (ref[0, place, :], ref[1, place, :])
                scale = (coef_ref[h, 2 * term], coef_ref[h, 2 * term + 1])
                product = c_mul(value, scale)
                total = product if total is None else c_add(total, product)
            values.append(total)
        values = small_dft(values, 1)
        for k in range(slots):
            twiddle = (
                turn_ref[k, 0, pl.ds(row, tile), :],
                turn_ref[k, 1, pl.ds(row, tile), :],
            )
            real_part, imag_part = c_mul(values[k], twiddle)
            held[pl.ds(row, tile), k * LANES : (k + 1) * LANES] = real_part
            held[pl.ds(rows + row, tile), k * LANES : (k + 1) * LANES] = imag_part
        return carry

    lax.fori_loop(0, rows // tile, step, 0)
    result = dot3(matrix_ref[0], matrix_ref[1], held[...], True)
    for k in range(slots):
        outputs[k][0] = result[:rows, k * LANES : (k + 1) * LANES]
        outputs[k][1] = result[rows:, k * LANES : (k + 1) * LANES]


def z_forward(parts, coef, turns, slots, rows):
    terms = len(parts[0])
    flat = [array for part in parts for array in part]
    matrix = jnp.asarray(dft_matrix(rows, -1, True))
    vmem = pl.BlockSpec(memory_space=pltpu.VMEM)
    return pl.pallas_call(
        functools.partial(z_forward_kernel, terms, len(parts), slots, rows),
        out_shape=[jax.ShapeDtypeStruct((2, rows, LANES), jnp.float32)] * slots,
        in_specs=[pl.BlockSpec(memory_space=pltpu.SMEM)] + [vmem] * (2 + len(flat)),
        out_specs=[vmem] * slots,
        scratch_shapes=[pltpu.VMEM((2 * rows, slots * LANES), jnp.float32)],
        compiler_params=pltpu.CompilerParams(vmem_limit_bytes=VMEM_LIMIT),
        cost_estimate=pl.CostEstimate(
            flops=12 * rows * rows * slots * LANES, bytes_accessed=32 * rows * slots * LANES, transcendentals=0
        ),
        name="z_forward",
    )(coef, matrix, turns, *flat)


def z_inverse_kernel(parts, slots, rows, coef_ref, matrix_ref, turn_ref, *refs):
    inputs = refs[:slots]
    outputs = refs[slots : slots + parts]
    held = refs[-1]
    per_part = slots // parts
    tile = min(rows, 8)
    for k in range(slots):
        held[:rows, k * LANES : (k + 1) * LANES] = inputs[k][0]
        held[rows:, k * LANES : (k + 1) * LANES] = inputs[k][1]
    held[...] = dot3(matrix_ref[0], matrix_ref[1], held[...], True)

    def step(index, carry):
        row = pl.multiple_of(index * tile, tile)
        values = []
        for k in range(slots):
            value = (
                held[pl.ds(row, tile), k * LANES : (k + 1) * LANES],
                held[pl.ds(rows + row, tile), k * LANES : (k + 1) * LANES],
            )
            twiddle = (
                turn_ref[k, 0, pl.ds(row, tile), :],
                -turn_ref[k, 1, pl.ds(row, tile), :],
            )
            values.append(c_mul(value, twiddle))
        values = small_dft(values, -1)
        for h in range(slots):
            part, inner = divmod(h, per_part)
            real_part, imag_part = c_mul(values[h], (coef_ref[h, 0], coef_ref[h, 1]))
            outputs[part][0, pl.ds(inner * rows + row, tile), :] = real_part
            outputs[part][1, pl.ds(inner * rows + row, tile), :] = imag_part
        return carry

    lax.fori_loop(0, rows // tile, step, 0)


def z_inverse(blocks, coef, turns, parts):
    slots, rows = len(blocks), blocks[0].shape[1]
    matrix = jnp.asarray(dft_matrix(rows, 1, True))
    vmem = pl.BlockSpec(memory_space=pltpu.VMEM)
    return pl.pallas_call(
        functools.partial(z_inverse_kernel, parts, slots, rows),
        out_shape=[jax.ShapeDtypeStruct((2, slots // parts * rows, LANES), jnp.float32)] * parts,
        in_specs=[pl.BlockSpec(memory_space=pltpu.SMEM)] + [vmem] * (2 + slots),
        out_specs=[vmem] * parts,
        scratch_shapes=[pltpu.VMEM((2 * rows, slots * LANES), jnp.float32)],
        compiler_params=pltpu.CompilerParams(vmem_limit_bytes=VMEM_LIMIT),
        cost_estimate=pl.CostEstimate(
            flops=12 * rows * rows * slots * LANES, bytes_accessed=20 * rows * slots * LANES, transcendentals=0
        ),
        name="z_inverse",
    )(coef, matrix, turns, *blocks)


def x_filter_kernel(slots, chunks, rows, coef_ref, forward_ref, inverse_ref, turn_ref, green_ref, *refs):
    blocks = slots * chunks
    inputs = refs[:blocks]
    outputs = refs[blocks : 2 * blocks]
    held = refs[-1]
    tile = 8

    def before(index, carry):
        row = pl.multiple_of(index * tile, tile)
        place = pl.ds(row, tile)
        columns = []
        for c in range(chunks):
            values = [
                (inputs[c * slots + k][0, place, :], inputs[c * slots + k][1, place, :])
                for k in range(slots)
            ]
            values = small_dft(values, -1)
            columns.append(
                [
                    c_mul(values[a], (coef_ref[a * chunks + c, 0], coef_ref[a * chunks + c, 1]))
                    for a in range(slots)
                ]
            )
        for a in range(slots):
            values = small_dft([columns[c][a] for c in range(chunks)], -1)
            for b in range(chunks):
                mode = a + slots * b
                twiddle = (turn_ref[0, mode : mode + 1, :], turn_ref[1, mode : mode + 1, :])
                real_part, imag_part = c_mul(values[b], twiddle)
                held[mode, place, :LANES] = real_part
                held[mode, place, LANES:] = imag_part
        return carry

    lax.fori_loop(0, rows // tile, before, 0)

    group = max(1, min(blocks, 256 // rows))

    def middle(index, carry):
        mode = pl.multiple_of(index * group, group)
        value = held[pl.ds(mode, group)].reshape(group * rows, 2 * LANES)
        value = dot3(forward_ref[0], forward_ref[1], value, False)
        green = green_ref[pl.ds(mode, group)].reshape(group * rows, LANES)
        value = value * jnp.concatenate([green, green], axis=1)
        value = dot3(inverse_ref[0], inverse_ref[1], value, False)
        held[pl.ds(mode, group)] = value.reshape(group, rows, 2 * LANES)
        return carry

    lax.fori_loop(0, blocks // group, middle, 0)

    def after(index, carry):
        row = pl.multiple_of(index * tile, tile)
        place = pl.ds(row, tile)
        columns = []
        for a in range(slots):
            values = []
            for b in range(chunks):
                mode = a + slots * b
                twiddle = (turn_ref[0, mode : mode + 1, :], -turn_ref[1, mode : mode + 1, :])
                values.append(c_mul((held[mode, place, :LANES], held[mode, place, LANES:]), twiddle))
            columns.append(small_dft(values, 1))
        for c in range(chunks):
            values = [
                c_mul(columns[a][c], (coef_ref[a * chunks + c, 0], -coef_ref[a * chunks + c, 1]))
                for a in range(slots)
            ]
            values = small_dft(values, 1)
            for k in range(slots):
                outputs[c * slots + k][0, place, :] = values[k][0]
                outputs[c * slots + k][1, place, :] = values[k][1]
        return carry

    lax.fori_loop(0, rows // tile, after, 0)


def x_filter(blocks, coef, turns, green, slots, chunks):
    rows = blocks[0].shape[1]
    step = min(rows, 32)
    count = slots * chunks
    forward = jnp.asarray(dft_matrix(LANES, -1, False))
    inverse = jnp.asarray(dft_matrix(LANES, 1, False))
    whole = pl.BlockSpec((2, 2 * LANES, 2 * LANES), lambda i: (0, 0, 0))
    block = pl.BlockSpec((2, step, LANES), lambda i: (0, i, 0))
    return pl.pallas_call(
        functools.partial(x_filter_kernel, slots, chunks, step),
        grid=(rows // step,),
        out_shape=[jax.ShapeDtypeStruct((2, rows, LANES), jnp.float32)] * count,
        in_specs=[
            pl.BlockSpec(memory_space=pltpu.SMEM),
            whole,
            whole,
            pl.BlockSpec((2, count, LANES), lambda i: (0, 0, 0)),
            pl.BlockSpec((count, step, LANES), lambda i: (0, i, 0)),
        ]
        + [block] * count,
        out_specs=[block] * count,
        scratch_shapes=[pltpu.VMEM((count, step, 2 * LANES), jnp.float32)],
        compiler_params=pltpu.CompilerParams(vmem_limit_bytes=VMEM_LIMIT),
        cost_estimate=pl.CostEstimate(
            flops=24 * LANES * LANES * 4 * count * rows, bytes_accessed=20 * count * rows * LANES, transcendentals=0
        ),
        name="x_filter",
    )(coef, forward, inverse, turns, green, *blocks)


def finish_kernel(terms, parts, coef_ref, *refs):
    inputs = refs[: terms * parts]
    out_ref = refs[-1]
    for part in range(parts):
        rows = inputs[part * terms].shape[1]
        total = None
        for term in range(terms):
            ref = inputs[part * terms + term]
            product = c_mul(
                (ref[0], ref[1]), (coef_ref[part, 2 * term], coef_ref[part, 2 * term + 1])
            )
            total = product if total is None else c_add(total, product)
        out_ref[0, part * rows : (part + 1) * rows, :] = total[0]
        out_ref[1, part * rows : (part + 1) * rows, :] = total[1]


def finish(parts, coef, chunk, chunks, so_far):
    terms = len(parts[0])
    flat = [array for part in parts for array in part]
    rows = sum(part[0].shape[1] for part in parts)
    step = 1
    vmem = [pl.BlockSpec(array.shape, lambda i: (0, 0, 0)) for array in flat]
    extra = [] if so_far is None else [so_far]
    return pl.pallas_call(
        functools.partial(finish_kernel, terms, len(parts)),
        grid=(step,),
        out_shape=jax.ShapeDtypeStruct((2, rows, chunks * LANES), jnp.float32),
        in_specs=[pl.BlockSpec(memory_space=pltpu.SMEM)]
        + vmem
        + [pl.BlockSpec(memory_space=pl.ANY)] * len(extra),
        out_specs=pl.BlockSpec((2, rows, LANES), lambda i: (0, 0, chunk)),
        input_output_aliases={1 + len(flat): 0} if extra else {},
        compiler_params=pltpu.CompilerParams(vmem_limit_bytes=VMEM_LIMIT),
        cost_estimate=pl.CostEstimate(
            flops=20 * rows * LANES, bytes_accessed=32 * rows * LANES, transcendentals=0
        ),
        name="finish",
    )(coef, *flat, *extra)


def swap(value, axis, mask):
    pairs = [(source, source ^ mask) for source in range(lax.axis_size(axis))]
    return lax.ppermute(value, axis, pairs)


def shift(value, axis, distance):
    size = lax.axis_size(axis)
    pairs = [(source, (source + distance) % size) for source in range(size)]
    return lax.ppermute(value, axis, pairs)


def mix(array, other, first, second):
    a = c_mul((array[0], array[1]), first)
    b = c_mul((other[0], other[1]), second)
    return jnp.stack(c_add(a, b))


def quarter(target, source, orient):
    step = target * source % 4
    real_part = jnp.where(step == 0, 1.0, jnp.where(step == 2, -1.0, 0.0))
    imag_part = jnp.where(step == 1, -1.0, jnp.where(step == 3, 1.0, 0.0))
    return (real_part, imag_part * orient)


def four_way(array, device, first, orient):
    second = 3 - first
    partner = swap(array, "narrow", first)
    there = device ^ second
    sent = mix(
        array,
        partner,
        quarter(there, device, orient),
        quarter(there, device ^ first, orient),
    )
    received = swap(sent, "narrow", second)
    return [array, partner, received]


def four_way_coef(device, first, orient):
    return [
        quarter(device, device, orient),
        quarter(device, device ^ first, orient),
        (jnp.float32(1.0), jnp.float32(0.0)),
    ]


def reversed_index(device, bit_count):
    result = jnp.int32(0)
    for level in range(bit_count):
        result = result + device // (1 << level) % 2 * (1 << bit_count - 1 - level)
    return result


def rotate(field, phase_angle, orient):
    return jnp.stack(
        c_mul((field[0], field[1]), (jnp.cos(phase_angle), -orient * jnp.sin(phase_angle)))
    )


def butterfly_forward(field, device, bit_count):
    for level in reversed(range(bit_count)):
        half_size = 1 << level
        partner = swap(field, "narrow", half_size)
        upper = device // half_size % 2
        phase_angle = (device % half_size).astype(jnp.float32) * (math.pi / half_size)
        field = jnp.where(upper == 0, field + partner, rotate(partner - field, phase_angle, 1.0))
    return field


def butterfly_inverse(field, device, bit_count):
    for level in range(bit_count):
        half_size = 1 << level
        partner = swap(field, "narrow", half_size)
        upper = device // half_size % 2
        phase_angle = (device % half_size).astype(jnp.float32) * (math.pi / half_size)
        turned = rotate(jnp.where(upper == 0, partner, field), phase_angle, -1.0)
        field = jnp.where(upper == 0, field + turned, partner - turned)
    return field


def green_values(plane_wave, wave_z, modes, total_z, total_x):
    signed_z = jnp.where(wave_z < total_z // 2, wave_z, wave_z - total_z)
    wave_x = jnp.arange(modes)[:, None] + modes * jnp.arange(total_x // modes)[None, :]
    signed_x = jnp.where(wave_x < total_x // 2, wave_x, wave_x - total_x)
    square = signed_z[None, :, None] ** 2 + plane_wave**2 + signed_x[:, None, :] ** 2
    square = square.astype(jnp.float32)
    green = 1.0 / (1.0 + square / float(SCREEN * SCREEN)) + float(AMP) / (square + 1.0)
    return green * (1.0 / (total_x * total_z))


def plane(density, plane_wave):
    narrow, wide = lax.axis_size("narrow"), lax.axis_size("wide")
    bits = narrow.bit_length() - 1
    device, place = lax.axis_index("narrow"), lax.axis_index("wide")
    z_local, x_local = density.shape[1:]
    total_z, total_x = z_local * narrow, x_local * wide
    rows = z_local // wide
    chunks = x_local // LANES
    modes = wide * chunks
    four = narrow == 4
    low_wave = device if four else reversed_index(device, bits)

    slot = jnp.arange(wide, dtype=jnp.int32)
    line = jnp.arange(rows, dtype=jnp.int32)
    lane = jnp.arange(LANES, dtype=jnp.int32)
    block = (place - slot) % wide
    turns = turn(line[None, :] * (low_wave + narrow * block)[:, None], total_z)
    turns = jnp.broadcast_to(jnp.stack(turns, axis=1)[..., None], (wide, 2, rows, LANES))
    head = turn(slot * (low_wave + narrow * place), narrow * wide)
    parts = 2 if four else 1
    inner = jnp.stack([head[0], -head[1]], axis=1)
    if four:
        firsts = [1, 2]
        table = []
        for h in range(wide):
            row = []
            for coef in four_way_coef(device, firsts[h * 2 // wide], 1.0):
                row += list(c_mul(coef, (head[0][h], head[1][h])))
            table.append(jnp.stack(row))
        outer = jnp.stack(table)
        last = jnp.stack(
            [
                jnp.stack([item for pair in four_way_coef(device, first, -1.0) for item in pair])
                for first in firsts
            ]
        )
    else:
        outer = jnp.stack(head, axis=1)
        last = jnp.array([[1.0, 0.0]], jnp.float32)

    digit = jnp.arange(chunks, dtype=jnp.int32)
    x_coef = turn(slot[:, None] * (place * chunks + digit[None, :]), modes)
    x_coef = jnp.stack([value.reshape(-1) for value in x_coef], axis=1)
    mode = jnp.arange(modes, dtype=jnp.int32)
    x_turns = jnp.stack(turn(mode[:, None] * lane[None, :], total_x))
    wave_z = low_wave + narrow * (place + wide * line)
    green = green_values(plane_wave, wave_z, modes, total_z, total_x)

    half = z_local // parts
    received = []
    for c in range(chunks):
        columns = slice(c * LANES, (c + 1) * LANES)
        pieces = [density[:, p * half : (p + 1) * half, columns] for p in range(parts)]
        if four:
            pieces = [four_way(piece, device, first, 1.0) for piece, first in zip(pieces, firsts)]
        else:
            pieces = [[butterfly_forward(piece, device, bits)] for piece in pieces]
        sent = z_forward(pieces, outer, turns, wide, rows)
        received += [sent[0]] + [shift(sent[k], "wide", -k) for k in range(1, wide)]

    filtered = x_filter(received, x_coef, x_turns, green, wide, chunks)

    result = None
    for c in range(chunks):
        sent = filtered[c * wide : (c + 1) * wide]
        blocks = [sent[0]] + [shift(sent[k], "wide", k) for k in range(1, wide)]
        pieces = z_inverse(blocks, inner, turns, parts)
        if four:
            pieces = [four_way(piece, device, first, -1.0) for piece, first in zip(pieces, firsts)]
        else:
            pieces = [[butterfly_inverse(piece, device, bits)] for piece in pieces]
        result = finish(pieces, last, c, chunks, result)
    return result


def shards(density, plane_wave):
    planes = [plane(density[:, y], plane_wave[y]) for y in range(density.shape[1])]
    return jnp.stack(planes, axis=1)


def solution(mesh):
    in_specs = (P(None, None, "narrow", "wide"), P())
    out_specs = P(None, None, "narrow", "wide")
    return jax.shard_map(shards, mesh=mesh, in_specs=in_specs, out_specs=out_specs, check_vma=False)
```

```python
import functools
import math

import jax
import jax.numpy as jnp
import numpy as np
from jax import lax
from jax.experimental import pallas as pl
from jax.experimental.pallas import tpu as pltpu
from jax.sharding import PartitionSpec as P

SCREEN = 1024
AMP = 2048
LANES = 128
MIX_WEIGHT = 480
VMEM_LIMIT = 48 * 1024 * 1024
FIRSTS = (1, 2)


def split_bf16(value):
    high = np.asarray(value, np.float64).astype(np.float32).astype(jnp.bfloat16)
    low = (value - high.astype(np.float64)).astype(np.float32).astype(jnp.bfloat16)
    return high, low


def dft_matrix(length, orient, left):
    index = np.arange(length)
    angle = 2.0 * np.pi * ((index[:, None] * index[None, :]) % length) / length
    cosine, sine = np.cos(angle), orient * np.sin(angle)
    if left:
        whole = np.block([[cosine, -sine], [sine, cosine]])
    else:
        whole = np.block([[cosine, sine], [-sine, cosine]])
    high, low = split_bf16(whole)
    return np.stack([high, low])


def turn(numerator, length):
    angle = (np.asarray(numerator) % length) * (2.0 * np.pi / length)
    return np.stack([np.cos(angle), -np.sin(angle)], axis=-1).astype(np.float32)


def c_add(a, b):
    return (a[0] + b[0], a[1] + b[1])


def c_sub(a, b):
    return (a[0] - b[0], a[1] - b[1])


def c_mul(a, b):
    return (a[0] * b[0] - a[1] * b[1], a[0] * b[1] + a[1] * b[0])


def c_const(a, numerator, length, orient):
    numerator = (orient * numerator) % length
    if numerator == 0:
        return a
    if 2 * numerator == length:
        return (-a[0], -a[1])
    if 4 * numerator == length:
        return (-a[1], a[0])
    if 4 * numerator == 3 * length:
        return (a[1], -a[0])
    angle = 2.0 * math.pi * numerator / length
    cosine, sine = math.cos(angle), math.sin(angle)
    if 8 * numerator % length == 0:
        root = math.sqrt(0.5)
        total, differ = (a[0] + a[1]) * root, (a[0] - a[1]) * root
        if cosine > 0 and sine > 0:
            return (differ, total)
        if cosine > 0:
            return (total, -differ)
        if sine > 0:
            return (-total, differ)
        return (-differ, -total)
    return (a[0] * cosine - a[1] * sine, a[0] * sine + a[1] * cosine)


def small_dft(values, orient):
    count = len(values)
    if count == 1:
        return values
    half = count // 2
    upper = [c_add(values[i], values[i + half]) for i in range(half)]
    lower = [
        c_const(c_sub(values[i], values[i + half]), i, count, orient) for i in range(half)
    ]
    even, odd = small_dft(upper, orient), small_dft(lower, orient)
    result = []
    for i in range(half):
        result += [even[i], odd[i]]
    return result


def dot3(high, low, value, left):
    value_high = value.astype(jnp.bfloat16)
    value_low = (value - value_high.astype(jnp.float32)).astype(jnp.bfloat16)
    dot = functools.partial(jnp.dot, preferred_element_type=jnp.float32)
    if left:
        return dot(high, value_high) + (dot(high, value_low) + dot(low, value_high))
    return dot(value_high, high) + (dot(value_low, high) + dot(value_high, low))


def whole_spec(shape):
    return pl.BlockSpec(shape, lambda *_: (0,) * len(shape))


def params():
    return pltpu.CompilerParams(vmem_limit_bytes=VMEM_LIMIT)


def combine(inputs, coef_ref, row, place):
    total = None
    for term, ref in enumerate(inputs):
        value = (ref[0, place, :], ref[1, place, :])
        product = c_mul(value, (coef_ref[row, 2 * term], coef_ref[row, 2 * term + 1]))
        total = product if total is None else c_add(total, product)
    return total


def z_forward_kernel(terms, parts, slots, rows, coef_ref, matrix_ref, turn_ref, *refs):
    inputs = refs[: terms * parts]
    out_ref, held = refs[-2:]
    per_part = slots // parts
    tile = min(rows, 8)

    def step(index, carry):
        row = pl.multiple_of(index * tile, tile)
        values = []
        for h in range(slots):
            part, inner = divmod(h, per_part)
            place = pl.ds(inner * rows + row, tile)
            values.append(combine(inputs[part * terms : (part + 1) * terms], coef_ref, h, place))
        values = small_dft(values, -1)
        for k in range(slots):
            twiddle = (
                turn_ref[k, 0, pl.ds(row, tile), :],
                turn_ref[k, 1, pl.ds(row, tile), :],
            )
            real_part, imag_part = c_mul(values[k], twiddle)
            held[pl.ds(row, tile), k * LANES : (k + 1) * LANES] = real_part
            held[pl.ds(rows + row, tile), k * LANES : (k + 1) * LANES] = imag_part
        return carry

    lax.fori_loop(0, rows // tile, step, 0)
    result = dot3(matrix_ref[0], matrix_ref[1], held[...], True)
    for k in range(slots):
        out_ref[k, 0] = result[:rows, k * LANES : (k + 1) * LANES]
        out_ref[k, 1] = result[rows:, k * LANES : (k + 1) * LANES]


def z_forward(parts, coef, turns, slots, rows):
    terms = len(parts[0])
    flat = [pair for part in parts for pair in part]
    matrix = jnp.asarray(dft_matrix(rows, -1, True))
    shape = (slots, 2, rows, LANES)
    return pl.pallas_call(
        functools.partial(z_forward_kernel, terms, len(parts), slots, rows),
        grid=(1,),
        out_shape=jax.ShapeDtypeStruct(shape, jnp.float32),
        in_specs=[
            pl.BlockSpec(memory_space=pltpu.SMEM),
            whole_spec(matrix.shape),
            whole_spec(turns.shape),
        ]
        + [spec for _, spec in flat],
        out_specs=whole_spec(shape),
        scratch_shapes=[pltpu.VMEM((2 * rows, slots * LANES), jnp.float32)],
        compiler_params=params(),
        cost_estimate=pl.CostEstimate(
            flops=700 * rows * rows * slots * LANES,
            bytes_accessed=32 * rows * slots * LANES,
            transcendentals=0,
        ),
        name="z_forward",
    )(coef, matrix, turns, *[array for array, _ in flat])


def z_inverse_kernel(parts, slots, rows, coef_ref, matrix_ref, turn_ref, in_ref, *refs):
    outputs, held = refs[:parts], refs[parts]
    per_part = slots // parts
    tile = min(rows, 8)
    for k in range(slots):
        held[:rows, k * LANES : (k + 1) * LANES] = in_ref[k, 0]
        held[rows:, k * LANES : (k + 1) * LANES] = in_ref[k, 1]
    held[...] = dot3(matrix_ref[0], matrix_ref[1], held[...], True)

    def step(index, carry):
        row = pl.multiple_of(index * tile, tile)
        values = []
        for k in range(slots):
            value = (
                held[pl.ds(row, tile), k * LANES : (k + 1) * LANES],
                held[pl.ds(rows + row, tile), k * LANES : (k + 1) * LANES],
            )
            twiddle = (
                turn_ref[k, 0, pl.ds(row, tile), :],
                -turn_ref[k, 1, pl.ds(row, tile), :],
            )
            values.append(c_mul(value, twiddle))
        values = small_dft(values, 1)
        for h in range(slots):
            part, inner = divmod(h, per_part)
            real_part, imag_part = c_mul(values[h], (coef_ref[h, 0], coef_ref[h, 1]))
            outputs[part][0, pl.ds(inner * rows + row, tile), :] = real_part
            outputs[part][1, pl.ds(inner * rows + row, tile), :] = imag_part
        return carry

    lax.fori_loop(0, rows // tile, step, 0)


def z_inverse(blocks, coef, turns, parts):
    slots, _, rows, _ = blocks.shape
    matrix = jnp.asarray(dft_matrix(rows, 1, True))
    shape = (2, slots // parts * rows, LANES)
    return pl.pallas_call(
        functools.partial(z_inverse_kernel, parts, slots, rows),
        grid=(1,),
        out_shape=[jax.ShapeDtypeStruct(shape, jnp.float32)] * parts,
        in_specs=[
            pl.BlockSpec(memory_space=pltpu.SMEM),
            whole_spec(matrix.shape),
            whole_spec(turns.shape),
            whole_spec(blocks.shape),
        ],
        out_specs=[whole_spec(shape)] * parts,
        scratch_shapes=[pltpu.VMEM((2 * rows, slots * LANES), jnp.float32)],
        compiler_params=params(),
        cost_estimate=pl.CostEstimate(
            flops=700 * rows * rows * slots * LANES,
            bytes_accessed=20 * rows * slots * LANES,
            transcendentals=0,
        ),
        name="z_inverse",
    )(coef, matrix, turns, blocks)


def x_filter_kernel(slots, chunks, rows, forward_ref, inverse_ref, turn_ref, green_ref, *refs):
    inputs = refs[:chunks]
    outputs = refs[chunks : 2 * chunks]
    held = refs[-1]
    tile = 8
    modes = slots * chunks

    def before(index, carry):
        row = pl.multiple_of(index * tile, tile)
        place = pl.ds(row, tile)
        columns = []
        for c in range(chunks):
            values = [
                (inputs[c][k, 0, place, :], inputs[c][k, 1, place, :]) for k in range(slots)
            ]
            values = small_dft(values, -1)
            columns.append([c_const(values[a], a * c, modes, -1) for a in range(slots)])
        for a in range(slots):
            values = small_dft([columns[c][a] for c in range(chunks)], -1)
            for b in range(chunks):
                mode = a + slots * b
                twiddle = (turn_ref[0, mode : mode + 1, :], turn_ref[1, mode : mode + 1, :])
                real_part, imag_part = c_mul(values[b], twiddle)
                held[mode, place, :LANES] = real_part
                held[mode, place, LANES:] = imag_part
        return carry

    lax.fori_loop(0, rows // tile, before, 0)

    group = max(1, min(modes, 256 // rows))

    def middle(index, carry):
        mode = pl.multiple_of(index * group, group)
        value = held[pl.ds(mode, group)].reshape(group * rows, 2 * LANES)
        value = dot3(forward_ref[0], forward_ref[1], value, False)
        green = green_ref[pl.ds(mode, group)].reshape(group * rows, LANES)
        value = value * jnp.concatenate([green, green], axis=1)
        value = dot3(inverse_ref[0], inverse_ref[1], value, False)
        held[pl.ds(mode, group)] = value.reshape(group, rows, 2 * LANES)
        return carry

    lax.fori_loop(0, modes // group, middle, 0)

    def after(index, carry):
        row = pl.multiple_of(index * tile, tile)
        place = pl.ds(row, tile)
        columns = []
        for a in range(slots):
            values = []
            for b in range(chunks):
                mode = a + slots * b
                twiddle = (turn_ref[0, mode : mode + 1, :], -turn_ref[1, mode : mode + 1, :])
                values.append(c_mul((held[mode, place, :LANES], held[mode, place, LANES:]), twiddle))
            columns.append(small_dft(values, 1))
        for c in range(chunks):
            values = [c_const(columns[a][c], a * c, modes, 1) for a in range(slots)]
            values = small_dft(values, 1)
            for k in range(slots):
                outputs[c][k, 0, place, :] = values[k][0]
                outputs[c][k, 1, place, :] = values[k][1]
        return carry

    lax.fori_loop(0, rows // tile, after, 0)


def x_filter(blocks, turns, green):
    chunks = len(blocks)
    slots, _, rows, _ = blocks[0].shape
    step = min(rows, 32)
    modes = slots * chunks
    forward = jnp.asarray(dft_matrix(LANES, -1, False))
    inverse = jnp.asarray(dft_matrix(LANES, 1, False))
    block = pl.BlockSpec((slots, 2, step, LANES), lambda i: (0, 0, i, 0))
    return pl.pallas_call(
        functools.partial(x_filter_kernel, slots, chunks, step),
        grid=(rows // step,),
        out_shape=[jax.ShapeDtypeStruct(blocks[0].shape, jnp.float32)] * chunks,
        in_specs=[
            whole_spec(forward.shape),
            whole_spec(inverse.shape),
            whole_spec(turns.shape),
            pl.BlockSpec((modes, step, LANES), lambda i: (0, i, 0)),
        ]
        + [block] * chunks,
        out_specs=[block] * chunks,
        scratch_shapes=[pltpu.VMEM((modes, step, 2 * LANES), jnp.float32)],
        compiler_params=params(),
        cost_estimate=pl.CostEstimate(
            flops=96 * LANES * LANES * modes * rows,
            bytes_accessed=20 * modes * rows * LANES,
            transcendentals=0,
        ),
        name="x_filter",
    )(forward, inverse, turns, green, *blocks)


def mix_kernel(terms, parts, coef_ref, *refs):
    for part in range(parts):
        out_ref = refs[terms * parts + part]
        inputs = refs[part * terms : (part + 1) * terms]
        total = combine(inputs, coef_ref, part, slice(None))
        out_ref[0], out_ref[1] = total


def mix(parts, coef, rows):
    terms = len(parts[0])
    flat = [pair for part in parts for pair in part]
    steps = 4 if rows % 32 == 0 else 1
    return pl.pallas_call(
        functools.partial(mix_kernel, terms, len(parts)),
        grid=(steps,),
        out_shape=[jax.ShapeDtypeStruct((2, rows, LANES), jnp.float32)] * len(parts),
        in_specs=[pl.BlockSpec(memory_space=pltpu.SMEM)] + [make(steps) for _, make in flat],
        out_specs=[pl.BlockSpec((2, rows // steps, LANES), lambda i: (0, i, 0))] * len(parts),
        compiler_params=params(),
        cost_estimate=pl.CostEstimate(
            flops=20 * rows * LANES * len(parts),
            bytes_accessed=MIX_WEIGHT * rows * LANES * len(parts),
            transcendentals=0,
        ),
        name="mix",
    )(coef, *[array for array, _ in flat])


def finish_kernel(terms, parts, coef_ref, *refs):
    out_ref = refs[-1]
    for part in range(parts):
        inputs = refs[part * terms : (part + 1) * terms]
        total = combine(inputs, coef_ref, part, slice(None))
        out_ref[0, part], out_ref[1, part] = total


def finish(parts, coef, chunk, chunks, so_far):
    terms = len(parts[0])
    flat = [array for part in parts for array in part]
    rows = parts[0][0].shape[1]
    steps = 4 if rows % 32 == 0 else 1
    extra = [] if so_far is None else [so_far]
    return pl.pallas_call(
        functools.partial(finish_kernel, terms, len(parts)),
        grid=(steps,),
        out_shape=jax.ShapeDtypeStruct((2, len(parts), rows, chunks * LANES), jnp.float32),
        in_specs=[pl.BlockSpec(memory_space=pltpu.SMEM)]
        + [pl.BlockSpec((2, rows // steps, LANES), lambda i: (0, i, 0))] * len(flat)
        + [pl.BlockSpec(memory_space=pl.ANY)] * len(extra),
        out_specs=pl.BlockSpec((2, len(parts), rows // steps, LANES), lambda i: (0, 0, i, chunk)),
        input_output_aliases={1 + len(flat): 0} if extra else {},
        compiler_params=params(),
        cost_estimate=pl.CostEstimate(
            flops=20 * rows * LANES * len(parts),
            bytes_accessed=32 * rows * LANES * len(parts),
            transcendentals=0,
        ),
        name="finish",
    )(coef, *flat, *extra)


def after(value, *others):
    return lax.optimization_barrier((value, others))[0]


def swap(value, axis, mask):
    pairs = [(source, source ^ mask) for source in range(lax.axis_size(axis))]
    return lax.ppermute(value, axis, pairs)


def trade(blocks):
    return lax.all_to_all(blocks, "wide", 0, 0, tiled=True)


def narrow_terms(orient, length):
    give, keep = [], []
    for device in range(4):
        for first in FIRSTS:
            there = device ^ (3 - first)
            unit = orient * (length // 4)
            give.append([there * device * unit, there * (device ^ first) * unit])
            keep.append([device * device * unit, device * (device ^ first) * unit, 0])
    shape = (4, len(FIRSTS), -1)
    return np.array(give).reshape(shape), np.array(keep).reshape(shape)


def pick(table, index):
    return lax.dynamic_index_in_dim(jnp.asarray(table), index, 0, keepdims=False)


def reversed_index(device, bit_count):
    result = jnp.int32(0)
    for level in range(bit_count):
        result = result + device // (1 << level) % 2 * (1 << bit_count - 1 - level)
    return result


def rotate(field, phase_angle, orient):
    return jnp.stack(
        c_mul((field[0], field[1]), (jnp.cos(phase_angle), -orient * jnp.sin(phase_angle)))
    )


def butterfly_forward(field, device, bit_count):
    for level in reversed(range(bit_count)):
        half_size = 1 << level
        partner = swap(field, "narrow", half_size)
        upper = device // half_size % 2
        phase_angle = (device % half_size).astype(jnp.float32) * (math.pi / half_size)
        field = jnp.where(upper == 0, field + partner, rotate(partner - field, phase_angle, 1.0))
    return field


def butterfly_inverse(field, device, bit_count):
    for level in range(bit_count):
        half_size = 1 << level
        partner = swap(field, "narrow", half_size)
        upper = device // half_size % 2
        phase_angle = (device % half_size).astype(jnp.float32) * (math.pi / half_size)
        turned = rotate(jnp.where(upper == 0, partner, field), phase_angle, -1.0)
        field = jnp.where(upper == 0, field + turned, partner - turned)
    return field


def green_values(plane_wave, wave_z, modes, total_z, total_x):
    signed_z = jnp.where(wave_z < total_z // 2, wave_z, wave_z - total_z)
    wave_x = jnp.arange(modes)[:, None] + modes * jnp.arange(total_x // modes)[None, :]
    signed_x = jnp.where(wave_x < total_x // 2, wave_x, wave_x - total_x)
    square = signed_z[None, :, None] ** 2 + plane_wave**2 + signed_x[:, None, :] ** 2
    square = square.astype(jnp.float32)
    green = 1.0 / (1.0 + square / float(SCREEN * SCREEN)) + float(AMP) / (square + 1.0)
    return green * (1.0 / (total_x * total_z))


def plane(density, plane_wave):
    narrow, wide = lax.axis_size("narrow"), lax.axis_size("wide")
    bits = narrow.bit_length() - 1
    device, place = lax.axis_index("narrow"), lax.axis_index("wide")
    z_local, x_local = density.shape[1:]
    total_z, total_x = z_local * narrow, x_local * wide
    rows = z_local // wide
    chunks = x_local // LANES
    modes = wide * chunks
    four = narrow == 4
    low_wave = device if four else reversed_index(device, bits)
    parts = 2 if four else 1
    half = z_local // parts

    waves = [d if four else int(format(d, "b").zfill(bits)[::-1], 2) for d in range(narrow)]
    waves = np.array(waves)
    block = waves[:, None] + narrow * np.arange(wide)
    turns = turn(np.arange(rows) * block[..., None], total_z)
    turns = pick(np.moveaxis(turns, 3, 2), device)
    turns = jnp.broadcast_to(turns[..., None], (wide, 2, rows, LANES))
    head = np.arange(wide) * waves[:, None]
    inner = pick(turn(-head, narrow * wide), device)
    if four:
        give, keep = narrow_terms(1, narrow * wide)
        outer = np.repeat(keep, wide // 2, axis=1) + head[..., None]
        outer = pick(turn(outer, narrow * wide).reshape(narrow, wide, 6), device)
        give = pick(turn(give, narrow * wide).reshape(narrow, 2, 4), device)
        give_back, keep = narrow_terms(-1, narrow * wide)
        give_back = pick(turn(give_back, narrow * wide).reshape(narrow, 2, 4), device)
        last = pick(turn(keep, narrow * wide).reshape(narrow, 2, 6), device)
    else:
        outer = pick(turn(head, narrow * wide), device)
        last = jnp.array([[1.0, 0.0]], jnp.float32)
    x_turns = turn(np.arange(modes)[:, None] * np.arange(LANES)[None, :], total_x)
    x_turns = jnp.asarray(np.moveaxis(x_turns, 2, 0))
    line = jnp.arange(rows, dtype=jnp.int32)
    wave_z = low_wave + narrow * (place + wide * line)
    green = green_values(plane_wave, wave_z, modes, total_z, total_x)

    def part_spec(part, chunk):
        def make(steps):
            first = part * steps
            return pl.BlockSpec((2, half // steps, LANES), lambda i: (0, first + i, chunk))

        return make

    def own_spec(steps):
        return pl.BlockSpec((2, half // steps, LANES), lambda i: (0, i, 0))

    def cut(c, source):
        columns = slice(c * LANES, (c + 1) * LANES)
        return [source[:, p * half : (p + 1) * half, columns] for p in range(parts)]

    def first_swap(pieces):
        return [swap(piece, "narrow", first) for piece, first in zip(pieces, FIRSTS)]

    def second_swap(pieces):
        return [swap(piece, "narrow", 3 - first) for piece, first in zip(pieces, FIRSTS)]

    arrived, pieces = [], [cut(0, density)]
    rest = after(density, pieces[0])
    pieces += [cut(c, rest) for c in range(1, chunks)]
    partner = received = sent = None
    for c in range(chunks):
        if four:
            if c == 0:
                partner = first_swap(pieces[0])
            else:
                partner = first_swap(after(pieces[c], received))
            ready = after(partner, sent) if c else partner
            mixed = mix(
                [[(density, part_spec(p, c)), (ready[p], own_spec)] for p in range(parts)], give, half
            )
            received = second_swap(mixed)
            terms = [
                [
                    (density, part_spec(p, c)(1)),
                    (partner[p], own_spec(1)),
                    (received[p], own_spec(1)),
                ]
                for p in range(parts)
            ]
        else:
            terms = [[(butterfly_forward(piece, device, bits), own_spec(1))] for piece in pieces[c]]
        sent = z_forward(terms, outer, turns, wide, rows)
        arrived.append(trade(sent))

    filtered = x_filter(arrived, x_turns, green)

    result, done = None, []
    for c in range(chunks):
        blocks = after(filtered[c], done[c - 2]) if four and c >= 2 else filtered[c]
        pieces = z_inverse(trade(blocks), inner, turns, parts)
        if four:
            partner = first_swap(pieces)
            ready = after(partner, received) if c else partner
            mixed = mix(
                [[(pieces[p], own_spec), (ready[p], own_spec)] for p in range(parts)], give_back, half
            )
            done.append(mixed)
            received = second_swap(mixed)
            pieces = [[pieces[p], partner[p], received[p]] for p in range(parts)]
        else:
            pieces = [[butterfly_inverse(piece, device, bits)] for piece in pieces]
        result = finish(pieces, last, c, chunks, result)
    return result.reshape(density.shape)


def shards(density, plane_wave):
    planes = [plane(density[:, y], plane_wave[y]) for y in range(density.shape[1])]
    return jnp.stack(planes, axis=1)


def solution(mesh):
    in_specs = (P(None, None, "narrow", "wide"), P())
    out_specs = P(None, None, "narrow", "wide")
    return jax.shard_map(shards, mesh=mesh, in_specs=in_specs, out_specs=out_specs, check_vma=False)
```

```python
import functools
import math

import jax
import jax.numpy as jnp
import numpy as np
from jax import lax
from jax.experimental import pallas as pl
from jax.experimental.pallas import tpu as pltpu
from jax.sharding import PartitionSpec as P

SCREEN = 1024
AMP = 2048
LANES = 128
MIX_WEIGHT = 480
LINE_WEIGHT = 3000
MIDDLE_UNROLL = 4
PLAN = ((0, 1), (2, 3))
VMEM_LIMIT = 48 * 1024 * 1024
FIRSTS = (1, 2)


def split_bf16(value):
    high = np.asarray(value, np.float64).astype(np.float32).astype(jnp.bfloat16)
    low = (value - high.astype(np.float64)).astype(np.float32).astype(jnp.bfloat16)
    return high, low


def dft_matrix(length, orient, left):
    index = np.arange(length)
    angle = 2.0 * np.pi * ((index[:, None] * index[None, :]) % length) / length
    cosine, sine = np.cos(angle), orient * np.sin(angle)
    if left:
        whole = np.block([[cosine, -sine], [sine, cosine]])
    else:
        whole = np.block([[cosine, sine], [-sine, cosine]])
    high, low = split_bf16(whole)
    return np.stack([high, low])


def turn(numerator, length):
    angle = (np.asarray(numerator) % length) * (2.0 * np.pi / length)
    return np.stack([np.cos(angle), -np.sin(angle)], axis=-1).astype(np.float32)


def c_add(a, b):
    return (a[0] + b[0], a[1] + b[1])


def c_sub(a, b):
    return (a[0] - b[0], a[1] - b[1])


def c_mul(a, b):
    return (a[0] * b[0] - a[1] * b[1], a[0] * b[1] + a[1] * b[0])


def c_const(a, numerator, length, orient):
    numerator = (orient * numerator) % length
    if numerator == 0:
        return a
    if 2 * numerator == length:
        return (-a[0], -a[1])
    if 4 * numerator == length:
        return (-a[1], a[0])
    if 4 * numerator == 3 * length:
        return (a[1], -a[0])
    angle = 2.0 * math.pi * numerator / length
    cosine, sine = math.cos(angle), math.sin(angle)
    if 8 * numerator % length == 0:
        root = math.sqrt(0.5)
        total, differ = (a[0] + a[1]) * root, (a[0] - a[1]) * root
        if cosine > 0 and sine > 0:
            return (differ, total)
        if cosine > 0:
            return (total, -differ)
        if sine > 0:
            return (-total, differ)
        return (-differ, -total)
    return (a[0] * cosine - a[1] * sine, a[0] * sine + a[1] * cosine)


def small_dft(values, orient):
    count = len(values)
    if count == 1:
        return values
    half = count // 2
    upper = [c_add(values[i], values[i + half]) for i in range(half)]
    lower = [
        c_const(c_sub(values[i], values[i + half]), i, count, orient) for i in range(half)
    ]
    even, odd = small_dft(upper, orient), small_dft(lower, orient)
    result = []
    for i in range(half):
        result += [even[i], odd[i]]
    return result


def dot3(high, low, value, left):
    value_high = value.astype(jnp.bfloat16)
    value_low = (value - value_high.astype(jnp.float32)).astype(jnp.bfloat16)
    dot = functools.partial(jnp.dot, preferred_element_type=jnp.float32)
    if left:
        return dot(high, value_high) + (dot(high, value_low) + dot(low, value_high))
    return dot(value_high, high) + (dot(value_low, high) + dot(value_high, low))


def whole_spec(shape):
    return pl.BlockSpec(shape, lambda *_: (0,) * len(shape))


def params():
    return pltpu.CompilerParams(vmem_limit_bytes=VMEM_LIMIT)


def combine(inputs, coef_ref, row, place):
    total = None
    for term, ref in enumerate(inputs):
        value = (ref[0, place, :], ref[1, place, :])
        product = c_mul(value, (coef_ref[row, 2 * term], coef_ref[row, 2 * term + 1]))
        total = product if total is None else c_add(total, product)
    return total


def z_forward_kernel(terms, parts, slots, rows, coef_ref, matrix_ref, turn_ref, *refs):
    inputs = refs[: terms * parts]
    out_ref, held = refs[-2:]
    per_part = slots // parts
    tile = min(rows, 8)

    def step(index, carry):
        row = pl.multiple_of(index * tile, tile)
        values = []
        for h in range(slots):
            part, inner = divmod(h, per_part)
            place = pl.ds(inner * rows + row, tile)
            values.append(combine(inputs[part * terms : (part + 1) * terms], coef_ref, h, place))
        values = small_dft(values, -1)
        for k in range(slots):
            twiddle = (
                turn_ref[k, 0, pl.ds(row, tile), :],
                turn_ref[k, 1, pl.ds(row, tile), :],
            )
            real_part, imag_part = c_mul(values[k], twiddle)
            held[pl.ds(row, tile), k * LANES : (k + 1) * LANES] = real_part
            held[pl.ds(rows + row, tile), k * LANES : (k + 1) * LANES] = imag_part
        return carry

    lax.fori_loop(0, rows // tile, step, 0)
    result = dot3(matrix_ref[0], matrix_ref[1], held[...], True)
    for k in range(slots):
        out_ref[k, 0] = result[:rows, k * LANES : (k + 1) * LANES]
        out_ref[k, 1] = result[rows:, k * LANES : (k + 1) * LANES]


def z_forward(parts, coef, turns, slots, rows):
    terms = len(parts[0])
    flat = [pair for part in parts for pair in part]
    matrix = jnp.asarray(dft_matrix(rows, -1, True))
    shape = (slots, 2, rows, LANES)
    return pl.pallas_call(
        functools.partial(z_forward_kernel, terms, len(parts), slots, rows),
        grid=(1,),
        out_shape=jax.ShapeDtypeStruct(shape, jnp.float32),
        in_specs=[
            pl.BlockSpec(memory_space=pltpu.SMEM),
            whole_spec(matrix.shape),
            whole_spec(turns.shape),
        ]
        + [spec for _, spec in flat],
        out_specs=whole_spec(shape),
        scratch_shapes=[pltpu.VMEM((2 * rows, slots * LANES), jnp.float32)],
        compiler_params=params(),
        cost_estimate=pl.CostEstimate(
            flops=700 * rows * rows * slots * LANES,
            bytes_accessed=32 * rows * slots * LANES,
            transcendentals=0,
        ),
        name="z_forward",
    )(coef, matrix, turns, *[array for array, _ in flat])


def z_inverse_kernel(parts, slots, rows, coef_ref, matrix_ref, turn_ref, in_ref, *refs):
    outputs, held = refs[:parts], refs[parts]
    per_part = slots // parts
    tile = min(rows, 8)
    for k in range(slots):
        held[:rows, k * LANES : (k + 1) * LANES] = in_ref[k, 0]
        held[rows:, k * LANES : (k + 1) * LANES] = in_ref[k, 1]
    held[...] = dot3(matrix_ref[0], matrix_ref[1], held[...], True)

    def step(index, carry):
        row = pl.multiple_of(index * tile, tile)
        values = []
        for k in range(slots):
            value = (
                held[pl.ds(row, tile), k * LANES : (k + 1) * LANES],
                held[pl.ds(rows + row, tile), k * LANES : (k + 1) * LANES],
            )
            twiddle = (
                turn_ref[k, 0, pl.ds(row, tile), :],
                -turn_ref[k, 1, pl.ds(row, tile), :],
            )
            values.append(c_mul(value, twiddle))
        values = small_dft(values, 1)
        for h in range(slots):
            part, inner = divmod(h, per_part)
            real_part, imag_part = c_mul(values[h], (coef_ref[h, 0], coef_ref[h, 1]))
            outputs[part][0, pl.ds(inner * rows + row, tile), :] = real_part
            outputs[part][1, pl.ds(inner * rows + row, tile), :] = imag_part
        return carry

    lax.fori_loop(0, rows // tile, step, 0)


def z_inverse(blocks, coef, turns, parts):
    slots, _, rows, _ = blocks.shape
    matrix = jnp.asarray(dft_matrix(rows, 1, True))
    shape = (2, slots // parts * rows, LANES)
    return pl.pallas_call(
        functools.partial(z_inverse_kernel, parts, slots, rows),
        grid=(1,),
        out_shape=[jax.ShapeDtypeStruct(shape, jnp.float32)] * parts,
        in_specs=[
            pl.BlockSpec(memory_space=pltpu.SMEM),
            whole_spec(matrix.shape),
            whole_spec(turns.shape),
            whole_spec(blocks.shape),
        ],
        out_specs=[whole_spec(shape)] * parts,
        scratch_shapes=[pltpu.VMEM((2 * rows, slots * LANES), jnp.float32)],
        compiler_params=params(),
        cost_estimate=pl.CostEstimate(
            flops=700 * rows * rows * slots * LANES,
            bytes_accessed=20 * rows * slots * LANES,
            transcendentals=0,
        ),
        name="z_inverse",
    )(coef, matrix, turns, blocks)


def x_filter_kernel(slots, chunks, rows, forward_ref, inverse_ref, turn_ref, green_ref, *refs):
    inputs = refs[:chunks]
    outputs = refs[chunks : 2 * chunks]
    held = refs[-1]
    tile = 8
    modes = slots * chunks

    def before(index, carry):
        row = pl.multiple_of(index * tile, tile)
        place = pl.ds(row, tile)
        columns = []
        for c in range(chunks):
            values = [
                (inputs[c][k, 0, place, :], inputs[c][k, 1, place, :]) for k in range(slots)
            ]
            values = small_dft(values, -1)
            columns.append([c_const(values[a], a * c, modes, -1) for a in range(slots)])
        for a in range(slots):
            values = small_dft([columns[c][a] for c in range(chunks)], -1)
            for b in range(chunks):
                mode = a + slots * b
                twiddle = (turn_ref[0, mode : mode + 1, :], turn_ref[1, mode : mode + 1, :])
                real_part, imag_part = c_mul(values[b], twiddle)
                held[mode, place, :LANES] = real_part
                held[mode, place, LANES:] = imag_part
        return carry

    lax.fori_loop(0, rows // tile, before, 0)

    group = max(1, min(modes, 256 // rows))

    def middle(index, carry):
        mode = pl.multiple_of(index * group, group)
        value = held[pl.ds(mode, group)].reshape(group * rows, 2 * LANES)
        value = dot3(forward_ref[0], forward_ref[1], value, False)
        green = green_ref[pl.ds(mode, group)].reshape(group * rows, LANES)
        value = value * jnp.concatenate([green, green], axis=1)
        value = dot3(inverse_ref[0], inverse_ref[1], value, False)
        held[pl.ds(mode, group)] = value.reshape(group, rows, 2 * LANES)
        return carry

    lax.fori_loop(0, modes // group, middle, 0)

    def after(index, carry):
        row = pl.multiple_of(index * tile, tile)
        place = pl.ds(row, tile)
        columns = []
        for a in range(slots):
            values = []
            for b in range(chunks):
                mode = a + slots * b
                twiddle = (turn_ref[0, mode : mode + 1, :], -turn_ref[1, mode : mode + 1, :])
                values.append(c_mul((held[mode, place, :LANES], held[mode, place, LANES:]), twiddle))
            columns.append(small_dft(values, 1))
        for c in range(chunks):
            values = [c_const(columns[a][c], a * c, modes, 1) for a in range(slots)]
            values = small_dft(values, 1)
            for k in range(slots):
                outputs[c][k, 0, place, :] = values[k][0]
                outputs[c][k, 1, place, :] = values[k][1]
        return carry

    lax.fori_loop(0, rows // tile, after, 0)


def x_filter(blocks, turns, green):
    chunks = len(blocks)
    slots, _, rows, _ = blocks[0].shape
    step = min(rows, 32)
    modes = slots * chunks
    forward = jnp.asarray(dft_matrix(LANES, -1, False))
    inverse = jnp.asarray(dft_matrix(LANES, 1, False))
    block = pl.BlockSpec((slots, 2, step, LANES), lambda i: (0, 0, i, 0))
    return pl.pallas_call(
        functools.partial(x_filter_kernel, slots, chunks, step),
        grid=(rows // step,),
        out_shape=[jax.ShapeDtypeStruct(blocks[0].shape, jnp.float32)] * chunks,
        in_specs=[
            whole_spec(forward.shape),
            whole_spec(inverse.shape),
            whole_spec(turns.shape),
            pl.BlockSpec((modes, step, LANES), lambda i: (0, i, 0)),
        ]
        + [block] * chunks,
        out_specs=[block] * chunks,
        scratch_shapes=[pltpu.VMEM((modes, step, 2 * LANES), jnp.float32)],
        compiler_params=params(),
        cost_estimate=pl.CostEstimate(
            flops=96 * LANES * LANES * modes * rows,
            bytes_accessed=20 * modes * rows * LANES,
            transcendentals=0,
        ),
        name="x_filter",
    )(forward, inverse, turns, green, *blocks)


def mix_kernel(terms, parts, coef_ref, *refs):
    for part in range(parts):
        out_ref = refs[terms * parts + part]
        inputs = refs[part * terms : (part + 1) * terms]
        total = combine(inputs, coef_ref, part, slice(None))
        out_ref[0], out_ref[1] = total


def mix(parts, coef, rows):
    terms = len(parts[0])
    flat = [pair for part in parts for pair in part]
    steps = 4 if rows % 32 == 0 else 1
    return pl.pallas_call(
        functools.partial(mix_kernel, terms, len(parts)),
        grid=(steps,),
        out_shape=[jax.ShapeDtypeStruct((2, rows, LANES), jnp.float32)] * len(parts),
        in_specs=[pl.BlockSpec(memory_space=pltpu.SMEM)] + [make(steps) for _, make in flat],
        out_specs=[pl.BlockSpec((2, rows // steps, LANES), lambda i: (0, i, 0))] * len(parts),
        compiler_params=params(),
        cost_estimate=pl.CostEstimate(
            flops=20 * rows * LANES * len(parts),
            bytes_accessed=MIX_WEIGHT * rows * LANES * len(parts),
            transcendentals=0,
        ),
        name="mix",
    )(coef, *[array for array, _ in flat])


def finish_kernel(terms, parts, coef_ref, *refs):
    out_ref = refs[-1]
    for part in range(parts):
        inputs = refs[part * terms : (part + 1) * terms]
        total = combine(inputs, coef_ref, part, slice(None))
        out_ref[0, part], out_ref[1, part] = total


def finish(parts, coef, chunk, chunks, so_far):
    terms = len(parts[0])
    flat = [array for part in parts for array in part]
    rows = parts[0][0].shape[1]
    steps = 4 if rows % 32 == 0 else 1
    extra = [] if so_far is None else [so_far]
    return pl.pallas_call(
        functools.partial(finish_kernel, terms, len(parts)),
        grid=(steps,),
        out_shape=jax.ShapeDtypeStruct((2, len(parts), rows, chunks * LANES), jnp.float32),
        in_specs=[pl.BlockSpec(memory_space=pltpu.SMEM)]
        + [pl.BlockSpec((2, rows // steps, LANES), lambda i: (0, i, 0))] * len(flat)
        + [pl.BlockSpec(memory_space=pl.ANY)] * len(extra),
        out_specs=pl.BlockSpec((2, len(parts), rows // steps, LANES), lambda i: (0, 0, i, chunk)),
        input_output_aliases={1 + len(flat): 0} if extra else {},
        compiler_params=params(),
        cost_estimate=pl.CostEstimate(
            flops=20 * rows * LANES * len(parts),
            bytes_accessed=32 * rows * LANES * len(parts),
            transcendentals=0,
        ),
        name="finish",
    )(coef, *flat, *extra)


def after(value, *others):
    return lax.optimization_barrier((value, others))[0]


def swap(value, axis, mask):
    pairs = [(source, source ^ mask) for source in range(lax.axis_size(axis))]
    return lax.ppermute(value, axis, pairs)


def trade(blocks):
    return lax.all_to_all(blocks, "wide", 0, 0, tiled=True)


def narrow_terms(orient, length):
    give, keep = [], []
    for device in range(4):
        for first in FIRSTS:
            there = device ^ (3 - first)
            unit = orient * (length // 4)
            give.append([there * device * unit, there * (device ^ first) * unit])
            keep.append([device * device * unit, device * (device ^ first) * unit, 0])
    shape = (4, len(FIRSTS), -1)
    return np.array(give).reshape(shape), np.array(keep).reshape(shape)


def pick(table, index):
    return lax.dynamic_index_in_dim(jnp.asarray(table), index, 0, keepdims=False)


def reversed_index(device, bit_count):
    result = jnp.int32(0)
    for level in range(bit_count):
        result = result + device // (1 << level) % 2 * (1 << bit_count - 1 - level)
    return result


def rotate(field, phase_angle, orient):
    return jnp.stack(
        c_mul((field[0], field[1]), (jnp.cos(phase_angle), -orient * jnp.sin(phase_angle)))
    )


def butterfly_forward(field, device, bit_count):
    for level in reversed(range(bit_count)):
        half_size = 1 << level
        partner = swap(field, "narrow", half_size)
        upper = device // half_size % 2
        phase_angle = (device % half_size).astype(jnp.float32) * (math.pi / half_size)
        field = jnp.where(upper == 0, field + partner, rotate(partner - field, phase_angle, 1.0))
    return field


def butterfly_inverse(field, device, bit_count):
    for level in range(bit_count):
        half_size = 1 << level
        partner = swap(field, "narrow", half_size)
        upper = device // half_size % 2
        phase_angle = (device % half_size).astype(jnp.float32) * (math.pi / half_size)
        turned = rotate(jnp.where(upper == 0, partner, field), phase_angle, -1.0)
        field = jnp.where(upper == 0, field + turned, partner - turned)
    return field


def green_of(plane_wave, wave_z, signed_x, total_z, total_x):
    signed_z = jnp.where(wave_z < total_z // 2, wave_z, wave_z - total_z)
    square = (signed_z**2 + plane_wave**2 + signed_x**2).astype(jnp.float32)
    green = 1.0 / (1.0 + square / float(SCREEN * SCREEN)) + float(AMP) / (square + 1.0)
    return green * (1.0 / (total_x * total_z))


def green_values(plane_wave, wave_z, modes, total_z, total_x):
    wave_x = jnp.arange(modes)[:, None] + modes * jnp.arange(total_x // modes)[None, :]
    signed_x = jnp.where(wave_x < total_x // 2, wave_x, wave_x - total_x)
    return green_of(plane_wave, wave_z[None, :, None], signed_x[:, None, :], total_z, total_x)


GROUPS = 4
WIDTH = LANES // GROUPS


def fits(narrow, wide, z_local, x_local):
    rows = z_local // GROUPS
    return (
        narrow == GROUPS
        and x_local == GROUPS * LANES
        and z_local % GROUPS == 0
        and rows % (8 * narrow * wide) == 0
        and rows == 8 * narrow * wide
    )


def swap_lanes(tiles):
    lane = lax.broadcasted_iota(jnp.int32, tiles[0].shape, len(tiles[0].shape) - 1)
    axis = len(tiles[0].shape) - 1
    low = lane % (2 * WIDTH) < WIDTH
    left = lane < 2 * WIDTH
    first = [None] * 4
    for a in range(2):
        one, two = tiles[a], tiles[a + 2]
        first[a] = jnp.where(left, one, pltpu.roll(two, 2 * WIDTH, axis))
        first[a + 2] = jnp.where(left, pltpu.roll(one, 2 * WIDTH, axis), two)
    second = [None] * 4
    for b in (0, 2):
        one, two = first[b], first[b + 1]
        second[b] = jnp.where(low, one, pltpu.roll(two, WIDTH, axis))
        second[b + 1] = jnp.where(low, pltpu.roll(one, LANES - WIDTH, axis), two)
    return second


def pick_lanes(tiles, which):
    axis = len(tiles[0].shape) - 1
    group = lax.broadcasted_iota(jnp.int32, tiles[0].shape, axis) // WIDTH
    result = None
    for g, tile in enumerate(tiles):
        distance = (g - which) * WIDTH % LANES
        moved = pltpu.roll(tile, distance, axis) if distance else tile
        result = moved if result is None else jnp.where(group == g, moved, result)
    return result


def cut_kernel(which, place_ref, in_ref, *out_refs):
    for k in range(GROUPS):
        lanes = pl.ds(pl.multiple_of(place_ref[k] * LANES, LANES), LANES)
        for part in range(2):
            tiles = [in_ref[part, g, :, lanes] for g in range(GROUPS)]
            if len(which) == 1:
                out_refs[k][0, part] = pick_lanes(tiles, which[0])
            else:
                tiles = swap_lanes(tiles)
                for index, q in enumerate(which):
                    out_refs[k][index, part] = tiles[q]


def cut_columns(density, places, which):
    rows, columns = density.shape[2:]
    step = min(rows, 128)
    block = pl.BlockSpec((len(which), 2, step, LANES), lambda i: (0, 0, i, 0))
    shape = jax.ShapeDtypeStruct((len(which), 2, rows, LANES), jnp.float32)
    return pl.pallas_call(
        functools.partial(cut_kernel, which),
        grid=(rows // step,),
        out_shape=[shape] * GROUPS,
        in_specs=[
            pl.BlockSpec(memory_space=pltpu.SMEM),
            pl.BlockSpec((2, GROUPS, step, columns), lambda i: (0, 0, i, 0)),
        ],
        out_specs=[block] * GROUPS,
        compiler_params=params(),
        cost_estimate=pl.CostEstimate(
            flops=8 * rows * columns * len(which),
            bytes_accessed=40 * rows * columns,
            transcendentals=0,
        ),
        name="cut",
    )(places, density)


def place_kernel(chunks, order, place_ref, *refs):
    inputs, out_ref = refs[:-1], refs[-1]
    for k in range(GROUPS):
        lanes = pl.ds(pl.multiple_of(place_ref[k] * LANES, LANES), LANES)
        for part in range(2):
            tiles = [inputs[c * GROUPS + k][index, part] for c, index in order]
            tiles = swap_lanes(tiles)
            for g in range(GROUPS):
                out_ref[part, g, :, lanes] = tiles[g]


def place_columns(chunks, plan, places):
    rows = chunks[0][0].shape[2]
    step = min(rows, 128)
    where = {q: (c, index) for c, which in enumerate(plan) for index, q in enumerate(which)}
    order = [where[q] for q in range(GROUPS)]
    specs, operands = [], []
    for which, chunk in zip(plan, chunks):
        specs += [pl.BlockSpec((len(which), 2, step, LANES), lambda i: (0, 0, i, 0))] * GROUPS
        operands += list(chunk)
    shape = (2, GROUPS, rows, GROUPS * LANES)
    return pl.pallas_call(
        functools.partial(place_kernel, len(plan), order),
        grid=(rows // step,),
        out_shape=jax.ShapeDtypeStruct(shape, jnp.float32),
        in_specs=[pl.BlockSpec(memory_space=pltpu.SMEM)] + specs,
        out_specs=pl.BlockSpec((2, GROUPS, step, GROUPS * LANES), lambda i: (0, 0, i, 0)),
        compiler_params=params(),
        cost_estimate=pl.CostEstimate(
            flops=64 * rows * LANES, bytes_accessed=128 * rows * LANES, transcendentals=0
        ),
        name="place",
    )(places, *operands)


def lines_forward_kernel(rows, slot_ref, mix_ref, high_ref, low_ref, head_ref, turn_ref, *refs):
    inputs, out_ref, first, second = refs[:4], refs[4], refs[5], refs[6]
    tile = 8

    def step(index, carry):
        place = pl.ds(pl.multiple_of(index * tile, tile), tile)
        x = [(ref[0, 0, place, :], ref[0, 1, place, :]) for ref in inputs]
        even = [c_add(x[0], x[2]), c_add(x[1], x[3])]
        odd = [c_sub(x[0], x[2]), c_sub(x[1], x[3])]
        turned = (odd[1][1], -odd[1][0])
        values = [
            c_add(even[0], even[1]),
            c_sub(even[0], even[1]),
            c_add(odd[0], turned),
            c_sub(odd[0], turned),
        ]
        for k in range(4):
            twiddle = (head_ref[k, 0, place, :], head_ref[k, 1, place, :])
            real_part, imag_part = c_mul(values[k], twiddle)
            first[slot_ref[k], place, :LANES] = real_part
            first[slot_ref[k], place, LANES:] = imag_part
        return carry

    lax.fori_loop(0, rows // tile, step, 0)
    dot = functools.partial(jnp.dot, preferred_element_type=jnp.float32)
    for k in range(4):
        value = first[k]
        high = value.astype(jnp.bfloat16)
        low = (value - high.astype(jnp.float32)).astype(jnp.bfloat16)
        value = dot(high, mix_ref[...]) + dot(low, mix_ref[...])
        real_part, imag_part = c_mul(
            (value[:, :LANES], value[:, LANES:]), (turn_ref[0], turn_ref[1])
        )
        second[:rows, k * LANES : (k + 1) * LANES] = real_part
        second[rows:, k * LANES : (k + 1) * LANES] = imag_part
    for side in range(2):
        lanes = slice(2 * side * LANES, 2 * (side + 1) * LANES)
        value = dot3(high_ref[...], low_ref[...], second[:, lanes], True)
        for k in range(2):
            for part in range(2):
                piece = value[part * rows : (part + 1) * rows, k * LANES : (k + 1) * LANES]
                out_ref[:, 0, part, 2 * side + k] = piece.reshape(rows // tile, tile, LANES)


def line_specs(rows, tables):
    return [pl.BlockSpec(memory_space=pltpu.SMEM)] + [whole_spec(table.shape) for table in tables]


def lines_forward(pieces, slots, head, orient_tables):
    count, _, rows, _ = pieces[0].shape
    mixing, matrix, turns = orient_tables
    tables = [mixing, matrix[0], matrix[1], head, turns]
    places = rows // 8
    return pl.pallas_call(
        functools.partial(lines_forward_kernel, rows),
        grid=(count,),
        out_shape=jax.ShapeDtypeStruct((places, count, 2, 4, 8, LANES), jnp.float32),
        in_specs=line_specs(rows, tables)
        + [pl.BlockSpec((1, 2, rows, LANES), lambda i: (i, 0, 0, 0))] * 4,
        out_specs=pl.BlockSpec((places, 1, 2, 4, 8, LANES), lambda i: (0, i, 0, 0, 0, 0)),
        scratch_shapes=[
            pltpu.VMEM((4, rows, 2 * LANES), jnp.float32),
            pltpu.VMEM((2 * rows, 4 * LANES), jnp.float32),
        ],
        compiler_params=params(),
        cost_estimate=pl.CostEstimate(
            flops=LINE_WEIGHT * rows * rows * LANES * count,
            bytes_accessed=64 * rows * LANES * count,
            transcendentals=0,
        ),
        name="lines_forward",
    )(slots, *tables, *pieces)


def lines_inverse_kernel(rows, slot_ref, mix_ref, high_ref, low_ref, head_ref, turn_ref, in_ref, *refs):
    outputs, first, second = refs[:4], refs[4], refs[5]
    tile = 8
    for k in range(4):
        for part in range(2):
            piece = in_ref[:, 0, part, k].reshape(rows, LANES)
            second[part * rows : (part + 1) * rows, k * LANES : (k + 1) * LANES] = piece
    dot = functools.partial(jnp.dot, preferred_element_type=jnp.float32)
    for side in range(2):
        lanes = slice(2 * side * LANES, 2 * (side + 1) * LANES)
        second[:, lanes] = dot3(high_ref[...], low_ref[...], second[:, lanes], True)
    for k in range(4):
        lanes = slice(k * LANES, (k + 1) * LANES)
        real_part, imag_part = c_mul(
            (second[:rows, lanes], second[rows:, lanes]), (turn_ref[0], -turn_ref[1])
        )
        value = jnp.concatenate([real_part, imag_part], axis=1)
        high = value.astype(jnp.bfloat16)
        low = (value - high.astype(jnp.float32)).astype(jnp.bfloat16)
        first[k] = dot(high, mix_ref[...]) + dot(low, mix_ref[...])

    def step(index, carry):
        place = pl.ds(pl.multiple_of(index * tile, tile), tile)
        values = []
        for k in range(4):
            value = (first[slot_ref[k], place, :LANES], first[slot_ref[k], place, LANES:])
            values.append(c_mul(value, (head_ref[k, 0, place, :], -head_ref[k, 1, place, :])))
        even = [c_add(values[0], values[1]), c_sub(values[0], values[1])]
        differ = c_sub(values[2], values[3])
        odd = [c_add(values[2], values[3]), (-differ[1], differ[0])]
        for k in range(2):
            for side, value in enumerate((c_add(even[k], odd[k]), c_sub(even[k], odd[k]))):
                outputs[k + 2 * side][0, 0, place, :] = value[0]
                outputs[k + 2 * side][0, 1, place, :] = value[1]
        return carry

    lax.fori_loop(0, rows // tile, step, 0)


def lines_inverse(blocks, slots, head, orient_tables):
    places, count = blocks.shape[:2]
    rows = places * 8
    mixing, matrix, turns = orient_tables
    tables = [mixing, matrix[0], matrix[1], head, turns]
    return pl.pallas_call(
        functools.partial(lines_inverse_kernel, rows),
        grid=(count,),
        out_shape=[jax.ShapeDtypeStruct((count, 2, rows, LANES), jnp.float32)] * 4,
        in_specs=line_specs(rows, tables)
        + [pl.BlockSpec((places, 1, 2, 4, 8, LANES), lambda i: (0, i, 0, 0, 0, 0))],
        out_specs=[pl.BlockSpec((1, 2, rows, LANES), lambda i: (i, 0, 0, 0))] * 4,
        scratch_shapes=[
            pltpu.VMEM((4, rows, 2 * LANES), jnp.float32),
            pltpu.VMEM((2 * rows, 4 * LANES), jnp.float32),
        ],
        compiler_params=params(),
        cost_estimate=pl.CostEstimate(
            flops=LINE_WEIGHT * rows * rows * LANES * count,
            bytes_accessed=64 * rows * LANES * count,
            transcendentals=0,
        ),
        name="lines_inverse",
    )(slots, *tables, blocks)


def row_filter_kernel(plan, slots, forward_ref, inverse_ref, turn_ref, green_ref, *refs):
    inputs, outputs = refs[: len(plan)], refs[len(plan) : 2 * len(plan)]
    x, held = refs[-2:]
    chunks = 4
    inner = slots * chunks
    modes = inner * GROUPS
    rows = 8
    where = {q: (c, index) for c, which in enumerate(plan) for index, q in enumerate(which)}

    for q in range(GROUPS):
        c, index = where[q]
        columns = []
        for n in range(chunks):
            values = [
                (inputs[c][n * slots + k, index, 0, 0], inputs[c][n * slots + k, index, 1, 0])
                for k in range(slots)
            ]
            values = small_dft(values, -1)
            columns.append([c_const(values[a], a * n, inner, -1) for a in range(slots)])
        for a in range(slots):
            values = small_dft([columns[n][a] for n in range(chunks)], -1)
            for b in range(chunks):
                mode = a + slots * b
                x[q, mode, 0], x[q, mode, 1] = c_const(values[b], q * mode, modes, -1)

    def before(mode, carry):
        values = [(x[q, mode, 0], x[q, mode, 1]) for q in range(GROUPS)]
        values = small_dft(values, -1)
        for e in range(GROUPS):
            where_to = mode + inner * e
            twiddle = (turn_ref[0, pl.ds(where_to, 1), :], turn_ref[1, pl.ds(where_to, 1), :])
            held[where_to, :, :LANES], held[where_to, :, LANES:] = c_mul(values[e], twiddle)
        return carry

    lax.fori_loop(0, inner, before, 0, unroll=8)

    group = 256 // rows

    def middle(index, carry):
        mode = pl.multiple_of(index * group, group)
        value = held[pl.ds(mode, group)].reshape(group * rows, 2 * LANES)
        value = dot3(forward_ref[0], forward_ref[1], value, False)
        green = green_ref[pl.ds(mode, group)].reshape(group * rows, LANES)
        value = value * jnp.concatenate([green, green], axis=1)
        value = dot3(inverse_ref[0], inverse_ref[1], value, False)
        held[pl.ds(mode, group)] = value.reshape(group, rows, 2 * LANES)
        return carry

    lax.fori_loop(0, modes // group, middle, 0, unroll=MIDDLE_UNROLL)

    def after_(mode, carry):
        values = []
        for e in range(GROUPS):
            where_from = mode + inner * e
            twiddle = (turn_ref[0, pl.ds(where_from, 1), :], -turn_ref[1, pl.ds(where_from, 1), :])
            values.append(c_mul((held[where_from, :, :LANES], held[where_from, :, LANES:]), twiddle))
        values = small_dft(values, 1)
        for q in range(GROUPS):
            x[q, mode, 0], x[q, mode, 1] = values[q]
        return carry

    lax.fori_loop(0, inner, after_, 0, unroll=8)

    for q in range(GROUPS):
        c, index = where[q]
        columns = []
        for a in range(slots):
            values = []
            for b in range(chunks):
                mode = a + slots * b
                values.append(c_const((x[q, mode, 0], x[q, mode, 1]), q * mode, modes, 1))
            columns.append(small_dft(values, 1))
        for n in range(chunks):
            values = [c_const(columns[a][n], a * n, inner, 1) for a in range(slots)]
            values = small_dft(values, 1)
            for k in range(slots):
                outputs[c][n * slots + k, index, 0, 0] = values[k][0]
                outputs[c][n * slots + k, index, 1, 0] = values[k][1]


def group_matrix(orient):
    index = np.arange(WIDTH)
    small = np.exp(orient * 2j * np.pi * (np.outer(index, index) % WIDTH) / WIDTH)
    whole = np.kron(np.eye(GROUPS), small)
    return np.stack(split_bf16(np.block([[whole.real, whole.imag], [-whole.imag, whole.real]])))


def row_filter(blocks, plan, turns, green, slots):
    sources = blocks[0].shape[0]
    modes = sources * GROUPS
    forward = jnp.asarray(group_matrix(-1))
    inverse = jnp.asarray(group_matrix(1))
    specs = [
        pl.BlockSpec((sources, len(which), 2, 1, 8, LANES), lambda i: (0, 0, 0, i, 0, 0))
        for which in plan
    ]
    return pl.pallas_call(
        functools.partial(row_filter_kernel, plan, slots),
        grid=(4,),
        out_shape=[jax.ShapeDtypeStruct(block.shape, jnp.float32) for block in blocks],
        in_specs=[
            whole_spec(forward.shape),
            whole_spec(inverse.shape),
            whole_spec(turns.shape),
            pl.BlockSpec((modes, 8, LANES), lambda i: (0, i, 0)),
        ]
        + specs,
        out_specs=specs,
        scratch_shapes=[
            pltpu.VMEM((GROUPS, sources, 2, 8, LANES), jnp.float32),
            pltpu.VMEM((modes, 8, 2 * LANES), jnp.float32),
        ],
        compiler_params=params(),
        cost_estimate=pl.CostEstimate(
            flops=96 * LANES * LANES * modes * 32,
            bytes_accessed=20 * modes * 32 * LANES,
            transcendentals=0,
        ),
        name="row_filter",
    )(forward, inverse, turns, green, *blocks)


def four_plane(density, plane_wave):
    narrow, wide = lax.axis_size("narrow"), lax.axis_size("wide")
    device, place = lax.axis_index("narrow"), lax.axis_index("wide")
    z_local, x_local = density.shape[1:]
    total_z, total_x = z_local * narrow, x_local * wide
    rows = z_local // GROUPS
    modes = narrow * wide * GROUPS
    partners = np.arange(4)

    own = np.arange(4)
    slots = np.stack([0 * own, 2 + 0 * own, 1 + 2 * (own % 2), 3 - 2 * (own % 2)], axis=1)
    sign_low, sign_high = 1.0 - 2.0 * (own % 2), 1.0 - 2.0 * (own // 2)
    phase = np.stack(
        [
            np.ones(4),
            sign_low,
            sign_high * np.where(own % 2 == 0, 1, 1j),
            sign_high * np.where(own % 2 == 0, 1, -1j),
        ],
        axis=1,
    )
    group = np.repeat(np.arange(GROUPS), WIDTH)
    depth = group[None, :] * rows + np.arange(rows)[:, None]
    angle = 2.0 * np.pi * (slots[:, :, None, None] * depth % total_z) / total_z
    head = phase[:, :, None, None] * np.exp(-1j * angle)
    head = pick(np.stack([head.real, head.imag], axis=2).astype(np.float32), device)
    slots = pick(slots.astype(np.int32), device)
    turns = turn(group[None, :] * np.arange(rows)[:, None], GROUPS * rows)
    turns = jnp.asarray(np.moveaxis(turns, 2, 0))
    four = np.exp(-2j * np.pi * (np.outer(partners, partners) % 4) / 4)
    mixing = np.round(np.kron(four, np.eye(WIDTH)))
    ahead = np.block([[mixing.real, mixing.imag], [-mixing.imag, mixing.real]])
    back = np.block([[mixing.real, -mixing.imag], [mixing.imag, mixing.real]])
    tables = (jnp.asarray(ahead.astype(jnp.bfloat16)), jnp.asarray(dft_matrix(rows, -1, True)), turns)
    tables_back = (jnp.asarray(back.astype(jnp.bfloat16)), jnp.asarray(dft_matrix(rows, 1, True)), turns)
    places = device ^ jnp.asarray(partners.astype(np.int32))
    cell = np.tile(np.arange(WIDTH), GROUPS)
    x_turns = turn(np.arange(modes)[:, None] * cell[None, :], total_x)
    x_turns = jnp.asarray(np.moveaxis(x_turns, 2, 0))
    residue = np.arange(4)[:, None, None] + 16 * np.arange(8)[:, None] + 4 * group
    wave_z = jnp.asarray(residue.reshape(32, LANES).astype(np.int32))
    wave_z = wave_z + 16 * 8 * (device * wide + place)
    wave_x = np.arange(modes)[:, None, None] + modes * cell
    signed_x = jnp.asarray(np.where(wave_x < total_x // 2, wave_x, wave_x - total_x).astype(np.int32))
    green = green_of(plane_wave, wave_z[None], signed_x, total_z, total_x)

    source = density.reshape(2, GROUPS, rows, x_local)

    def send(pieces):
        return [pieces[0]] + [swap(pieces[k], "narrow", k) for k in range(1, 4)]

    def trade_all(blocks):
        return lax.all_to_all(blocks, ("narrow", "wide"), 0, 0, tiled=True)

    arrived, got = [], None
    for which in PLAN:
        pieces = cut_columns(source if got is None else source, places, which)
        got = send(pieces if got is None else after(pieces, got))
        arrived.append(trade_all(lines_forward(got, slots, head, tables)))

    filtered = row_filter(arrived, PLAN, x_turns, green, wide)

    back = [None] * len(PLAN)
    for c in reversed(range(len(PLAN))):
        pieces = lines_inverse(trade_all(filtered[c]), slots, head, tables_back)
        back[c] = send(pieces)
    return place_columns(back, PLAN, places).reshape(density.shape)


def plane(density, plane_wave):
    narrow, wide = lax.axis_size("narrow"), lax.axis_size("wide")
    bits = narrow.bit_length() - 1
    device, place = lax.axis_index("narrow"), lax.axis_index("wide")
    z_local, x_local = density.shape[1:]
    total_z, total_x = z_local * narrow, x_local * wide
    rows = z_local // wide
    chunks = x_local // LANES
    modes = wide * chunks
    four = narrow == 4
    low_wave = device if four else reversed_index(device, bits)
    parts = 2 if four else 1
    half = z_local // parts

    waves = [d if four else int(format(d, "b").zfill(bits)[::-1], 2) for d in range(narrow)]
    waves = np.array(waves)
    block = waves[:, None] + narrow * np.arange(wide)
    turns = turn(np.arange(rows) * block[..., None], total_z)
    turns = pick(np.moveaxis(turns, 3, 2), device)
    turns = jnp.broadcast_to(turns[..., None], (wide, 2, rows, LANES))
    head = np.arange(wide) * waves[:, None]
    inner = pick(turn(-head, narrow * wide), device)
    if four:
        give, keep = narrow_terms(1, narrow * wide)
        outer = np.repeat(keep, wide // 2, axis=1) + head[..., None]
        outer = pick(turn(outer, narrow * wide).reshape(narrow, wide, 6), device)
        give = pick(turn(give, narrow * wide).reshape(narrow, 2, 4), device)
        give_back, keep = narrow_terms(-1, narrow * wide)
        give_back = pick(turn(give_back, narrow * wide).reshape(narrow, 2, 4), device)
        last = pick(turn(keep, narrow * wide).reshape(narrow, 2, 6), device)
    else:
        outer = pick(turn(head, narrow * wide), device)
        last = jnp.array([[1.0, 0.0]], jnp.float32)
    x_turns = turn(np.arange(modes)[:, None] * np.arange(LANES)[None, :], total_x)
    x_turns = jnp.asarray(np.moveaxis(x_turns, 2, 0))
    line = jnp.arange(rows, dtype=jnp.int32)
    wave_z = low_wave + narrow * (place + wide * line)
    green = green_values(plane_wave, wave_z, modes, total_z, total_x)

    def part_spec(part, chunk):
        def make(steps):
            first = part * steps
            return pl.BlockSpec((2, half // steps, LANES), lambda i: (0, first + i, chunk))

        return make

    def own_spec(steps):
        return pl.BlockSpec((2, half // steps, LANES), lambda i: (0, i, 0))

    def cut(c, source):
        columns = slice(c * LANES, (c + 1) * LANES)
        return [source[:, p * half : (p + 1) * half, columns] for p in range(parts)]

    def first_swap(pieces):
        return [swap(piece, "narrow", first) for piece, first in zip(pieces, FIRSTS)]

    def second_swap(pieces):
        return [swap(piece, "narrow", 3 - first) for piece, first in zip(pieces, FIRSTS)]

    arrived, pieces = [], [cut(0, density)]
    rest = after(density, pieces[0])
    pieces += [cut(c, rest) for c in range(1, chunks)]
    partner = received = sent = None
    for c in range(chunks):
        if four:
            if c == 0:
                partner = first_swap(pieces[0])
            else:
                partner = first_swap(after(pieces[c], received))
            ready = after(partner, sent) if c else partner
            mixed = mix(
                [[(density, part_spec(p, c)), (ready[p], own_spec)] for p in range(parts)], give, half
            )
            received = second_swap(mixed)
            terms = [
                [
                    (density, part_spec(p, c)(1)),
                    (partner[p], own_spec(1)),
                    (received[p], own_spec(1)),
                ]
                for p in range(parts)
            ]
        else:
            terms = [[(butterfly_forward(piece, device, bits), own_spec(1))] for piece in pieces[c]]
        sent = z_forward(terms, outer, turns, wide, rows)
        arrived.append(trade(sent))

    filtered = x_filter(arrived, x_turns, green)

    result, done = None, []
    for c in range(chunks):
        blocks = after(filtered[c], done[c - 2]) if four and c >= 2 else filtered[c]
        pieces = z_inverse(trade(blocks), inner, turns, parts)
        if four:
            partner = first_swap(pieces)
            ready = after(partner, received) if c else partner
            mixed = mix(
                [[(pieces[p], own_spec), (ready[p], own_spec)] for p in range(parts)], give_back, half
            )
            done.append(mixed)
            received = second_swap(mixed)
            pieces = [[pieces[p], partner[p], received[p]] for p in range(parts)]
        else:
            pieces = [[butterfly_inverse(piece, device, bits)] for piece in pieces]
        result = finish(pieces, last, c, chunks, result)
    return result.reshape(density.shape)


def shards(density, plane_wave):
    sizes = lax.axis_size("narrow"), lax.axis_size("wide")
    one = four_plane if fits(*sizes, *density.shape[2:]) else plane
    planes = [one(density[:, y], plane_wave[y]) for y in range(density.shape[1])]
    return jnp.stack(planes, axis=1)


def solution(mesh):
    in_specs = (P(None, None, "narrow", "wide"), P())
    out_specs = P(None, None, "narrow", "wide")
    return jax.shard_map(shards, mesh=mesh, in_specs=in_specs, out_specs=out_specs, check_vma=False)
```

```python
import functools
import math

import jax
import jax.numpy as jnp
import numpy as np
from jax import lax
from jax.experimental import pallas as pl
from jax.experimental.pallas import tpu as pltpu
from jax.sharding import PartitionSpec as P

SCREEN = 1024
AMP = 2048
LANES = 128
MIX_WEIGHT = 480
LINE_WEIGHT = 3000
BACK_WEIGHT = 3000
ADD_STEP = 128
MIDDLE_UNROLL = 4
PLAN = ((0,), (1,), (2, 3))
VMEM_LIMIT = 48 * 1024 * 1024
FIRSTS = (1, 2)


def split_bf16(value):
    high = np.asarray(value, np.float64).astype(np.float32).astype(jnp.bfloat16)
    low = (value - high.astype(np.float64)).astype(np.float32).astype(jnp.bfloat16)
    return high, low


def dft_matrix(length, orient, left):
    index = np.arange(length)
    angle = 2.0 * np.pi * ((index[:, None] * index[None, :]) % length) / length
    cosine, sine = np.cos(angle), orient * np.sin(angle)
    if left:
        whole = np.block([[cosine, -sine], [sine, cosine]])
    else:
        whole = np.block([[cosine, sine], [-sine, cosine]])
    high, low = split_bf16(whole)
    return np.stack([high, low])


def turn(numerator, length):
    angle = (np.asarray(numerator) % length) * (2.0 * np.pi / length)
    return np.stack([np.cos(angle), -np.sin(angle)], axis=-1).astype(np.float32)


def c_add(a, b):
    return (a[0] + b[0], a[1] + b[1])


def c_sub(a, b):
    return (a[0] - b[0], a[1] - b[1])


def c_mul(a, b):
    return (a[0] * b[0] - a[1] * b[1], a[0] * b[1] + a[1] * b[0])


def c_const(a, numerator, length, orient):
    numerator = (orient * numerator) % length
    if numerator == 0:
        return a
    if 2 * numerator == length:
        return (-a[0], -a[1])
    if 4 * numerator == length:
        return (-a[1], a[0])
    if 4 * numerator == 3 * length:
        return (a[1], -a[0])
    angle = 2.0 * math.pi * numerator / length
    cosine, sine = math.cos(angle), math.sin(angle)
    if 8 * numerator % length == 0:
        root = math.sqrt(0.5)
        total, differ = (a[0] + a[1]) * root, (a[0] - a[1]) * root
        if cosine > 0 and sine > 0:
            return (differ, total)
        if cosine > 0:
            return (total, -differ)
        if sine > 0:
            return (-total, differ)
        return (-differ, -total)
    return (a[0] * cosine - a[1] * sine, a[0] * sine + a[1] * cosine)


def small_dft(values, orient):
    count = len(values)
    if count == 1:
        return values
    half = count // 2
    upper = [c_add(values[i], values[i + half]) for i in range(half)]
    lower = [
        c_const(c_sub(values[i], values[i + half]), i, count, orient) for i in range(half)
    ]
    even, odd = small_dft(upper, orient), small_dft(lower, orient)
    result = []
    for i in range(half):
        result += [even[i], odd[i]]
    return result


def dot3(high, low, value, left):
    value_high = value.astype(jnp.bfloat16)
    value_low = (value - value_high.astype(jnp.float32)).astype(jnp.bfloat16)
    dot = functools.partial(jnp.dot, preferred_element_type=jnp.float32)
    if left:
        return dot(high, value_high) + (dot(high, value_low) + dot(low, value_high))
    return dot(value_high, high) + (dot(value_low, high) + dot(value_high, low))


def whole_spec(shape):
    return pl.BlockSpec(shape, lambda *_: (0,) * len(shape))


def params():
    return pltpu.CompilerParams(vmem_limit_bytes=VMEM_LIMIT)


def combine(inputs, coef_ref, row, place):
    total = None
    for term, ref in enumerate(inputs):
        value = (ref[0, place, :], ref[1, place, :])
        product = c_mul(value, (coef_ref[row, 2 * term], coef_ref[row, 2 * term + 1]))
        total = product if total is None else c_add(total, product)
    return total


def z_forward_kernel(terms, parts, slots, rows, coef_ref, matrix_ref, turn_ref, *refs):
    inputs = refs[: terms * parts]
    out_ref, held = refs[-2:]
    per_part = slots // parts
    tile = min(rows, 8)

    def step(index, carry):
        row = pl.multiple_of(index * tile, tile)
        values = []
        for h in range(slots):
            part, inner = divmod(h, per_part)
            place = pl.ds(inner * rows + row, tile)
            values.append(combine(inputs[part * terms : (part + 1) * terms], coef_ref, h, place))
        values = small_dft(values, -1)
        for k in range(slots):
            twiddle = (
                turn_ref[k, 0, pl.ds(row, tile), :],
                turn_ref[k, 1, pl.ds(row, tile), :],
            )
            real_part, imag_part = c_mul(values[k], twiddle)
            held[pl.ds(row, tile), k * LANES : (k + 1) * LANES] = real_part
            held[pl.ds(rows + row, tile), k * LANES : (k + 1) * LANES] = imag_part
        return carry

    lax.fori_loop(0, rows // tile, step, 0)
    result = dot3(matrix_ref[0], matrix_ref[1], held[...], True)
    for k in range(slots):
        out_ref[k, 0] = result[:rows, k * LANES : (k + 1) * LANES]
        out_ref[k, 1] = result[rows:, k * LANES : (k + 1) * LANES]


def z_forward(parts, coef, turns, slots, rows):
    terms = len(parts[0])
    flat = [pair for part in parts for pair in part]
    matrix = jnp.asarray(dft_matrix(rows, -1, True))
    shape = (slots, 2, rows, LANES)
    return pl.pallas_call(
        functools.partial(z_forward_kernel, terms, len(parts), slots, rows),
        grid=(1,),
        out_shape=jax.ShapeDtypeStruct(shape, jnp.float32),
        in_specs=[
            pl.BlockSpec(memory_space=pltpu.SMEM),
            whole_spec(matrix.shape),
            whole_spec(turns.shape),
        ]
        + [spec for _, spec in flat],
        out_specs=whole_spec(shape),
        scratch_shapes=[pltpu.VMEM((2 * rows, slots * LANES), jnp.float32)],
        compiler_params=params(),
        cost_estimate=pl.CostEstimate(
            flops=700 * rows * rows * slots * LANES,
            bytes_accessed=32 * rows * slots * LANES,
            transcendentals=0,
        ),
        name="z_forward",
    )(coef, matrix, turns, *[array for array, _ in flat])


def z_inverse_kernel(parts, slots, rows, coef_ref, matrix_ref, turn_ref, in_ref, *refs):
    outputs, held = refs[:parts], refs[parts]
    per_part = slots // parts
    tile = min(rows, 8)
    for k in range(slots):
        held[:rows, k * LANES : (k + 1) * LANES] = in_ref[k, 0]
        held[rows:, k * LANES : (k + 1) * LANES] = in_ref[k, 1]
    held[...] = dot3(matrix_ref[0], matrix_ref[1], held[...], True)

    def step(index, carry):
        row = pl.multiple_of(index * tile, tile)
        values = []
        for k in range(slots):
            value = (
                held[pl.ds(row, tile), k * LANES : (k + 1) * LANES],
                held[pl.ds(rows + row, tile), k * LANES : (k + 1) * LANES],
            )
            twiddle = (
                turn_ref[k, 0, pl.ds(row, tile), :],
                -turn_ref[k, 1, pl.ds(row, tile), :],
            )
            values.append(c_mul(value, twiddle))
        values = small_dft(values, 1)
        for h in range(slots):
            part, inner = divmod(h, per_part)
            real_part, imag_part = c_mul(values[h], (coef_ref[h, 0], coef_ref[h, 1]))
            outputs[part][0, pl.ds(inner * rows + row, tile), :] = real_part
            outputs[part][1, pl.ds(inner * rows + row, tile), :] = imag_part
        return carry

    lax.fori_loop(0, rows // tile, step, 0)


def z_inverse(blocks, coef, turns, parts):
    slots, _, rows, _ = blocks.shape
    matrix = jnp.asarray(dft_matrix(rows, 1, True))
    shape = (2, slots // parts * rows, LANES)
    return pl.pallas_call(
        functools.partial(z_inverse_kernel, parts, slots, rows),
        grid=(1,),
        out_shape=[jax.ShapeDtypeStruct(shape, jnp.float32)] * parts,
        in_specs=[
            pl.BlockSpec(memory_space=pltpu.SMEM),
            whole_spec(matrix.shape),
            whole_spec(turns.shape),
            whole_spec(blocks.shape),
        ],
        out_specs=[whole_spec(shape)] * parts,
        scratch_shapes=[pltpu.VMEM((2 * rows, slots * LANES), jnp.float32)],
        compiler_params=params(),
        cost_estimate=pl.CostEstimate(
            flops=700 * rows * rows * slots * LANES,
            bytes_accessed=20 * rows * slots * LANES,
            transcendentals=0,
        ),
        name="z_inverse",
    )(coef, matrix, turns, blocks)


def x_filter_kernel(slots, chunks, rows, forward_ref, inverse_ref, turn_ref, green_ref, *refs):
    inputs = refs[:chunks]
    outputs = refs[chunks : 2 * chunks]
    held = refs[-1]
    tile = 8
    modes = slots * chunks

    def before(index, carry):
        row = pl.multiple_of(index * tile, tile)
        place = pl.ds(row, tile)
        columns = []
        for c in range(chunks):
            values = [
                (inputs[c][k, 0, place, :], inputs[c][k, 1, place, :]) for k in range(slots)
            ]
            values = small_dft(values, -1)
            columns.append([c_const(values[a], a * c, modes, -1) for a in range(slots)])
        for a in range(slots):
            values = small_dft([columns[c][a] for c in range(chunks)], -1)
            for b in range(chunks):
                mode = a + slots * b
                twiddle = (turn_ref[0, mode : mode + 1, :], turn_ref[1, mode : mode + 1, :])
                real_part, imag_part = c_mul(values[b], twiddle)
                held[mode, place, :LANES] = real_part
                held[mode, place, LANES:] = imag_part
        return carry

    lax.fori_loop(0, rows // tile, before, 0)

    group = max(1, min(modes, 256 // rows))

    def middle(index, carry):
        mode = pl.multiple_of(index * group, group)
        value = held[pl.ds(mode, group)].reshape(group * rows, 2 * LANES)
        value = dot3(forward_ref[0], forward_ref[1], value, False)
        green = green_ref[pl.ds(mode, group)].reshape(group * rows, LANES)
        value = value * jnp.concatenate([green, green], axis=1)
        value = dot3(inverse_ref[0], inverse_ref[1], value, False)
        held[pl.ds(mode, group)] = value.reshape(group, rows, 2 * LANES)
        return carry

    lax.fori_loop(0, modes // group, middle, 0)

    def after(index, carry):
        row = pl.multiple_of(index * tile, tile)
        place = pl.ds(row, tile)
        columns = []
        for a in range(slots):
            values = []
            for b in range(chunks):
                mode = a + slots * b
                twiddle = (turn_ref[0, mode : mode + 1, :], -turn_ref[1, mode : mode + 1, :])
                values.append(c_mul((held[mode, place, :LANES], held[mode, place, LANES:]), twiddle))
            columns.append(small_dft(values, 1))
        for c in range(chunks):
            values = [c_const(columns[a][c], a * c, modes, 1) for a in range(slots)]
            values = small_dft(values, 1)
            for k in range(slots):
                outputs[c][k, 0, place, :] = values[k][0]
                outputs[c][k, 1, place, :] = values[k][1]
        return carry

    lax.fori_loop(0, rows // tile, after, 0)


def x_filter(blocks, turns, green):
    chunks = len(blocks)
    slots, _, rows, _ = blocks[0].shape
    step = min(rows, 32)
    modes = slots * chunks
    forward = jnp.asarray(dft_matrix(LANES, -1, False))
    inverse = jnp.asarray(dft_matrix(LANES, 1, False))
    block = pl.BlockSpec((slots, 2, step, LANES), lambda i: (0, 0, i, 0))
    return pl.pallas_call(
        functools.partial(x_filter_kernel, slots, chunks, step),
        grid=(rows // step,),
        out_shape=[jax.ShapeDtypeStruct(blocks[0].shape, jnp.float32)] * chunks,
        in_specs=[
            whole_spec(forward.shape),
            whole_spec(inverse.shape),
            whole_spec(turns.shape),
            pl.BlockSpec((modes, step, LANES), lambda i: (0, i, 0)),
        ]
        + [block] * chunks,
        out_specs=[block] * chunks,
        scratch_shapes=[pltpu.VMEM((modes, step, 2 * LANES), jnp.float32)],
        compiler_params=params(),
        cost_estimate=pl.CostEstimate(
            flops=96 * LANES * LANES * modes * rows,
            bytes_accessed=20 * modes * rows * LANES,
            transcendentals=0,
        ),
        name="x_filter",
    )(forward, inverse, turns, green, *blocks)


def mix_kernel(terms, parts, coef_ref, *refs):
    for part in range(parts):
        out_ref = refs[terms * parts + part]
        inputs = refs[part * terms : (part + 1) * terms]
        total = combine(inputs, coef_ref, part, slice(None))
        out_ref[0], out_ref[1] = total


def mix(parts, coef, rows):
    terms = len(parts[0])
    flat = [pair for part in parts for pair in part]
    steps = 4 if rows % 32 == 0 else 1
    return pl.pallas_call(
        functools.partial(mix_kernel, terms, len(parts)),
        grid=(steps,),
        out_shape=[jax.ShapeDtypeStruct((2, rows, LANES), jnp.float32)] * len(parts),
        in_specs=[pl.BlockSpec(memory_space=pltpu.SMEM)] + [make(steps) for _, make in flat],
        out_specs=[pl.BlockSpec((2, rows // steps, LANES), lambda i: (0, i, 0))] * len(parts),
        compiler_params=params(),
        cost_estimate=pl.CostEstimate(
            flops=20 * rows * LANES * len(parts),
            bytes_accessed=MIX_WEIGHT * rows * LANES * len(parts),
            transcendentals=0,
        ),
        name="mix",
    )(coef, *[array for array, _ in flat])


def finish_kernel(terms, parts, coef_ref, *refs):
    out_ref = refs[-1]
    for part in range(parts):
        inputs = refs[part * terms : (part + 1) * terms]
        total = combine(inputs, coef_ref, part, slice(None))
        out_ref[0, part], out_ref[1, part] = total


def finish(parts, coef, chunk, chunks, so_far):
    terms = len(parts[0])
    flat = [array for part in parts for array in part]
    rows = parts[0][0].shape[1]
    steps = 4 if rows % 32 == 0 else 1
    extra = [] if so_far is None else [so_far]
    return pl.pallas_call(
        functools.partial(finish_kernel, terms, len(parts)),
        grid=(steps,),
        out_shape=jax.ShapeDtypeStruct((2, len(parts), rows, chunks * LANES), jnp.float32),
        in_specs=[pl.BlockSpec(memory_space=pltpu.SMEM)]
        + [pl.BlockSpec((2, rows // steps, LANES), lambda i: (0, i, 0))] * len(flat)
        + [pl.BlockSpec(memory_space=pl.ANY)] * len(extra),
        out_specs=pl.BlockSpec((2, len(parts), rows // steps, LANES), lambda i: (0, 0, i, chunk)),
        input_output_aliases={1 + len(flat): 0} if extra else {},
        compiler_params=params(),
        cost_estimate=pl.CostEstimate(
            flops=20 * rows * LANES * len(parts),
            bytes_accessed=32 * rows * LANES * len(parts),
            transcendentals=0,
        ),
        name="finish",
    )(coef, *flat, *extra)


def after(value, *others):
    return lax.optimization_barrier((value, others))[0]


def swap(value, axis, mask):
    pairs = [(source, source ^ mask) for source in range(lax.axis_size(axis))]
    return lax.ppermute(value, axis, pairs)


def trade(blocks):
    return lax.all_to_all(blocks, "wide", 0, 0, tiled=True)


def narrow_terms(orient, length):
    give, keep = [], []
    for device in range(4):
        for first in FIRSTS:
            there = device ^ (3 - first)
            unit = orient * (length // 4)
            give.append([there * device * unit, there * (device ^ first) * unit])
            keep.append([device * device * unit, device * (device ^ first) * unit, 0])
    shape = (4, len(FIRSTS), -1)
    return np.array(give).reshape(shape), np.array(keep).reshape(shape)


def pick(table, index):
    return lax.dynamic_index_in_dim(jnp.asarray(table), index, 0, keepdims=False)


def reversed_index(device, bit_count):
    result = jnp.int32(0)
    for level in range(bit_count):
        result = result + device // (1 << level) % 2 * (1 << bit_count - 1 - level)
    return result


def rotate(field, phase_angle, orient):
    return jnp.stack(
        c_mul((field[0], field[1]), (jnp.cos(phase_angle), -orient * jnp.sin(phase_angle)))
    )


def butterfly_forward(field, device, bit_count):
    for level in reversed(range(bit_count)):
        half_size = 1 << level
        partner = swap(field, "narrow", half_size)
        upper = device // half_size % 2
        phase_angle = (device % half_size).astype(jnp.float32) * (math.pi / half_size)
        field = jnp.where(upper == 0, field + partner, rotate(partner - field, phase_angle, 1.0))
    return field


def butterfly_inverse(field, device, bit_count):
    for level in range(bit_count):
        half_size = 1 << level
        partner = swap(field, "narrow", half_size)
        upper = device // half_size % 2
        phase_angle = (device % half_size).astype(jnp.float32) * (math.pi / half_size)
        turned = rotate(jnp.where(upper == 0, partner, field), phase_angle, -1.0)
        field = jnp.where(upper == 0, field + turned, partner - turned)
    return field


def green_of(plane_wave, wave_z, signed_x, total_z, total_x):
    signed_z = jnp.where(wave_z < total_z // 2, wave_z, wave_z - total_z)
    square = (signed_z**2 + plane_wave**2 + signed_x**2).astype(jnp.float32)
    green = 1.0 / (1.0 + square / float(SCREEN * SCREEN)) + float(AMP) / (square + 1.0)
    return green * (1.0 / (total_x * total_z))


def green_values(plane_wave, wave_z, modes, total_z, total_x):
    wave_x = jnp.arange(modes)[:, None] + modes * jnp.arange(total_x // modes)[None, :]
    signed_x = jnp.where(wave_x < total_x // 2, wave_x, wave_x - total_x)
    return green_of(plane_wave, wave_z[None, :, None], signed_x[:, None, :], total_z, total_x)


GROUPS = 4
WIDTH = LANES // GROUPS


def fits(narrow, wide, z_local, x_local):
    rows = z_local // GROUPS
    return (
        narrow == GROUPS
        and x_local == GROUPS * LANES
        and z_local % GROUPS == 0
        and rows % (8 * narrow * wide) == 0
        and rows == 8 * narrow * wide
    )


def swap_lanes(tiles):
    lane = lax.broadcasted_iota(jnp.int32, tiles[0].shape, len(tiles[0].shape) - 1)
    axis = len(tiles[0].shape) - 1
    low = lane % (2 * WIDTH) < WIDTH
    left = lane < 2 * WIDTH
    first = [None] * 4
    for a in range(2):
        one, two = tiles[a], tiles[a + 2]
        first[a] = jnp.where(left, one, pltpu.roll(two, 2 * WIDTH, axis))
        first[a + 2] = jnp.where(left, pltpu.roll(one, 2 * WIDTH, axis), two)
    second = [None] * 4
    for b in (0, 2):
        one, two = first[b], first[b + 1]
        second[b] = jnp.where(low, one, pltpu.roll(two, WIDTH, axis))
        second[b + 1] = jnp.where(low, pltpu.roll(one, LANES - WIDTH, axis), two)
    return second


def pick_lanes(tiles, which):
    axis = len(tiles[0].shape) - 1
    group = lax.broadcasted_iota(jnp.int32, tiles[0].shape, axis) // WIDTH
    result = None
    for g, tile in enumerate(tiles):
        distance = (g - which) * WIDTH % LANES
        moved = pltpu.roll(tile, distance, axis) if distance else tile
        result = moved if result is None else jnp.where(group == g, moved, result)
    return result


def cut_kernel(which, in_ref, out_ref):
    for part in range(2):
        tiles = [in_ref[part, g] for g in range(GROUPS)]
        if len(which) == 1:
            out_ref[0, part] = pick_lanes(tiles, which[0])
        else:
            tiles = swap_lanes(tiles)
            for index, q in enumerate(which):
                out_ref[index, part] = tiles[q]


def cut_columns(density, which, partner):
    rows = density.shape[2]
    step = min(rows, 128)
    return pl.pallas_call(
        functools.partial(cut_kernel, which),
        grid=(rows // step,),
        in_specs=[
            pl.BlockSpec(
                (2, GROUPS, step, LANES), lambda i: (0, 0, i, lax.axis_index("narrow") ^ partner)
            )
        ],
        out_specs=pl.BlockSpec((len(which), 2, step, LANES), lambda i: (0, 0, i, 0)),
        out_shape=jax.ShapeDtypeStruct((len(which), 2, rows, LANES), jnp.float32),
        compiler_params=params(),
        cost_estimate=pl.CostEstimate(
            flops=8 * rows * LANES * len(which),
            bytes_accessed=40 * rows * LANES,
            transcendentals=0,
        ),
        name="cut",
    )(density)


def place_kernel(order, *refs):
    inputs, out_ref = refs[:-1], refs[-1]
    device = lax.axis_index("narrow")
    for k in range(GROUPS):
        lanes = pl.ds(pl.multiple_of((device ^ k) * LANES, LANES), LANES)
        for part in range(2):
            tiles = [
                jnp.zeros(out_ref.shape[2:3] + (LANES,), jnp.float32)
                if spot is None
                else inputs[spot[0] * GROUPS + k][spot[1], part]
                for spot in order
            ]
            for g, value in enumerate(swap_lanes(tiles)):
                out_ref[part, g, :, lanes] = value


def add_kernel(which, *refs):
    inputs, so_far_ref, out_ref = refs[:4], refs[4], refs[5]
    device = lax.axis_index("narrow")
    group = lax.broadcasted_iota(jnp.int32, (out_ref.shape[2], LANES), 1) // WIDTH
    for k in range(GROUPS):
        lanes = pl.ds(pl.multiple_of((device ^ k) * LANES, LANES), LANES)
        for part in range(2):
            tile = inputs[k][0, part]
            for g in range(GROUPS):
                distance = (which - g) * WIDTH % LANES
                moved = pltpu.roll(tile, distance, 1) if distance else tile
                value = jnp.where(group == which, moved, so_far_ref[part, g, :, lanes])
                out_ref[part, g, :, lanes] = value


def place_columns(chunks, plan):
    specs, operands, order = [], [], [None] * GROUPS
    for which, chunk in zip(plan, chunks):
        if chunk is None:
            continue
        rows = chunk[0].shape[2]
        step = min(rows, 128)
        for index, q in enumerate(which):
            order[q] = (len(operands) // GROUPS, index)
        specs += [pl.BlockSpec((len(which), 2, step, LANES), lambda i: (0, 0, i, 0))] * GROUPS
        operands += list(chunk)
    shape = (2, GROUPS, rows, GROUPS * LANES)
    return pl.pallas_call(
        functools.partial(place_kernel, order),
        grid=(rows // step,),
        out_shape=jax.ShapeDtypeStruct(shape, jnp.float32),
        in_specs=specs,
        out_specs=pl.BlockSpec((2, GROUPS, step, GROUPS * LANES), lambda i: (0, 0, i, 0)),
        compiler_params=params(),
        cost_estimate=pl.CostEstimate(
            flops=64 * rows * LANES, bytes_accessed=128 * rows * LANES, transcendentals=0
        ),
        name="place",
    )(*operands)


def add_columns(chunk, which, so_far):
    rows = chunk[0].shape[2]
    step = min(rows, ADD_STEP)
    block = pl.BlockSpec((2, GROUPS, step, GROUPS * LANES), lambda i: (0, 0, i, 0))
    return pl.pallas_call(
        functools.partial(add_kernel, which),
        grid=(rows // step,),
        out_shape=jax.ShapeDtypeStruct(so_far.shape, jnp.float32),
        in_specs=[pl.BlockSpec((1, 2, step, LANES), lambda i: (0, 0, i, 0))] * GROUPS + [block],
        out_specs=block,
        input_output_aliases={GROUPS: 0},
        compiler_params=params(),
        cost_estimate=pl.CostEstimate(
            flops=64 * rows * LANES, bytes_accessed=128 * rows * LANES, transcendentals=0
        ),
        name="add",
    )(*chunk, so_far)


def fetch(sources, held, semaphores):
    copies = [
        pltpu.make_async_copy(source, there, semaphores.at[i])
        for i, (source, there) in enumerate(zip(sources, held))
    ]

    @pl.when(pl.program_id(0) == 0)
    def start():
        for copy in copies:
            copy.start()

    def wait(*which):
        @pl.when(pl.program_id(0) == 0)
        def finish_copies():
            for i in which:
                copies[i].wait()

    return wait


def lines_forward_kernel(rows, slot_ref, *refs):
    sources, inputs = refs[:4], refs[4:8]
    out_ref, first, second, head_ref, mix_ref, matrix_ref, turn_ref, semaphores = refs[8:]
    tile = 8
    wait = fetch(sources, (head_ref, mix_ref, matrix_ref, turn_ref), semaphores)
    wait(0)

    def step(index, carry):
        place = pl.ds(pl.multiple_of(index * tile, tile), tile)
        x = [(ref[0, 0, place, :], ref[0, 1, place, :]) for ref in inputs]
        even = [c_add(x[0], x[2]), c_add(x[1], x[3])]
        odd = [c_sub(x[0], x[2]), c_sub(x[1], x[3])]
        turned = (odd[1][1], -odd[1][0])
        values = [
            c_add(even[0], even[1]),
            c_sub(even[0], even[1]),
            c_add(odd[0], turned),
            c_sub(odd[0], turned),
        ]
        for k in range(4):
            twiddle = (head_ref[k, 0, place, :], head_ref[k, 1, place, :])
            real_part, imag_part = c_mul(values[k], twiddle)
            first[slot_ref[k], place, :LANES] = real_part
            first[slot_ref[k], place, LANES:] = imag_part
        return carry

    lax.fori_loop(0, rows // tile, step, 0)
    wait(1, 2, 3)
    dot = functools.partial(jnp.dot, preferred_element_type=jnp.float32)
    for k in range(4):
        value = first[k]
        high = value.astype(jnp.bfloat16)
        low = (value - high.astype(jnp.float32)).astype(jnp.bfloat16)
        value = dot(high, mix_ref[...]) + dot(low, mix_ref[...])
        real_part, imag_part = c_mul(
            (value[:, :LANES], value[:, LANES:]), (turn_ref[0], turn_ref[1])
        )
        second[:rows, k * LANES : (k + 1) * LANES] = real_part
        second[rows:, k * LANES : (k + 1) * LANES] = imag_part
    for side in range(2):
        lanes = slice(2 * side * LANES, 2 * (side + 1) * LANES)
        value = dot3(matrix_ref[0], matrix_ref[1], second[:, lanes], True)
        for k in range(2):
            for part in range(2):
                piece = value[part * rows : (part + 1) * rows, k * LANES : (k + 1) * LANES]
                out_ref[:, 0, part, 2 * side + k] = piece.reshape(rows // tile, tile, LANES)


def line_specs():
    return [pl.BlockSpec(memory_space=pltpu.SMEM)] + [pl.BlockSpec(memory_space=pl.ANY)] * 4


def line_scratch(rows, tables):
    return (
        [
            pltpu.VMEM((4, rows, 2 * LANES), jnp.float32),
            pltpu.VMEM((2 * rows, 4 * LANES), jnp.float32),
        ]
        + [pltpu.VMEM(table.shape, table.dtype) for table in tables]
        + [pltpu.SemaphoreType.DMA((len(tables),))]
    )


def lines_forward(pieces, slots, head, tables):
    count, _, rows, _ = pieces[0].shape
    places = rows // 8
    return pl.pallas_call(
        functools.partial(lines_forward_kernel, rows),
        grid=(count,),
        out_shape=jax.ShapeDtypeStruct((places, count, 2, 4, 8, LANES), jnp.float32),
        in_specs=line_specs()
        + [pl.BlockSpec((1, 2, rows, LANES), lambda i: (i, 0, 0, 0))] * 4,
        out_specs=pl.BlockSpec((places, 1, 2, 4, 8, LANES), lambda i: (0, i, 0, 0, 0, 0)),
        scratch_shapes=line_scratch(rows, (head, *tables)),
        compiler_params=params(),
        cost_estimate=pl.CostEstimate(
            flops=LINE_WEIGHT * rows * rows * LANES * count,
            bytes_accessed=64 * rows * LANES * count,
            transcendentals=0,
        ),
        name="lines_forward",
    )(slots, head, *tables, *pieces)


def lines_inverse_kernel(rows, slot_ref, *refs):
    sources, in_ref, outputs = refs[:4], refs[4], refs[5:9]
    first, second, head_ref, mix_ref, matrix_ref, turn_ref, semaphores = refs[9:]
    tile = 8
    wait = fetch(sources, (head_ref, mix_ref, matrix_ref, turn_ref), semaphores)
    for k in range(4):
        for part in range(2):
            piece = in_ref[:, 0, part, k].reshape(rows, LANES)
            second[part * rows : (part + 1) * rows, k * LANES : (k + 1) * LANES] = piece
    dot = functools.partial(jnp.dot, preferred_element_type=jnp.float32)
    wait(2)
    for side in range(2):
        lanes = slice(2 * side * LANES, 2 * (side + 1) * LANES)
        second[:, lanes] = dot3(matrix_ref[0], matrix_ref[1], second[:, lanes], True)
    wait(0, 1, 3)
    for k in range(4):
        lanes = slice(k * LANES, (k + 1) * LANES)
        real_part, imag_part = c_mul(
            (second[:rows, lanes], second[rows:, lanes]), (turn_ref[0], -turn_ref[1])
        )
        value = jnp.concatenate([real_part, imag_part], axis=1)
        high = value.astype(jnp.bfloat16)
        low = (value - high.astype(jnp.float32)).astype(jnp.bfloat16)
        first[k] = dot(high, mix_ref[...]) + dot(low, mix_ref[...])

    def step(index, carry):
        place = pl.ds(pl.multiple_of(index * tile, tile), tile)
        values = []
        for k in range(4):
            value = (first[slot_ref[k], place, :LANES], first[slot_ref[k], place, LANES:])
            values.append(c_mul(value, (head_ref[k, 0, place, :], -head_ref[k, 1, place, :])))
        even = [c_add(values[0], values[1]), c_sub(values[0], values[1])]
        differ = c_sub(values[2], values[3])
        odd = [c_add(values[2], values[3]), (-differ[1], differ[0])]
        for k in range(2):
            for side, value in enumerate((c_add(even[k], odd[k]), c_sub(even[k], odd[k]))):
                outputs[k + 2 * side][0, 0, place, :] = value[0]
                outputs[k + 2 * side][0, 1, place, :] = value[1]
        return carry

    lax.fori_loop(0, rows // tile, step, 0)


def lines_inverse(blocks, slots, head, tables):
    places, count = blocks.shape[:2]
    rows = places * 8
    return pl.pallas_call(
        functools.partial(lines_inverse_kernel, rows),
        grid=(count,),
        out_shape=[jax.ShapeDtypeStruct((count, 2, rows, LANES), jnp.float32)] * 4,
        in_specs=line_specs()
        + [pl.BlockSpec((places, 1, 2, 4, 8, LANES), lambda i: (0, i, 0, 0, 0, 0))],
        out_specs=[pl.BlockSpec((1, 2, rows, LANES), lambda i: (i, 0, 0, 0))] * 4,
        scratch_shapes=line_scratch(rows, (head, *tables)),
        compiler_params=params(),
        cost_estimate=pl.CostEstimate(
            flops=BACK_WEIGHT * rows * rows * LANES * count,
            bytes_accessed=64 * rows * LANES * count,
            transcendentals=0,
        ),
        name="lines_inverse",
    )(slots, head, *tables, blocks)


def row_filter_kernel(plan, slots, forward_ref, inverse_ref, turn_ref, green_ref, *refs):
    inputs, outputs = refs[: len(plan)], refs[len(plan) : 2 * len(plan)]
    x, held = refs[-2:]
    chunks = 4
    inner = slots * chunks
    modes = inner * GROUPS
    rows = 8
    where = {q: (c, index) for c, which in enumerate(plan) for index, q in enumerate(which)}

    for q in range(GROUPS):
        c, index = where[q]
        columns = []
        for n in range(chunks):
            values = [
                (inputs[c][n * slots + k, index, 0, 0], inputs[c][n * slots + k, index, 1, 0])
                for k in range(slots)
            ]
            values = small_dft(values, -1)
            columns.append([c_const(values[a], a * n, inner, -1) for a in range(slots)])
        for a in range(slots):
            values = small_dft([columns[n][a] for n in range(chunks)], -1)
            for b in range(chunks):
                mode = a + slots * b
                x[q, mode, 0], x[q, mode, 1] = c_const(values[b], q * mode, modes, -1)

    def before(mode, carry):
        values = [(x[q, mode, 0], x[q, mode, 1]) for q in range(GROUPS)]
        values = small_dft(values, -1)
        for e in range(GROUPS):
            where_to = mode + inner * e
            twiddle = (turn_ref[0, pl.ds(where_to, 1), :], turn_ref[1, pl.ds(where_to, 1), :])
            held[where_to, :, :LANES], held[where_to, :, LANES:] = c_mul(values[e], twiddle)
        return carry

    lax.fori_loop(0, inner, before, 0, unroll=8)

    group = 256 // rows

    def middle(index, carry):
        mode = pl.multiple_of(index * group, group)
        value = held[pl.ds(mode, group)].reshape(group * rows, 2 * LANES)
        value = dot3(forward_ref[0], forward_ref[1], value, False)
        green = green_ref[pl.ds(mode, group)].reshape(group * rows, LANES)
        value = value * jnp.concatenate([green, green], axis=1)
        value = dot3(inverse_ref[0], inverse_ref[1], value, False)
        held[pl.ds(mode, group)] = value.reshape(group, rows, 2 * LANES)
        return carry

    lax.fori_loop(0, modes // group, middle, 0, unroll=MIDDLE_UNROLL)

    def after_(mode, carry):
        values = []
        for e in range(GROUPS):
            where_from = mode + inner * e
            twiddle = (turn_ref[0, pl.ds(where_from, 1), :], -turn_ref[1, pl.ds(where_from, 1), :])
            values.append(c_mul((held[where_from, :, :LANES], held[where_from, :, LANES:]), twiddle))
        values = small_dft(values, 1)
        for q in range(GROUPS):
            x[q, mode, 0], x[q, mode, 1] = values[q]
        return carry

    lax.fori_loop(0, inner, after_, 0, unroll=8)

    for q in range(GROUPS):
        c, index = where[q]
        columns = []
        for a in range(slots):
            values = []
            for b in range(chunks):
                mode = a + slots * b
                values.append(c_const((x[q, mode, 0], x[q, mode, 1]), q * mode, modes, 1))
            columns.append(small_dft(values, 1))
        for n in range(chunks):
            values = [c_const(columns[a][n], a * n, inner, 1) for a in range(slots)]
            values = small_dft(values, 1)
            for k in range(slots):
                outputs[c][n * slots + k, index, 0, 0] = values[k][0]
                outputs[c][n * slots + k, index, 1, 0] = values[k][1]


def group_matrix(orient):
    index = np.arange(WIDTH)
    small = np.exp(orient * 2j * np.pi * (np.outer(index, index) % WIDTH) / WIDTH)
    whole = np.kron(np.eye(GROUPS), small)
    return np.stack(split_bf16(np.block([[whole.real, whole.imag], [-whole.imag, whole.real]])))


def row_filter(blocks, plan, turns, green, slots):
    sources = blocks[0].shape[0]
    modes = sources * GROUPS
    forward = jnp.asarray(group_matrix(-1))
    inverse = jnp.asarray(group_matrix(1))
    specs = [
        pl.BlockSpec((sources, len(which), 2, 1, 8, LANES), lambda i: (0, 0, 0, i, 0, 0))
        for which in plan
    ]
    return pl.pallas_call(
        functools.partial(row_filter_kernel, plan, slots),
        grid=(4,),
        out_shape=[jax.ShapeDtypeStruct(block.shape, jnp.float32) for block in blocks],
        in_specs=[
            whole_spec(forward.shape),
            whole_spec(inverse.shape),
            whole_spec(turns.shape),
            pl.BlockSpec((modes, 8, LANES), lambda i: (0, i, 0)),
        ]
        + specs,
        out_specs=specs,
        scratch_shapes=[
            pltpu.VMEM((GROUPS, sources, 2, 8, LANES), jnp.float32),
            pltpu.VMEM((modes, 8, 2 * LANES), jnp.float32),
        ],
        compiler_params=params(),
        cost_estimate=pl.CostEstimate(
            flops=96 * LANES * LANES * modes * 32,
            bytes_accessed=20 * modes * 32 * LANES,
            transcendentals=0,
        ),
        name="row_filter",
    )(forward, inverse, turns, green, *blocks)


def four_plane(density, plane_wave):
    narrow, wide = lax.axis_size("narrow"), lax.axis_size("wide")
    device, place = lax.axis_index("narrow"), lax.axis_index("wide")
    z_local, x_local = density.shape[1:]
    total_z, total_x = z_local * narrow, x_local * wide
    rows = z_local // GROUPS
    modes = narrow * wide * GROUPS
    partners = np.arange(4)

    own = np.arange(4)
    slots = np.stack([0 * own, 2 + 0 * own, 1 + 2 * (own % 2), 3 - 2 * (own % 2)], axis=1)
    sign_low, sign_high = 1.0 - 2.0 * (own % 2), 1.0 - 2.0 * (own // 2)
    phase = np.stack(
        [
            np.ones(4),
            sign_low,
            sign_high * np.where(own % 2 == 0, 1, 1j),
            sign_high * np.where(own % 2 == 0, 1, -1j),
        ],
        axis=1,
    )
    group = np.repeat(np.arange(GROUPS), WIDTH)
    depth = group[None, :] * rows + np.arange(rows)[:, None]
    angle = 2.0 * np.pi * (slots[:, :, None, None] * depth % total_z) / total_z
    head = phase[:, :, None, None] * np.exp(-1j * angle)
    head = pick(np.stack([head.real, head.imag], axis=2).astype(np.float32), device)
    slots = pick(slots.astype(np.int32), device)
    turns = np.moveaxis(turn(group[None, :] * np.arange(rows)[:, None], GROUPS * rows), 2, 0)
    four = np.exp(-2j * np.pi * (np.outer(partners, partners) % 4) / 4)
    mixing = np.round(np.kron(four, np.eye(WIDTH)))
    ahead = np.block([[mixing.real, mixing.imag], [-mixing.imag, mixing.real]])
    backward = np.block([[mixing.real, -mixing.imag], [mixing.imag, mixing.real]])
    tables = (
        jnp.asarray(ahead.astype(jnp.bfloat16)),
        jnp.asarray(dft_matrix(rows, -1, True)),
        jnp.asarray(turns),
    )
    tables_back = (
        jnp.asarray(backward.astype(jnp.bfloat16)),
        jnp.asarray(dft_matrix(rows, 1, True)),
        jnp.asarray(turns),
    )
    cell = np.tile(np.arange(WIDTH), GROUPS)
    x_turns = turn(np.arange(modes)[:, None] * cell[None, :], total_x)
    x_turns = jnp.asarray(np.moveaxis(x_turns, 2, 0))
    residue = np.arange(4)[:, None, None] + 16 * np.arange(8)[:, None] + 4 * group
    wave_z = jnp.asarray(residue.reshape(32, LANES).astype(np.int32))
    wave_z = wave_z + 16 * 8 * (device * wide + place)
    wave_x = np.arange(modes)[:, None, None] + modes * cell
    signed_x = jnp.asarray(np.where(wave_x < total_x // 2, wave_x, wave_x - total_x).astype(np.int32))
    green = green_of(plane_wave, wave_z[None], signed_x, total_z, total_x)

    source = density.reshape(2, GROUPS, rows, x_local)

    def send(pieces):
        moved = {k: swap(pieces[k], "narrow", k) for k in (3, 1, 2)}
        return [pieces[0], moved[1], moved[2], moved[3]]

    def trade_all(blocks):
        return lax.all_to_all(blocks, ("narrow", "wide"), 0, 0, tiled=True)

    arrived, got, made = [], None, []
    for c, which in enumerate(PLAN):
        wanted = after(source, made[c - 2]) if c >= 2 else source
        pieces = [cut_columns(wanted, which, k) for k in range(4)]
        got = send(pieces if got is None else after(pieces, got))
        made.append(lines_forward(got, slots, head, tables))
        arrived.append(trade_all(made[c]))

    filtered = row_filter(arrived, PLAN, x_turns, green, wide)

    back, blocks, made = [None] * len(PLAN), None, []
    for c in reversed(range(len(PLAN))):
        wanted = filtered[c] if blocks is None else after(filtered[c], blocks)
        if len(made) >= 2:
            wanted = after(wanted, made[-2])
        blocks = trade_all(wanted)
        made.append(lines_inverse(blocks, slots, head, tables_back))
        back[c] = send(made[-1] if c + 1 == len(PLAN) else after(made[-1], back[c + 1]))
    if len(PLAN[0]) > 1:
        return place_columns(back, PLAN).reshape(density.shape)
    so_far = place_columns([None] + back[1:], PLAN)
    return add_columns(back[0], PLAN[0][0], so_far).reshape(density.shape)


def plane(density, plane_wave):
    narrow, wide = lax.axis_size("narrow"), lax.axis_size("wide")
    bits = narrow.bit_length() - 1
    device, place = lax.axis_index("narrow"), lax.axis_index("wide")
    z_local, x_local = density.shape[1:]
    total_z, total_x = z_local * narrow, x_local * wide
    rows = z_local // wide
    chunks = x_local // LANES
    modes = wide * chunks
    four = narrow == 4
    low_wave = device if four else reversed_index(device, bits)
    parts = 2 if four else 1
    half = z_local // parts

    waves = [d if four else int(format(d, "b").zfill(bits)[::-1], 2) for d in range(narrow)]
    waves = np.array(waves)
    block = waves[:, None] + narrow * np.arange(wide)
    turns = turn(np.arange(rows) * block[..., None], total_z)
    turns = pick(np.moveaxis(turns, 3, 2), device)
    turns = jnp.broadcast_to(turns[..., None], (wide, 2, rows, LANES))
    head = np.arange(wide) * waves[:, None]
    inner = pick(turn(-head, narrow * wide), device)
    if four:
        give, keep = narrow_terms(1, narrow * wide)
        outer = np.repeat(keep, wide // 2, axis=1) + head[..., None]
        outer = pick(turn(outer, narrow * wide).reshape(narrow, wide, 6), device)
        give = pick(turn(give, narrow * wide).reshape(narrow, 2, 4), device)
        give_back, keep = narrow_terms(-1, narrow * wide)
        give_back = pick(turn(give_back, narrow * wide).reshape(narrow, 2, 4), device)
        last = pick(turn(keep, narrow * wide).reshape(narrow, 2, 6), device)
    else:
        outer = pick(turn(head, narrow * wide), device)
        last = jnp.array([[1.0, 0.0]], jnp.float32)
    x_turns = turn(np.arange(modes)[:, None] * np.arange(LANES)[None, :], total_x)
    x_turns = jnp.asarray(np.moveaxis(x_turns, 2, 0))
    line = jnp.arange(rows, dtype=jnp.int32)
    wave_z = low_wave + narrow * (place + wide * line)
    green = green_values(plane_wave, wave_z, modes, total_z, total_x)

    def part_spec(part, chunk):
        def make(steps):
            first = part * steps
            return pl.BlockSpec((2, half // steps, LANES), lambda i: (0, first + i, chunk))

        return make

    def own_spec(steps):
        return pl.BlockSpec((2, half // steps, LANES), lambda i: (0, i, 0))

    def cut(c, source):
        columns = slice(c * LANES, (c + 1) * LANES)
        return [source[:, p * half : (p + 1) * half, columns] for p in range(parts)]

    def first_swap(pieces):
        return [swap(piece, "narrow", first) for piece, first in zip(pieces, FIRSTS)]

    def second_swap(pieces):
        return [swap(piece, "narrow", 3 - first) for piece, first in zip(pieces, FIRSTS)]

    arrived, pieces = [], [cut(0, density)]
    rest = after(density, pieces[0])
    pieces += [cut(c, rest) for c in range(1, chunks)]
    partner = received = sent = None
    for c in range(chunks):
        if four:
            if c == 0:
                partner = first_swap(pieces[0])
            else:
                partner = first_swap(after(pieces[c], received))
            ready = after(partner, sent) if c else partner
            mixed = mix(
                [[(density, part_spec(p, c)), (ready[p], own_spec)] for p in range(parts)], give, half
            )
            received = second_swap(mixed)
            terms = [
                [
                    (density, part_spec(p, c)(1)),
                    (partner[p], own_spec(1)),
                    (received[p], own_spec(1)),
                ]
                for p in range(parts)
            ]
        else:
            terms = [[(butterfly_forward(piece, device, bits), own_spec(1))] for piece in pieces[c]]
        sent = z_forward(terms, outer, turns, wide, rows)
        arrived.append(trade(sent))

    filtered = x_filter(arrived, x_turns, green)

    result, done = None, []
    for c in range(chunks):
        blocks = after(filtered[c], done[c - 2]) if four and c >= 2 else filtered[c]
        pieces = z_inverse(trade(blocks), inner, turns, parts)
        if four:
            partner = first_swap(pieces)
            ready = after(partner, received) if c else partner
            mixed = mix(
                [[(pieces[p], own_spec), (ready[p], own_spec)] for p in range(parts)], give_back, half
            )
            done.append(mixed)
            received = second_swap(mixed)
            pieces = [[pieces[p], partner[p], received[p]] for p in range(parts)]
        else:
            pieces = [[butterfly_inverse(piece, device, bits)] for piece in pieces]
        result = finish(pieces, last, c, chunks, result)
    return result.reshape(density.shape)


def shards(density, plane_wave):
    sizes = lax.axis_size("narrow"), lax.axis_size("wide")
    one = four_plane if fits(*sizes, *density.shape[2:]) else plane
    planes = [one(density[:, y], plane_wave[y]) for y in range(density.shape[1])]
    return jnp.stack(planes, axis=1)


def solution(mesh):
    in_specs = (P(None, None, "narrow", "wide"), P())
    out_specs = P(None, None, "narrow", "wide")
    return jax.shard_map(shards, mesh=mesh, in_specs=in_specs, out_specs=out_specs, check_vma=False)
```

```python
import functools
import math

import jax
import jax.numpy as jnp
import numpy as np
from jax import lax
from jax.experimental import pallas as pl
from jax.experimental.pallas import tpu as pltpu
from jax.sharding import PartitionSpec as P

SCREEN = 1024
AMP = 2048
LANES = 128
MIX_WEIGHT = 480
LINE_WEIGHT = 3000
BACK_WEIGHT = 3000
ADD_STEP = 128
MIDDLE_UNROLL = 4
PLAN = ((0,), (1,), (2, 3))
VMEM_LIMIT = 48 * 1024 * 1024
FIRSTS = (1, 2)


def split_bf16(value):
    high = np.asarray(value, np.float64).astype(np.float32).astype(jnp.bfloat16)
    low = (value - high.astype(np.float64)).astype(np.float32).astype(jnp.bfloat16)
    return high, low


def dft_matrix(length, orient, left):
    index = np.arange(length)
    angle = 2.0 * np.pi * ((index[:, None] * index[None, :]) % length) / length
    cosine, sine = np.cos(angle), orient * np.sin(angle)
    if left:
        whole = np.block([[cosine, -sine], [sine, cosine]])
    else:
        whole = np.block([[cosine, sine], [-sine, cosine]])
    high, low = split_bf16(whole)
    return np.stack([high, low])


def turn(numerator, length):
    angle = (np.asarray(numerator) % length) * (2.0 * np.pi / length)
    return np.stack([np.cos(angle), -np.sin(angle)], axis=-1).astype(np.float32)


def c_add(a, b):
    return (a[0] + b[0], a[1] + b[1])


def c_sub(a, b):
    return (a[0] - b[0], a[1] - b[1])


def c_mul(a, b):
    return (a[0] * b[0] - a[1] * b[1], a[0] * b[1] + a[1] * b[0])


def c_const(a, numerator, length, orient):
    numerator = (orient * numerator) % length
    if numerator == 0:
        return a
    if 2 * numerator == length:
        return (-a[0], -a[1])
    if 4 * numerator == length:
        return (-a[1], a[0])
    if 4 * numerator == 3 * length:
        return (a[1], -a[0])
    angle = 2.0 * math.pi * numerator / length
    cosine, sine = math.cos(angle), math.sin(angle)
    if 8 * numerator % length == 0:
        root = math.sqrt(0.5)
        total, differ = (a[0] + a[1]) * root, (a[0] - a[1]) * root
        if cosine > 0 and sine > 0:
            return (differ, total)
        if cosine > 0:
            return (total, -differ)
        if sine > 0:
            return (-total, differ)
        return (-differ, -total)
    return (a[0] * cosine - a[1] * sine, a[0] * sine + a[1] * cosine)


def small_dft(values, orient):
    count = len(values)
    if count == 1:
        return values
    half = count // 2
    upper = [c_add(values[i], values[i + half]) for i in range(half)]
    lower = [
        c_const(c_sub(values[i], values[i + half]), i, count, orient) for i in range(half)
    ]
    even, odd = small_dft(upper, orient), small_dft(lower, orient)
    result = []
    for i in range(half):
        result += [even[i], odd[i]]
    return result


def dot3(high, low, value, left):
    value_high = value.astype(jnp.bfloat16)
    value_low = (value - value_high.astype(jnp.float32)).astype(jnp.bfloat16)
    dot = functools.partial(jnp.dot, preferred_element_type=jnp.float32)
    if left:
        return dot(high, value_high) + (dot(high, value_low) + dot(low, value_high))
    return dot(value_high, high) + (dot(value_low, high) + dot(value_high, low))


def whole_spec(shape):
    return pl.BlockSpec(shape, lambda *_: (0,) * len(shape))


def params():
    return pltpu.CompilerParams(vmem_limit_bytes=VMEM_LIMIT)


def combine(inputs, coef_ref, row, place):
    total = None
    for term, ref in enumerate(inputs):
        value = (ref[0, place, :], ref[1, place, :])
        product = c_mul(value, (coef_ref[row, 2 * term], coef_ref[row, 2 * term + 1]))
        total = product if total is None else c_add(total, product)
    return total


def z_forward_kernel(terms, parts, slots, rows, coef_ref, matrix_ref, turn_ref, *refs):
    inputs = refs[: terms * parts]
    out_ref, held = refs[-2:]
    per_part = slots // parts
    tile = min(rows, 8)

    def step(index, carry):
        row = pl.multiple_of(index * tile, tile)
        values = []
        for h in range(slots):
            part, inner = divmod(h, per_part)
            place = pl.ds(inner * rows + row, tile)
            values.append(combine(inputs[part * terms : (part + 1) * terms], coef_ref, h, place))
        values = small_dft(values, -1)
        for k in range(slots):
            twiddle = (
                turn_ref[k, 0, pl.ds(row, tile), :],
                turn_ref[k, 1, pl.ds(row, tile), :],
            )
            real_part, imag_part = c_mul(values[k], twiddle)
            held[pl.ds(row, tile), k * LANES : (k + 1) * LANES] = real_part
            held[pl.ds(rows + row, tile), k * LANES : (k + 1) * LANES] = imag_part
        return carry

    lax.fori_loop(0, rows // tile, step, 0)
    result = dot3(matrix_ref[0], matrix_ref[1], held[...], True)
    for k in range(slots):
        out_ref[k, 0] = result[:rows, k * LANES : (k + 1) * LANES]
        out_ref[k, 1] = result[rows:, k * LANES : (k + 1) * LANES]


def z_forward(parts, coef, turns, slots, rows):
    terms = len(parts[0])
    flat = [pair for part in parts for pair in part]
    matrix = jnp.asarray(dft_matrix(rows, -1, True))
    shape = (slots, 2, rows, LANES)
    return pl.pallas_call(
        functools.partial(z_forward_kernel, terms, len(parts), slots, rows),
        grid=(1,),
        out_shape=jax.ShapeDtypeStruct(shape, jnp.float32),
        in_specs=[
            pl.BlockSpec(memory_space=pltpu.SMEM),
            whole_spec(matrix.shape),
            whole_spec(turns.shape),
        ]
        + [spec for _, spec in flat],
        out_specs=whole_spec(shape),
        scratch_shapes=[pltpu.VMEM((2 * rows, slots * LANES), jnp.float32)],
        compiler_params=params(),
        cost_estimate=pl.CostEstimate(
            flops=700 * rows * rows * slots * LANES,
            bytes_accessed=32 * rows * slots * LANES,
            transcendentals=0,
        ),
        name="z_forward",
    )(coef, matrix, turns, *[array for array, _ in flat])


def z_inverse_kernel(parts, slots, rows, coef_ref, matrix_ref, turn_ref, in_ref, *refs):
    outputs, held = refs[:parts], refs[parts]
    per_part = slots // parts
    tile = min(rows, 8)
    for k in range(slots):
        held[:rows, k * LANES : (k + 1) * LANES] = in_ref[k, 0]
        held[rows:, k * LANES : (k + 1) * LANES] = in_ref[k, 1]
    held[...] = dot3(matrix_ref[0], matrix_ref[1], held[...], True)

    def step(index, carry):
        row = pl.multiple_of(index * tile, tile)
        values = []
        for k in range(slots):
            value = (
                held[pl.ds(row, tile), k * LANES : (k + 1) * LANES],
                held[pl.ds(rows + row, tile), k * LANES : (k + 1) * LANES],
            )
            twiddle = (
                turn_ref[k, 0, pl.ds(row, tile), :],
                -turn_ref[k, 1, pl.ds(row, tile), :],
            )
            values.append(c_mul(value, twiddle))
        values = small_dft(values, 1)
        for h in range(slots):
            part, inner = divmod(h, per_part)
            real_part, imag_part = c_mul(values[h], (coef_ref[h, 0], coef_ref[h, 1]))
            outputs[part][0, pl.ds(inner * rows + row, tile), :] = real_part
            outputs[part][1, pl.ds(inner * rows + row, tile), :] = imag_part
        return carry

    lax.fori_loop(0, rows // tile, step, 0)


def z_inverse(blocks, coef, turns, parts):
    slots, _, rows, _ = blocks.shape
    matrix = jnp.asarray(dft_matrix(rows, 1, True))
    shape = (2, slots // parts * rows, LANES)
    return pl.pallas_call(
        functools.partial(z_inverse_kernel, parts, slots, rows),
        grid=(1,),
        out_shape=[jax.ShapeDtypeStruct(shape, jnp.float32)] * parts,
        in_specs=[
            pl.BlockSpec(memory_space=pltpu.SMEM),
            whole_spec(matrix.shape),
            whole_spec(turns.shape),
            whole_spec(blocks.shape),
        ],
        out_specs=[whole_spec(shape)] * parts,
        scratch_shapes=[pltpu.VMEM((2 * rows, slots * LANES), jnp.float32)],
        compiler_params=params(),
        cost_estimate=pl.CostEstimate(
            flops=700 * rows * rows * slots * LANES,
            bytes_accessed=20 * rows * slots * LANES,
            transcendentals=0,
        ),
        name="z_inverse",
    )(coef, matrix, turns, blocks)


def x_filter_kernel(slots, chunks, rows, forward_ref, inverse_ref, turn_ref, green_ref, *refs):
    inputs = refs[:chunks]
    outputs = refs[chunks : 2 * chunks]
    held = refs[-1]
    tile = 8
    modes = slots * chunks

    def before(index, carry):
        row = pl.multiple_of(index * tile, tile)
        place = pl.ds(row, tile)
        columns = []
        for c in range(chunks):
            values = [
                (inputs[c][k, 0, place, :], inputs[c][k, 1, place, :]) for k in range(slots)
            ]
            values = small_dft(values, -1)
            columns.append([c_const(values[a], a * c, modes, -1) for a in range(slots)])
        for a in range(slots):
            values = small_dft([columns[c][a] for c in range(chunks)], -1)
            for b in range(chunks):
                mode = a + slots * b
                twiddle = (turn_ref[0, mode : mode + 1, :], turn_ref[1, mode : mode + 1, :])
                real_part, imag_part = c_mul(values[b], twiddle)
                held[mode, place, :LANES] = real_part
                held[mode, place, LANES:] = imag_part
        return carry

    lax.fori_loop(0, rows // tile, before, 0)

    group = max(1, min(modes, 256 // rows))

    def middle(index, carry):
        mode = pl.multiple_of(index * group, group)
        value = held[pl.ds(mode, group)].reshape(group * rows, 2 * LANES)
        value = dot3(forward_ref[0], forward_ref[1], value, False)
        green = green_ref[pl.ds(mode, group)].reshape(group * rows, LANES)
        value = value * jnp.concatenate([green, green], axis=1)
        value = dot3(inverse_ref[0], inverse_ref[1], value, False)
        held[pl.ds(mode, group)] = value.reshape(group, rows, 2 * LANES)
        return carry

    lax.fori_loop(0, modes // group, middle, 0)

    def after(index, carry):
        row = pl.multiple_of(index * tile, tile)
        place = pl.ds(row, tile)
        columns = []
        for a in range(slots):
            values = []
            for b in range(chunks):
                mode = a + slots * b
                twiddle = (turn_ref[0, mode : mode + 1, :], -turn_ref[1, mode : mode + 1, :])
                values.append(c_mul((held[mode, place, :LANES], held[mode, place, LANES:]), twiddle))
            columns.append(small_dft(values, 1))
        for c in range(chunks):
            values = [c_const(columns[a][c], a * c, modes, 1) for a in range(slots)]
            values = small_dft(values, 1)
            for k in range(slots):
                outputs[c][k, 0, place, :] = values[k][0]
                outputs[c][k, 1, place, :] = values[k][1]
        return carry

    lax.fori_loop(0, rows // tile, after, 0)


def x_filter(blocks, turns, green):
    chunks = len(blocks)
    slots, _, rows, _ = blocks[0].shape
    step = min(rows, 32)
    modes = slots * chunks
    forward = jnp.asarray(dft_matrix(LANES, -1, False))
    inverse = jnp.asarray(dft_matrix(LANES, 1, False))
    block = pl.BlockSpec((slots, 2, step, LANES), lambda i: (0, 0, i, 0))
    return pl.pallas_call(
        functools.partial(x_filter_kernel, slots, chunks, step),
        grid=(rows // step,),
        out_shape=[jax.ShapeDtypeStruct(blocks[0].shape, jnp.float32)] * chunks,
        in_specs=[
            whole_spec(forward.shape),
            whole_spec(inverse.shape),
            whole_spec(turns.shape),
            pl.BlockSpec((modes, step, LANES), lambda i: (0, i, 0)),
        ]
        + [block] * chunks,
        out_specs=[block] * chunks,
        scratch_shapes=[pltpu.VMEM((modes, step, 2 * LANES), jnp.float32)],
        compiler_params=params(),
        cost_estimate=pl.CostEstimate(
            flops=96 * LANES * LANES * modes * rows,
            bytes_accessed=20 * modes * rows * LANES,
            transcendentals=0,
        ),
        name="x_filter",
    )(forward, inverse, turns, green, *blocks)


def mix_kernel(terms, parts, coef_ref, *refs):
    for part in range(parts):
        out_ref = refs[terms * parts + part]
        inputs = refs[part * terms : (part + 1) * terms]
        total = combine(inputs, coef_ref, part, slice(None))
        out_ref[0], out_ref[1] = total


def mix(parts, coef, rows):
    terms = len(parts[0])
    flat = [pair for part in parts for pair in part]
    steps = 4 if rows % 32 == 0 else 1
    return pl.pallas_call(
        functools.partial(mix_kernel, terms, len(parts)),
        grid=(steps,),
        out_shape=[jax.ShapeDtypeStruct((2, rows, LANES), jnp.float32)] * len(parts),
        in_specs=[pl.BlockSpec(memory_space=pltpu.SMEM)] + [make(steps) for _, make in flat],
        out_specs=[pl.BlockSpec((2, rows // steps, LANES), lambda i: (0, i, 0))] * len(parts),
        compiler_params=params(),
        cost_estimate=pl.CostEstimate(
            flops=20 * rows * LANES * len(parts),
            bytes_accessed=MIX_WEIGHT * rows * LANES * len(parts),
            transcendentals=0,
        ),
        name="mix",
    )(coef, *[array for array, _ in flat])


def finish_kernel(terms, parts, coef_ref, *refs):
    out_ref = refs[-1]
    for part in range(parts):
        inputs = refs[part * terms : (part + 1) * terms]
        total = combine(inputs, coef_ref, part, slice(None))
        out_ref[0, part], out_ref[1, part] = total


def finish(parts, coef, chunk, chunks, so_far):
    terms = len(parts[0])
    flat = [array for part in parts for array in part]
    rows = parts[0][0].shape[1]
    steps = 4 if rows % 32 == 0 else 1
    extra = [] if so_far is None else [so_far]
    return pl.pallas_call(
        functools.partial(finish_kernel, terms, len(parts)),
        grid=(steps,),
        out_shape=jax.ShapeDtypeStruct((2, len(parts), rows, chunks * LANES), jnp.float32),
        in_specs=[pl.BlockSpec(memory_space=pltpu.SMEM)]
        + [pl.BlockSpec((2, rows // steps, LANES), lambda i: (0, i, 0))] * len(flat)
        + [pl.BlockSpec(memory_space=pl.ANY)] * len(extra),
        out_specs=pl.BlockSpec((2, len(parts), rows // steps, LANES), lambda i: (0, 0, i, chunk)),
        input_output_aliases={1 + len(flat): 0} if extra else {},
        compiler_params=params(),
        cost_estimate=pl.CostEstimate(
            flops=20 * rows * LANES * len(parts),
            bytes_accessed=32 * rows * LANES * len(parts),
            transcendentals=0,
        ),
        name="finish",
    )(coef, *flat, *extra)


def after(value, *others):
    return lax.optimization_barrier((value, others))[0]


def swap(value, axis, mask):
    pairs = [(source, source ^ mask) for source in range(lax.axis_size(axis))]
    return lax.ppermute(value, axis, pairs)


def trade(blocks):
    return lax.all_to_all(blocks, "wide", 0, 0, tiled=True)


def narrow_terms(orient, length):
    give, keep = [], []
    for device in range(4):
        for first in FIRSTS:
            there = device ^ (3 - first)
            unit = orient * (length // 4)
            give.append([there * device * unit, there * (device ^ first) * unit])
            keep.append([device * device * unit, device * (device ^ first) * unit, 0])
    shape = (4, len(FIRSTS), -1)
    return np.array(give).reshape(shape), np.array(keep).reshape(shape)


def pick(table, index):
    return lax.dynamic_index_in_dim(jnp.asarray(table), index, 0, keepdims=False)


def reversed_index(device, bit_count):
    result = jnp.int32(0)
    for level in range(bit_count):
        result = result + device // (1 << level) % 2 * (1 << bit_count - 1 - level)
    return result


def rotate(field, phase_angle, orient):
    return jnp.stack(
        c_mul((field[0], field[1]), (jnp.cos(phase_angle), -orient * jnp.sin(phase_angle)))
    )


def butterfly_forward(field, device, bit_count):
    for level in reversed(range(bit_count)):
        half_size = 1 << level
        partner = swap(field, "narrow", half_size)
        upper = device // half_size % 2
        phase_angle = (device % half_size).astype(jnp.float32) * (math.pi / half_size)
        field = jnp.where(upper == 0, field + partner, rotate(partner - field, phase_angle, 1.0))
    return field


def butterfly_inverse(field, device, bit_count):
    for level in range(bit_count):
        half_size = 1 << level
        partner = swap(field, "narrow", half_size)
        upper = device // half_size % 2
        phase_angle = (device % half_size).astype(jnp.float32) * (math.pi / half_size)
        turned = rotate(jnp.where(upper == 0, partner, field), phase_angle, -1.0)
        field = jnp.where(upper == 0, field + turned, partner - turned)
    return field


def green_of(plane_wave, wave_z, signed_x, total_z, total_x):
    signed_z = jnp.where(wave_z < total_z // 2, wave_z, wave_z - total_z)
    square = (signed_z**2 + plane_wave**2 + signed_x**2).astype(jnp.float32)
    green = 1.0 / (1.0 + square / float(SCREEN * SCREEN)) + float(AMP) / (square + 1.0)
    return green * (1.0 / (total_x * total_z))


def green_values(plane_wave, wave_z, modes, total_z, total_x):
    wave_x = jnp.arange(modes)[:, None] + modes * jnp.arange(total_x // modes)[None, :]
    signed_x = jnp.where(wave_x < total_x // 2, wave_x, wave_x - total_x)
    return green_of(plane_wave, wave_z[None, :, None], signed_x[:, None, :], total_z, total_x)


GROUPS = 4
WIDTH = LANES // GROUPS


def fits(narrow, wide, z_local, x_local):
    rows = z_local // GROUPS
    return (
        narrow == GROUPS
        and x_local == GROUPS * LANES
        and z_local % GROUPS == 0
        and rows % (8 * narrow * wide) == 0
        and rows == 8 * narrow * wide
    )


def swap_lanes(tiles):
    lane = lax.broadcasted_iota(jnp.int32, tiles[0].shape, len(tiles[0].shape) - 1)
    axis = len(tiles[0].shape) - 1
    low = lane % (2 * WIDTH) < WIDTH
    left = lane < 2 * WIDTH
    first = [None] * 4
    for a in range(2):
        one, two = tiles[a], tiles[a + 2]
        first[a] = jnp.where(left, one, pltpu.roll(two, 2 * WIDTH, axis))
        first[a + 2] = jnp.where(left, pltpu.roll(one, 2 * WIDTH, axis), two)
    second = [None] * 4
    for b in (0, 2):
        one, two = first[b], first[b + 1]
        second[b] = jnp.where(low, one, pltpu.roll(two, WIDTH, axis))
        second[b + 1] = jnp.where(low, pltpu.roll(one, LANES - WIDTH, axis), two)
    return second


def pick_lanes(tiles, which):
    axis = len(tiles[0].shape) - 1
    group = lax.broadcasted_iota(jnp.int32, tiles[0].shape, axis) // WIDTH
    result = None
    for g, tile in enumerate(tiles):
        distance = (g - which) * WIDTH % LANES
        moved = pltpu.roll(tile, distance, axis) if distance else tile
        result = moved if result is None else jnp.where(group == g, moved, result)
    return result


def cut_kernel(which, in_ref, out_ref):
    for part in range(2):
        tiles = [in_ref[part, g] for g in range(GROUPS)]
        if len(which) == 1:
            out_ref[0, part] = pick_lanes(tiles, which[0])
        else:
            tiles = swap_lanes(tiles)
            for index, q in enumerate(which):
                out_ref[index, part] = tiles[q]


def cut_columns(density, which, partner):
    rows = density.shape[2]
    step = min(rows, 128)
    return pl.pallas_call(
        functools.partial(cut_kernel, which),
        grid=(rows // step,),
        in_specs=[
            pl.BlockSpec(
                (2, GROUPS, step, LANES), lambda i: (0, 0, i, lax.axis_index("narrow") ^ partner)
            )
        ],
        out_specs=pl.BlockSpec((len(which), 2, step, LANES), lambda i: (0, 0, i, 0)),
        out_shape=jax.ShapeDtypeStruct((len(which), 2, rows, LANES), jnp.float32),
        compiler_params=params(),
        cost_estimate=pl.CostEstimate(
            flops=8 * rows * LANES * len(which),
            bytes_accessed=40 * rows * LANES,
            transcendentals=0,
        ),
        name="cut",
    )(density)


def place_kernel(order, *refs):
    inputs, out_ref = refs[:-1], refs[-1]
    device = lax.axis_index("narrow")
    for k in range(GROUPS):
        lanes = pl.ds(pl.multiple_of((device ^ k) * LANES, LANES), LANES)
        for part in range(2):
            tiles = [
                jnp.zeros(out_ref.shape[2:3] + (LANES,), jnp.float32)
                if spot is None
                else inputs[spot[0] * GROUPS + k][spot[1], part]
                for spot in order
            ]
            for g, value in enumerate(swap_lanes(tiles)):
                out_ref[part, g, :, lanes] = value


def add_kernel(which, *refs):
    inputs, so_far_ref, out_ref = refs[:4], refs[4], refs[5]
    device = lax.axis_index("narrow")
    group = lax.broadcasted_iota(jnp.int32, (out_ref.shape[2], LANES), 1) // WIDTH
    for k in range(GROUPS):
        lanes = pl.ds(pl.multiple_of((device ^ k) * LANES, LANES), LANES)
        for part in range(2):
            tile = inputs[k][0, part]
            for g in range(GROUPS):
                distance = (which - g) * WIDTH % LANES
                moved = pltpu.roll(tile, distance, 1) if distance else tile
                value = jnp.where(group == which, moved, so_far_ref[part, g, :, lanes])
                out_ref[part, g, :, lanes] = value


def place_columns(chunks, plan):
    specs, operands, order = [], [], [None] * GROUPS
    for which, chunk in zip(plan, chunks):
        if chunk is None:
            continue
        rows = chunk[0].shape[2]
        step = min(rows, 128)
        for index, q in enumerate(which):
            order[q] = (len(operands) // GROUPS, index)
        specs += [pl.BlockSpec((len(which), 2, step, LANES), lambda i: (0, 0, i, 0))] * GROUPS
        operands += list(chunk)
    shape = (2, GROUPS, rows, GROUPS * LANES)
    return pl.pallas_call(
        functools.partial(place_kernel, order),
        grid=(rows // step,),
        out_shape=jax.ShapeDtypeStruct(shape, jnp.float32),
        in_specs=specs,
        out_specs=pl.BlockSpec((2, GROUPS, step, GROUPS * LANES), lambda i: (0, 0, i, 0)),
        compiler_params=params(),
        cost_estimate=pl.CostEstimate(
            flops=64 * rows * LANES, bytes_accessed=128 * rows * LANES, transcendentals=0
        ),
        name="place",
    )(*operands)


def add_columns(chunk, which, so_far):
    rows = chunk[0].shape[2]
    step = min(rows, ADD_STEP)
    block = pl.BlockSpec((2, GROUPS, step, GROUPS * LANES), lambda i: (0, 0, i, 0))
    return pl.pallas_call(
        functools.partial(add_kernel, which),
        grid=(rows // step,),
        out_shape=jax.ShapeDtypeStruct(so_far.shape, jnp.float32),
        in_specs=[pl.BlockSpec((1, 2, step, LANES), lambda i: (0, 0, i, 0))] * GROUPS + [block],
        out_specs=block,
        input_output_aliases={GROUPS: 0},
        compiler_params=params(),
        cost_estimate=pl.CostEstimate(
            flops=64 * rows * LANES, bytes_accessed=128 * rows * LANES, transcendentals=0
        ),
        name="add",
    )(*chunk, so_far)


def fetch(sources, held, semaphores):
    copies = [
        pltpu.make_async_copy(source, there, semaphores.at[i])
        for i, (source, there) in enumerate(zip(sources, held))
    ]

    @pl.when(pl.program_id(0) == 0)
    def start():
        for copy in copies:
            copy.start()

    def wait(*which):
        @pl.when(pl.program_id(0) == 0)
        def finish_copies():
            for i in which:
                copies[i].wait()

    return wait


def lines_forward_kernel(rows, slot_ref, *refs):
    sources, inputs = refs[:4], refs[4:8]
    out_ref, first, second, head_ref, mix_ref, matrix_ref, turn_ref, semaphores = refs[8:]
    tile = 8
    wait = fetch(sources, (head_ref, mix_ref, matrix_ref, turn_ref), semaphores)
    wait(0)

    def step(index, carry):
        place = pl.ds(pl.multiple_of(index * tile, tile), tile)
        x = [(ref[0, 0, place, :], ref[0, 1, place, :]) for ref in inputs]
        even = [c_add(x[0], x[2]), c_add(x[1], x[3])]
        odd = [c_sub(x[0], x[2]), c_sub(x[1], x[3])]
        turned = (odd[1][1], -odd[1][0])
        values = [
            c_add(even[0], even[1]),
            c_sub(even[0], even[1]),
            c_add(odd[0], turned),
            c_sub(odd[0], turned),
        ]
        for k in range(4):
            twiddle = (head_ref[k, 0, place, :], head_ref[k, 1, place, :])
            real_part, imag_part = c_mul(values[k], twiddle)
            first[slot_ref[k], place, :LANES] = real_part
            first[slot_ref[k], place, LANES:] = imag_part
        return carry

    lax.fori_loop(0, rows // tile, step, 0)
    wait(1, 2, 3)
    dot = functools.partial(jnp.dot, preferred_element_type=jnp.float32)
    for k in range(4):
        value = first[k]
        high = value.astype(jnp.bfloat16)
        low = (value - high.astype(jnp.float32)).astype(jnp.bfloat16)
        value = dot(high, mix_ref[...]) + dot(low, mix_ref[...])
        real_part, imag_part = c_mul(
            (value[:, :LANES], value[:, LANES:]), (turn_ref[0], turn_ref[1])
        )
        second[:rows, k * LANES : (k + 1) * LANES] = real_part
        second[rows:, k * LANES : (k + 1) * LANES] = imag_part
    for side in range(2):
        lanes = slice(2 * side * LANES, 2 * (side + 1) * LANES)
        value = dot3(matrix_ref[0], matrix_ref[1], second[:, lanes], True)
        for k in range(2):
            for part in range(2):
                piece = value[part * rows : (part + 1) * rows, k * LANES : (k + 1) * LANES]
                out_ref[:, 0, part, 2 * side + k] = piece.reshape(rows // tile, tile, LANES)


def line_specs():
    return [pl.BlockSpec(memory_space=pltpu.SMEM)] + [pl.BlockSpec(memory_space=pl.ANY)] * 4


def line_scratch(rows, tables):
    return (
        [
            pltpu.VMEM((4, rows, 2 * LANES), jnp.float32),
            pltpu.VMEM((2 * rows, 4 * LANES), jnp.float32),
        ]
        + [pltpu.VMEM(table.shape, table.dtype) for table in tables]
        + [pltpu.SemaphoreType.DMA((len(tables),))]
    )


def lines_forward(pieces, slots, head, tables):
    count, _, rows, _ = pieces[0].shape
    places = rows // 8
    return pl.pallas_call(
        functools.partial(lines_forward_kernel, rows),
        grid=(count,),
        out_shape=jax.ShapeDtypeStruct((places, count, 2, 4, 8, LANES), jnp.float32),
        in_specs=line_specs()
        + [pl.BlockSpec((1, 2, rows, LANES), lambda i: (i, 0, 0, 0))] * 4,
        out_specs=pl.BlockSpec((places, 1, 2, 4, 8, LANES), lambda i: (0, i, 0, 0, 0, 0)),
        scratch_shapes=line_scratch(rows, (head, *tables)),
        compiler_params=params(),
        cost_estimate=pl.CostEstimate(
            flops=LINE_WEIGHT * rows * rows * LANES * count,
            bytes_accessed=64 * rows * LANES * count,
            transcendentals=0,
        ),
        name="lines_forward",
    )(slots, head, *tables, *pieces)


def lines_inverse_kernel(rows, slot_ref, *refs):
    sources, in_ref, outputs = refs[:4], refs[4], refs[5:9]
    first, second, head_ref, mix_ref, matrix_ref, turn_ref, semaphores = refs[9:]
    tile = 8
    wait = fetch(sources, (head_ref, mix_ref, matrix_ref, turn_ref), semaphores)
    for k in range(4):
        for part in range(2):
            piece = in_ref[:, 0, part, k].reshape(rows, LANES)
            second[part * rows : (part + 1) * rows, k * LANES : (k + 1) * LANES] = piece
    dot = functools.partial(jnp.dot, preferred_element_type=jnp.float32)
    wait(2)
    for side in range(2):
        lanes = slice(2 * side * LANES, 2 * (side + 1) * LANES)
        second[:, lanes] = dot3(matrix_ref[0], matrix_ref[1], second[:, lanes], True)
    wait(0, 1, 3)
    for k in range(4):
        lanes = slice(k * LANES, (k + 1) * LANES)
        real_part, imag_part = c_mul(
            (second[:rows, lanes], second[rows:, lanes]), (turn_ref[0], -turn_ref[1])
        )
        value = jnp.concatenate([real_part, imag_part], axis=1)
        high = value.astype(jnp.bfloat16)
        low = (value - high.astype(jnp.float32)).astype(jnp.bfloat16)
        first[k] = dot(high, mix_ref[...]) + dot(low, mix_ref[...])

    def step(index, carry):
        place = pl.ds(pl.multiple_of(index * tile, tile), tile)
        values = []
        for k in range(4):
            value = (first[slot_ref[k], place, :LANES], first[slot_ref[k], place, LANES:])
            values.append(c_mul(value, (head_ref[k, 0, place, :], -head_ref[k, 1, place, :])))
        even = [c_add(values[0], values[1]), c_sub(values[0], values[1])]
        differ = c_sub(values[2], values[3])
        odd = [c_add(values[2], values[3]), (-differ[1], differ[0])]
        for k in range(2):
            for side, value in enumerate((c_add(even[k], odd[k]), c_sub(even[k], odd[k]))):
                outputs[k + 2 * side][0, 0, place, :] = value[0]
                outputs[k + 2 * side][0, 1, place, :] = value[1]
        return carry

    lax.fori_loop(0, rows // tile, step, 0)


def lines_inverse(blocks, slots, head, tables):
    places, count = blocks.shape[:2]
    rows = places * 8
    return pl.pallas_call(
        functools.partial(lines_inverse_kernel, rows),
        grid=(count,),
        out_shape=[jax.ShapeDtypeStruct((count, 2, rows, LANES), jnp.float32)] * 4,
        in_specs=line_specs()
        + [pl.BlockSpec((places, 1, 2, 4, 8, LANES), lambda i: (0, i, 0, 0, 0, 0))],
        out_specs=[pl.BlockSpec((1, 2, rows, LANES), lambda i: (i, 0, 0, 0))] * 4,
        scratch_shapes=line_scratch(rows, (head, *tables)),
        compiler_params=params(),
        cost_estimate=pl.CostEstimate(
            flops=BACK_WEIGHT * rows * rows * LANES * count,
            bytes_accessed=64 * rows * LANES * count,
            transcendentals=0,
        ),
        name="lines_inverse",
    )(slots, head, *tables, blocks)


def row_filter_kernel(plan, slots, forward_ref, inverse_ref, turn_ref, green_ref, *refs):
    inputs, outputs = refs[: len(plan)], refs[len(plan) : 2 * len(plan)]
    x, held = refs[-2:]
    chunks = 4
    inner = slots * chunks
    modes = inner * GROUPS
    rows = 8
    where = {q: (c, index) for c, which in enumerate(plan) for index, q in enumerate(which)}

    for q in range(GROUPS):
        c, index = where[q]
        columns = []
        for n in range(chunks):
            values = [
                (inputs[c][n * slots + k, index, 0, 0], inputs[c][n * slots + k, index, 1, 0])
                for k in range(slots)
            ]
            values = small_dft(values, -1)
            columns.append([c_const(values[a], a * n, inner, -1) for a in range(slots)])
        for a in range(slots):
            values = small_dft([columns[n][a] for n in range(chunks)], -1)
            for b in range(chunks):
                mode = a + slots * b
                x[q, mode, 0], x[q, mode, 1] = c_const(values[b], q * mode, modes, -1)

    def before(mode, carry):
        values = [(x[q, mode, 0], x[q, mode, 1]) for q in range(GROUPS)]
        values = small_dft(values, -1)
        for e in range(GROUPS):
            where_to = mode + inner * e
            twiddle = (turn_ref[0, pl.ds(where_to, 1), :], turn_ref[1, pl.ds(where_to, 1), :])
            held[where_to, :, :LANES], held[where_to, :, LANES:] = c_mul(values[e], twiddle)
        return carry

    lax.fori_loop(0, inner, before, 0, unroll=8)

    group = 256 // rows

    def middle(index, carry):
        mode = pl.multiple_of(index * group, group)
        value = held[pl.ds(mode, group)].reshape(group * rows, 2 * LANES)
        value = dot3(forward_ref[0], forward_ref[1], value, False)
        green = green_ref[pl.ds(mode, group)].reshape(group * rows, LANES)
        value = value * jnp.concatenate([green, green], axis=1)
        value = dot3(inverse_ref[0], inverse_ref[1], value, False)
        held[pl.ds(mode, group)] = value.reshape(group, rows, 2 * LANES)
        return carry

    lax.fori_loop(0, modes // group, middle, 0, unroll=MIDDLE_UNROLL)

    def after_(mode, carry):
        values = []
        for e in range(GROUPS):
            where_from = mode + inner * e
            twiddle = (turn_ref[0, pl.ds(where_from, 1), :], -turn_ref[1, pl.ds(where_from, 1), :])
            values.append(c_mul((held[where_from, :, :LANES], held[where_from, :, LANES:]), twiddle))
        values = small_dft(values, 1)
        for q in range(GROUPS):
            x[q, mode, 0], x[q, mode, 1] = values[q]
        return carry

    lax.fori_loop(0, inner, after_, 0, unroll=8)

    for q in range(GROUPS):
        c, index = where[q]
        columns = []
        for a in range(slots):
            values = []
            for b in range(chunks):
                mode = a + slots * b
                values.append(c_const((x[q, mode, 0], x[q, mode, 1]), q * mode, modes, 1))
            columns.append(small_dft(values, 1))
        for n in range(chunks):
            values = [c_const(columns[a][n], a * n, inner, 1) for a in range(slots)]
            values = small_dft(values, 1)
            for k in range(slots):
                outputs[c][n * slots + k, index, 0, 0] = values[k][0]
                outputs[c][n * slots + k, index, 1, 0] = values[k][1]


def group_matrix(orient):
    index = np.arange(WIDTH)
    small = np.exp(orient * 2j * np.pi * (np.outer(index, index) % WIDTH) / WIDTH)
    whole = np.kron(np.eye(GROUPS), small)
    return np.stack(split_bf16(np.block([[whole.real, whole.imag], [-whole.imag, whole.real]])))


def row_filter(blocks, plan, turns, green, slots):
    sources = blocks[0].shape[0]
    modes = sources * GROUPS
    forward = jnp.asarray(group_matrix(-1))
    inverse = jnp.asarray(group_matrix(1))
    specs = [
        pl.BlockSpec((sources, len(which), 2, 1, 8, LANES), lambda i: (0, 0, 0, i, 0, 0))
        for which in plan
    ]
    return pl.pallas_call(
        functools.partial(row_filter_kernel, plan, slots),
        grid=(4,),
        out_shape=[jax.ShapeDtypeStruct(block.shape, jnp.float32) for block in blocks],
        in_specs=[
            whole_spec(forward.shape),
            whole_spec(inverse.shape),
            whole_spec(turns.shape),
            pl.BlockSpec((modes, 8, LANES), lambda i: (0, i, 0)),
        ]
        + specs,
        out_specs=specs,
        scratch_shapes=[
            pltpu.VMEM((GROUPS, sources, 2, 8, LANES), jnp.float32),
            pltpu.VMEM((modes, 8, 2 * LANES), jnp.float32),
        ],
        compiler_params=params(),
        cost_estimate=pl.CostEstimate(
            flops=96 * LANES * LANES * modes * 32,
            bytes_accessed=20 * modes * 32 * LANES,
            transcendentals=0,
        ),
        name="row_filter",
    )(forward, inverse, turns, green, *blocks)


def four_plane(density, plane_wave):
    narrow, wide = lax.axis_size("narrow"), lax.axis_size("wide")
    device, place = lax.axis_index("narrow"), lax.axis_index("wide")
    z_local, x_local = density.shape[1:]
    total_z, total_x = z_local * narrow, x_local * wide
    rows = z_local // GROUPS
    modes = narrow * wide * GROUPS
    partners = np.arange(4)

    own = np.arange(4)
    slots = np.stack([0 * own, 2 + 0 * own, 1 + 2 * (own % 2), 3 - 2 * (own % 2)], axis=1)
    sign_low, sign_high = 1.0 - 2.0 * (own % 2), 1.0 - 2.0 * (own // 2)
    phase = np.stack(
        [
            np.ones(4),
            sign_low,
            sign_high * np.where(own % 2 == 0, 1, 1j),
            sign_high * np.where(own % 2 == 0, 1, -1j),
        ],
        axis=1,
    )
    group = np.repeat(np.arange(GROUPS), WIDTH)
    depth = group[None, :] * rows + np.arange(rows)[:, None]
    angle = 2.0 * np.pi * (slots[:, :, None, None] * depth % total_z) / total_z
    head = phase[:, :, None, None] * np.exp(-1j * angle)
    head = pick(np.stack([head.real, head.imag], axis=2).astype(np.float32), device)
    slots = pick(slots.astype(np.int32), device)
    turns = np.moveaxis(turn(group[None, :] * np.arange(rows)[:, None], GROUPS * rows), 2, 0)
    four = np.exp(-2j * np.pi * (np.outer(partners, partners) % 4) / 4)
    mixing = np.round(np.kron(four, np.eye(WIDTH)))
    ahead = np.block([[mixing.real, mixing.imag], [-mixing.imag, mixing.real]])
    backward = np.block([[mixing.real, -mixing.imag], [mixing.imag, mixing.real]])
    way = lax.optimization_barrier(jnp.arange(2, dtype=jnp.int32))
    tables = [
        pick(np.stack([one, two]), way[0])
        for one, two in (
            (ahead.astype(jnp.bfloat16), backward.astype(jnp.bfloat16)),
            (dft_matrix(rows, -1, True), dft_matrix(rows, 1, True)),
            (turns, turns),
        )
    ]
    tables_back = (
        jnp.asarray(backward.astype(jnp.bfloat16)),
        jnp.asarray(dft_matrix(rows, 1, True)),
        jnp.asarray(turns),
    )
    cell = np.tile(np.arange(WIDTH), GROUPS)
    x_turns = turn(np.arange(modes)[:, None] * cell[None, :], total_x)
    x_turns = jnp.asarray(np.moveaxis(x_turns, 2, 0))
    residue = np.arange(4)[:, None, None] + 16 * np.arange(8)[:, None] + 4 * group
    wave_z = jnp.asarray(residue.reshape(32, LANES).astype(np.int32))
    wave_z = wave_z + 16 * 8 * (device * wide + place)
    wave_x = np.arange(modes)[:, None, None] + modes * cell
    signed_x = jnp.asarray(np.where(wave_x < total_x // 2, wave_x, wave_x - total_x).astype(np.int32))
    green = green_of(plane_wave, wave_z[None], signed_x, total_z, total_x)

    source = density.reshape(2, GROUPS, rows, x_local)

    def send(pieces):
        moved = {k: swap(pieces[k], "narrow", k) for k in (3, 1, 2)}
        return [pieces[0], moved[1], moved[2], moved[3]]

    def trade_all(blocks):
        return lax.all_to_all(blocks, ("narrow", "wide"), 0, 0, tiled=True)

    arrived, got, made = [], None, []
    for c, which in enumerate(PLAN):
        wanted = after(source, made[c - 2]) if c >= 2 else source
        pieces = [cut_columns(wanted, which, k) for k in range(4)]
        got = send(pieces if got is None else after(pieces, got))
        made.append(lines_forward(got, slots, head, tables))
        arrived.append(trade_all(made[c]))

    filtered = row_filter(arrived, PLAN, x_turns, green, wide)

    back, blocks, made = [None] * len(PLAN), None, []
    for c in reversed(range(len(PLAN))):
        wanted = filtered[c] if blocks is None else after(filtered[c], blocks)
        if len(made) >= 2:
            wanted = after(wanted, made[-2])
        blocks = trade_all(wanted)
        made.append(lines_inverse(blocks, slots, head, tables_back))
        back[c] = send(made[-1] if c + 1 == len(PLAN) else after(made[-1], back[c + 1]))
    if len(PLAN[0]) > 1:
        return place_columns(back, PLAN).reshape(density.shape)
    so_far = place_columns([None] + back[1:], PLAN)
    return add_columns(back[0], PLAN[0][0], so_far).reshape(density.shape)


def plane(density, plane_wave):
    narrow, wide = lax.axis_size("narrow"), lax.axis_size("wide")
    bits = narrow.bit_length() - 1
    device, place = lax.axis_index("narrow"), lax.axis_index("wide")
    z_local, x_local = density.shape[1:]
    total_z, total_x = z_local * narrow, x_local * wide
    rows = z_local // wide
    chunks = x_local // LANES
    modes = wide * chunks
    four = narrow == 4
    low_wave = device if four else reversed_index(device, bits)
    parts = 2 if four else 1
    half = z_local // parts

    waves = [d if four else int(format(d, "b").zfill(bits)[::-1], 2) for d in range(narrow)]
    waves = np.array(waves)
    block = waves[:, None] + narrow * np.arange(wide)
    turns = turn(np.arange(rows) * block[..., None], total_z)
    turns = pick(np.moveaxis(turns, 3, 2), device)
    turns = jnp.broadcast_to(turns[..., None], (wide, 2, rows, LANES))
    head = np.arange(wide) * waves[:, None]
    inner = pick(turn(-head, narrow * wide), device)
    if four:
        give, keep = narrow_terms(1, narrow * wide)
        outer = np.repeat(keep, wide // 2, axis=1) + head[..., None]
        outer = pick(turn(outer, narrow * wide).reshape(narrow, wide, 6), device)
        give = pick(turn(give, narrow * wide).reshape(narrow, 2, 4), device)
        give_back, keep = narrow_terms(-1, narrow * wide)
        give_back = pick(turn(give_back, narrow * wide).reshape(narrow, 2, 4), device)
        last = pick(turn(keep, narrow * wide).reshape(narrow, 2, 6), device)
    else:
        outer = pick(turn(head, narrow * wide), device)
        last = jnp.array([[1.0, 0.0]], jnp.float32)
    x_turns = turn(np.arange(modes)[:, None] * np.arange(LANES)[None, :], total_x)
    x_turns = jnp.asarray(np.moveaxis(x_turns, 2, 0))
    line = jnp.arange(rows, dtype=jnp.int32)
    wave_z = low_wave + narrow * (place + wide * line)
    green = green_values(plane_wave, wave_z, modes, total_z, total_x)

    def part_spec(part, chunk):
        def make(steps):
            first = part * steps
            return pl.BlockSpec((2, half // steps, LANES), lambda i: (0, first + i, chunk))

        return make

    def own_spec(steps):
        return pl.BlockSpec((2, half // steps, LANES), lambda i: (0, i, 0))

    def cut(c, source):
        columns = slice(c * LANES, (c + 1) * LANES)
        return [source[:, p * half : (p + 1) * half, columns] for p in range(parts)]

    def first_swap(pieces):
        return [swap(piece, "narrow", first) for piece, first in zip(pieces, FIRSTS)]

    def second_swap(pieces):
        return [swap(piece, "narrow", 3 - first) for piece, first in zip(pieces, FIRSTS)]

    arrived, pieces = [], [cut(0, density)]
    rest = after(density, pieces[0])
    pieces += [cut(c, rest) for c in range(1, chunks)]
    partner = received = sent = None
    for c in range(chunks):
        if four:
            if c == 0:
                partner = first_swap(pieces[0])
            else:
                partner = first_swap(after(pieces[c], received))
            ready = after(partner, sent) if c else partner
            mixed = mix(
                [[(density, part_spec(p, c)), (ready[p], own_spec)] for p in range(parts)], give, half
            )
            received = second_swap(mixed)
            terms = [
                [
                    (density, part_spec(p, c)(1)),
                    (partner[p], own_spec(1)),
                    (received[p], own_spec(1)),
                ]
                for p in range(parts)
            ]
        else:
            terms = [[(butterfly_forward(piece, device, bits), own_spec(1))] for piece in pieces[c]]
        sent = z_forward(terms, outer, turns, wide, rows)
        arrived.append(trade(sent))

    filtered = x_filter(arrived, x_turns, green)

    result, done = None, []
    for c in range(chunks):
        blocks = after(filtered[c], done[c - 2]) if four and c >= 2 else filtered[c]
        pieces = z_inverse(trade(blocks), inner, turns, parts)
        if four:
            partner = first_swap(pieces)
            ready = after(partner, received) if c else partner
            mixed = mix(
                [[(pieces[p], own_spec), (ready[p], own_spec)] for p in range(parts)], give_back, half
            )
            done.append(mixed)
            received = second_swap(mixed)
            pieces = [[pieces[p], partner[p], received[p]] for p in range(parts)]
        else:
            pieces = [[butterfly_inverse(piece, device, bits)] for piece in pieces]
        result = finish(pieces, last, c, chunks, result)
    return result.reshape(density.shape)


def shards(density, plane_wave):
    sizes = lax.axis_size("narrow"), lax.axis_size("wide")
    one = four_plane if fits(*sizes, *density.shape[2:]) else plane
    planes = [one(density[:, y], plane_wave[y]) for y in range(density.shape[1])]
    return jnp.stack(planes, axis=1)


def solution(mesh):
    in_specs = (P(None, None, "narrow", "wide"), P())
    out_specs = P(None, None, "narrow", "wide")
    return jax.shard_map(shards, mesh=mesh, in_specs=in_specs, out_specs=out_specs, check_vma=False)
```

```python
import functools
import math

import jax
import jax.numpy as jnp
import numpy as np
from jax import lax
from jax.experimental import pallas as pl
from jax.experimental.pallas import tpu as pltpu
from jax.sharding import PartitionSpec as P

SCREEN = 1024
AMP = 2048
LANES = 128
MIX_WEIGHT = 480
LINE_WEIGHT = 3000
BACK_WEIGHT = 3000
ADD_STEP = 128
MIDDLE_UNROLL = 4
PLAN = ((0,), (1,), (2, 3))
VMEM_LIMIT = 48 * 1024 * 1024
FIRSTS = (1, 2)


def split_bf16(value):
    high = np.asarray(value, np.float64).astype(np.float32).astype(jnp.bfloat16)
    low = (value - high.astype(np.float64)).astype(np.float32).astype(jnp.bfloat16)
    return high, low


def dft_matrix(length, orient, left):
    index = np.arange(length)
    angle = 2.0 * np.pi * ((index[:, None] * index[None, :]) % length) / length
    cosine, sine = np.cos(angle), orient * np.sin(angle)
    if left:
        whole = np.block([[cosine, -sine], [sine, cosine]])
    else:
        whole = np.block([[cosine, sine], [-sine, cosine]])
    high, low = split_bf16(whole)
    return np.stack([high, low])


def turn(numerator, length):
    angle = (np.asarray(numerator) % length) * (2.0 * np.pi / length)
    return np.stack([np.cos(angle), -np.sin(angle)], axis=-1).astype(np.float32)


def c_add(a, b):
    return (a[0] + b[0], a[1] + b[1])


def c_sub(a, b):
    return (a[0] - b[0], a[1] - b[1])


def c_mul(a, b):
    return (a[0] * b[0] - a[1] * b[1], a[0] * b[1] + a[1] * b[0])


def c_const(a, numerator, length, orient):
    numerator = (orient * numerator) % length
    if numerator == 0:
        return a
    if 2 * numerator == length:
        return (-a[0], -a[1])
    if 4 * numerator == length:
        return (-a[1], a[0])
    if 4 * numerator == 3 * length:
        return (a[1], -a[0])
    angle = 2.0 * math.pi * numerator / length
    cosine, sine = math.cos(angle), math.sin(angle)
    if 8 * numerator % length == 0:
        root = math.sqrt(0.5)
        total, differ = (a[0] + a[1]) * root, (a[0] - a[1]) * root
        if cosine > 0 and sine > 0:
            return (differ, total)
        if cosine > 0:
            return (total, -differ)
        if sine > 0:
            return (-total, differ)
        return (-differ, -total)
    return (a[0] * cosine - a[1] * sine, a[0] * sine + a[1] * cosine)


def small_dft(values, orient):
    count = len(values)
    if count == 1:
        return values
    half = count // 2
    upper = [c_add(values[i], values[i + half]) for i in range(half)]
    lower = [
        c_const(c_sub(values[i], values[i + half]), i, count, orient) for i in range(half)
    ]
    even, odd = small_dft(upper, orient), small_dft(lower, orient)
    result = []
    for i in range(half):
        result += [even[i], odd[i]]
    return result


def dot3(high, low, value, left):
    value_high = value.astype(jnp.bfloat16)
    value_low = (value - value_high.astype(jnp.float32)).astype(jnp.bfloat16)
    dot = functools.partial(jnp.dot, preferred_element_type=jnp.float32)
    if left:
        return dot(high, value_high) + (dot(high, value_low) + dot(low, value_high))
    return dot(value_high, high) + (dot(value_low, high) + dot(value_high, low))


def whole_spec(shape):
    return pl.BlockSpec(shape, lambda *_: (0,) * len(shape))


def params():
    return pltpu.CompilerParams(vmem_limit_bytes=VMEM_LIMIT)


def combine(inputs, coef_ref, row, place):
    total = None
    for term, ref in enumerate(inputs):
        value = (ref[0, place, :], ref[1, place, :])
        product = c_mul(value, (coef_ref[row, 2 * term], coef_ref[row, 2 * term + 1]))
        total = product if total is None else c_add(total, product)
    return total


def z_forward_kernel(terms, parts, slots, rows, coef_ref, matrix_ref, turn_ref, *refs):
    inputs = refs[: terms * parts]
    out_ref, held = refs[-2:]
    per_part = slots // parts
    tile = min(rows, 8)

    def step(index, carry):
        row = pl.multiple_of(index * tile, tile)
        values = []
        for h in range(slots):
            part, inner = divmod(h, per_part)
            place = pl.ds(inner * rows + row, tile)
            values.append(combine(inputs[part * terms : (part + 1) * terms], coef_ref, h, place))
        values = small_dft(values, -1)
        for k in range(slots):
            twiddle = (
                turn_ref[k, 0, pl.ds(row, tile), :],
                turn_ref[k, 1, pl.ds(row, tile), :],
            )
            real_part, imag_part = c_mul(values[k], twiddle)
            held[pl.ds(row, tile), k * LANES : (k + 1) * LANES] = real_part
            held[pl.ds(rows + row, tile), k * LANES : (k + 1) * LANES] = imag_part
        return carry

    lax.fori_loop(0, rows // tile, step, 0)
    result = dot3(matrix_ref[0], matrix_ref[1], held[...], True)
    for k in range(slots):
        out_ref[k, 0] = result[:rows, k * LANES : (k + 1) * LANES]
        out_ref[k, 1] = result[rows:, k * LANES : (k + 1) * LANES]


def z_forward(parts, coef, turns, slots, rows):
    terms = len(parts[0])
    flat = [pair for part in parts for pair in part]
    matrix = jnp.asarray(dft_matrix(rows, -1, True))
    shape = (slots, 2, rows, LANES)
    return pl.pallas_call(
        functools.partial(z_forward_kernel, terms, len(parts), slots, rows),
        grid=(1,),
        out_shape=jax.ShapeDtypeStruct(shape, jnp.float32),
        in_specs=[
            pl.BlockSpec(memory_space=pltpu.SMEM),
            whole_spec(matrix.shape),
            whole_spec(turns.shape),
        ]
        + [spec for _, spec in flat],
        out_specs=whole_spec(shape),
        scratch_shapes=[pltpu.VMEM((2 * rows, slots * LANES), jnp.float32)],
        compiler_params=params(),
        cost_estimate=pl.CostEstimate(
            flops=700 * rows * rows * slots * LANES,
            bytes_accessed=32 * rows * slots * LANES,
            transcendentals=0,
        ),
        name="z_forward",
    )(coef, matrix, turns, *[array for array, _ in flat])


def z_inverse_kernel(parts, slots, rows, coef_ref, matrix_ref, turn_ref, in_ref, *refs):
    outputs, held = refs[:parts], refs[parts]
    per_part = slots // parts
    tile = min(rows, 8)
    for k in range(slots):
        held[:rows, k * LANES : (k + 1) * LANES] = in_ref[k, 0]
        held[rows:, k * LANES : (k + 1) * LANES] = in_ref[k, 1]
    held[...] = dot3(matrix_ref[0], matrix_ref[1], held[...], True)

    def step(index, carry):
        row = pl.multiple_of(index * tile, tile)
        values = []
        for k in range(slots):
            value = (
                held[pl.ds(row, tile), k * LANES : (k + 1) * LANES],
                held[pl.ds(rows + row, tile), k * LANES : (k + 1) * LANES],
            )
            twiddle = (
                turn_ref[k, 0, pl.ds(row, tile), :],
                -turn_ref[k, 1, pl.ds(row, tile), :],
            )
            values.append(c_mul(value, twiddle))
        values = small_dft(values, 1)
        for h in range(slots):
            part, inner = divmod(h, per_part)
            real_part, imag_part = c_mul(values[h], (coef_ref[h, 0], coef_ref[h, 1]))
            outputs[part][0, pl.ds(inner * rows + row, tile), :] = real_part
            outputs[part][1, pl.ds(inner * rows + row, tile), :] = imag_part
        return carry

    lax.fori_loop(0, rows // tile, step, 0)


def z_inverse(blocks, coef, turns, parts):
    slots, _, rows, _ = blocks.shape
    matrix = jnp.asarray(dft_matrix(rows, 1, True))
    shape = (2, slots // parts * rows, LANES)
    return pl.pallas_call(
        functools.partial(z_inverse_kernel, parts, slots, rows),
        grid=(1,),
        out_shape=[jax.ShapeDtypeStruct(shape, jnp.float32)] * parts,
        in_specs=[
            pl.BlockSpec(memory_space=pltpu.SMEM),
            whole_spec(matrix.shape),
            whole_spec(turns.shape),
            whole_spec(blocks.shape),
        ],
        out_specs=[whole_spec(shape)] * parts,
        scratch_shapes=[pltpu.VMEM((2 * rows, slots * LANES), jnp.float32)],
        compiler_params=params(),
        cost_estimate=pl.CostEstimate(
            flops=700 * rows * rows * slots * LANES,
            bytes_accessed=20 * rows * slots * LANES,
            transcendentals=0,
        ),
        name="z_inverse",
    )(coef, matrix, turns, blocks)


def x_filter_kernel(slots, chunks, rows, forward_ref, inverse_ref, turn_ref, green_ref, *refs):
    inputs = refs[:chunks]
    outputs = refs[chunks : 2 * chunks]
    held = refs[-1]
    tile = 8
    modes = slots * chunks

    def before(index, carry):
        row = pl.multiple_of(index * tile, tile)
        place = pl.ds(row, tile)
        columns = []
        for c in range(chunks):
            values = [
                (inputs[c][k, 0, place, :], inputs[c][k, 1, place, :]) for k in range(slots)
            ]
            values = small_dft(values, -1)
            columns.append([c_const(values[a], a * c, modes, -1) for a in range(slots)])
        for a in range(slots):
            values = small_dft([columns[c][a] for c in range(chunks)], -1)
            for b in range(chunks):
                mode = a + slots * b
                twiddle = (turn_ref[0, mode : mode + 1, :], turn_ref[1, mode : mode + 1, :])
                real_part, imag_part = c_mul(values[b], twiddle)
                held[mode, place, :LANES] = real_part
                held[mode, place, LANES:] = imag_part
        return carry

    lax.fori_loop(0, rows // tile, before, 0)

    group = max(1, min(modes, 256 // rows))

    def middle(index, carry):
        mode = pl.multiple_of(index * group, group)
        value = held[pl.ds(mode, group)].reshape(group * rows, 2 * LANES)
        value = dot3(forward_ref[0], forward_ref[1], value, False)
        green = green_ref[pl.ds(mode, group)].reshape(group * rows, LANES)
        value = value * jnp.concatenate([green, green], axis=1)
        value = dot3(inverse_ref[0], inverse_ref[1], value, False)
        held[pl.ds(mode, group)] = value.reshape(group, rows, 2 * LANES)
        return carry

    lax.fori_loop(0, modes // group, middle, 0)

    def after(index, carry):
        row = pl.multiple_of(index * tile, tile)
        place = pl.ds(row, tile)
        columns = []
        for a in range(slots):
            values = []
            for b in range(chunks):
                mode = a + slots * b
                twiddle = (turn_ref[0, mode : mode + 1, :], -turn_ref[1, mode : mode + 1, :])
                values.append(c_mul((held[mode, place, :LANES], held[mode, place, LANES:]), twiddle))
            columns.append(small_dft(values, 1))
        for c in range(chunks):
            values = [c_const(columns[a][c], a * c, modes, 1) for a in range(slots)]
            values = small_dft(values, 1)
            for k in range(slots):
                outputs[c][k, 0, place, :] = values[k][0]
                outputs[c][k, 1, place, :] = values[k][1]
        return carry

    lax.fori_loop(0, rows // tile, after, 0)


def x_filter(blocks, turns, green):
    chunks = len(blocks)
    slots, _, rows, _ = blocks[0].shape
    step = min(rows, 32)
    modes = slots * chunks
    forward = jnp.asarray(dft_matrix(LANES, -1, False))
    inverse = jnp.asarray(dft_matrix(LANES, 1, False))
    block = pl.BlockSpec((slots, 2, step, LANES), lambda i: (0, 0, i, 0))
    return pl.pallas_call(
        functools.partial(x_filter_kernel, slots, chunks, step),
        grid=(rows // step,),
        out_shape=[jax.ShapeDtypeStruct(blocks[0].shape, jnp.float32)] * chunks,
        in_specs=[
            whole_spec(forward.shape),
            whole_spec(inverse.shape),
            whole_spec(turns.shape),
            pl.BlockSpec((modes, step, LANES), lambda i: (0, i, 0)),
        ]
        + [block] * chunks,
        out_specs=[block] * chunks,
        scratch_shapes=[pltpu.VMEM((modes, step, 2 * LANES), jnp.float32)],
        compiler_params=params(),
        cost_estimate=pl.CostEstimate(
            flops=96 * LANES * LANES * modes * rows,
            bytes_accessed=20 * modes * rows * LANES,
            transcendentals=0,
        ),
        name="x_filter",
    )(forward, inverse, turns, green, *blocks)


def mix_kernel(terms, parts, coef_ref, *refs):
    for part in range(parts):
        out_ref = refs[terms * parts + part]
        inputs = refs[part * terms : (part + 1) * terms]
        total = combine(inputs, coef_ref, part, slice(None))
        out_ref[0], out_ref[1] = total


def mix(parts, coef, rows):
    terms = len(parts[0])
    flat = [pair for part in parts for pair in part]
    steps = 4 if rows % 32 == 0 else 1
    return pl.pallas_call(
        functools.partial(mix_kernel, terms, len(parts)),
        grid=(steps,),
        out_shape=[jax.ShapeDtypeStruct((2, rows, LANES), jnp.float32)] * len(parts),
        in_specs=[pl.BlockSpec(memory_space=pltpu.SMEM)] + [make(steps) for _, make in flat],
        out_specs=[pl.BlockSpec((2, rows // steps, LANES), lambda i: (0, i, 0))] * len(parts),
        compiler_params=params(),
        cost_estimate=pl.CostEstimate(
            flops=20 * rows * LANES * len(parts),
            bytes_accessed=MIX_WEIGHT * rows * LANES * len(parts),
            transcendentals=0,
        ),
        name="mix",
    )(coef, *[array for array, _ in flat])


def finish_kernel(terms, parts, coef_ref, *refs):
    out_ref = refs[-1]
    for part in range(parts):
        inputs = refs[part * terms : (part + 1) * terms]
        total = combine(inputs, coef_ref, part, slice(None))
        out_ref[0, part], out_ref[1, part] = total


def finish(parts, coef, chunk, chunks, so_far):
    terms = len(parts[0])
    flat = [array for part in parts for array in part]
    rows = parts[0][0].shape[1]
    steps = 4 if rows % 32 == 0 else 1
    extra = [] if so_far is None else [so_far]
    return pl.pallas_call(
        functools.partial(finish_kernel, terms, len(parts)),
        grid=(steps,),
        out_shape=jax.ShapeDtypeStruct((2, len(parts), rows, chunks * LANES), jnp.float32),
        in_specs=[pl.BlockSpec(memory_space=pltpu.SMEM)]
        + [pl.BlockSpec((2, rows // steps, LANES), lambda i: (0, i, 0))] * len(flat)
        + [pl.BlockSpec(memory_space=pl.ANY)] * len(extra),
        out_specs=pl.BlockSpec((2, len(parts), rows // steps, LANES), lambda i: (0, 0, i, chunk)),
        input_output_aliases={1 + len(flat): 0} if extra else {},
        compiler_params=params(),
        cost_estimate=pl.CostEstimate(
            flops=20 * rows * LANES * len(parts),
            bytes_accessed=32 * rows * LANES * len(parts),
            transcendentals=0,
        ),
        name="finish",
    )(coef, *flat, *extra)


def after(value, *others):
    return lax.optimization_barrier((value, others))[0]


def swap(value, axis, mask):
    pairs = [(source, source ^ mask) for source in range(lax.axis_size(axis))]
    return lax.ppermute(value, axis, pairs)


def trade(blocks):
    return lax.all_to_all(blocks, "wide", 0, 0, tiled=True)


def narrow_terms(orient, length):
    give, keep = [], []
    for device in range(4):
        for first in FIRSTS:
            there = device ^ (3 - first)
            unit = orient * (length // 4)
            give.append([there * device * unit, there * (device ^ first) * unit])
            keep.append([device * device * unit, device * (device ^ first) * unit, 0])
    shape = (4, len(FIRSTS), -1)
    return np.array(give).reshape(shape), np.array(keep).reshape(shape)


def pick(table, index):
    return lax.dynamic_index_in_dim(jnp.asarray(table), index, 0, keepdims=False)


def reversed_index(device, bit_count):
    result = jnp.int32(0)
    for level in range(bit_count):
        result = result + device // (1 << level) % 2 * (1 << bit_count - 1 - level)
    return result


def rotate(field, phase_angle, orient):
    return jnp.stack(
        c_mul((field[0], field[1]), (jnp.cos(phase_angle), -orient * jnp.sin(phase_angle)))
    )


def butterfly_forward(field, device, bit_count):
    for level in reversed(range(bit_count)):
        half_size = 1 << level
        partner = swap(field, "narrow", half_size)
        upper = device // half_size % 2
        phase_angle = (device % half_size).astype(jnp.float32) * (math.pi / half_size)
        field = jnp.where(upper == 0, field + partner, rotate(partner - field, phase_angle, 1.0))
    return field


def butterfly_inverse(field, device, bit_count):
    for level in range(bit_count):
        half_size = 1 << level
        partner = swap(field, "narrow", half_size)
        upper = device // half_size % 2
        phase_angle = (device % half_size).astype(jnp.float32) * (math.pi / half_size)
        turned = rotate(jnp.where(upper == 0, partner, field), phase_angle, -1.0)
        field = jnp.where(upper == 0, field + turned, partner - turned)
    return field


def green_of(plane_wave, wave_z, signed_x, total_z, total_x):
    signed_z = jnp.where(wave_z < total_z // 2, wave_z, wave_z - total_z)
    square = (signed_z**2 + plane_wave**2 + signed_x**2).astype(jnp.float32)
    green = 1.0 / (1.0 + square / float(SCREEN * SCREEN)) + float(AMP) / (square + 1.0)
    return green * (1.0 / (total_x * total_z))


def green_values(plane_wave, wave_z, modes, total_z, total_x):
    wave_x = jnp.arange(modes)[:, None] + modes * jnp.arange(total_x // modes)[None, :]
    signed_x = jnp.where(wave_x < total_x // 2, wave_x, wave_x - total_x)
    return green_of(plane_wave, wave_z[None, :, None], signed_x[:, None, :], total_z, total_x)


GROUPS = 4
WIDTH = LANES // GROUPS


def fits(narrow, wide, z_local, x_local):
    rows = z_local // GROUPS
    return (
        narrow == GROUPS
        and x_local == GROUPS * LANES
        and z_local % GROUPS == 0
        and rows % (8 * narrow * wide) == 0
        and rows == 8 * narrow * wide
    )


def swap_lanes(tiles):
    lane = lax.broadcasted_iota(jnp.int32, tiles[0].shape, len(tiles[0].shape) - 1)
    axis = len(tiles[0].shape) - 1
    low = lane % (2 * WIDTH) < WIDTH
    left = lane < 2 * WIDTH
    first = [None] * 4
    for a in range(2):
        one, two = tiles[a], tiles[a + 2]
        first[a] = jnp.where(left, one, pltpu.roll(two, 2 * WIDTH, axis))
        first[a + 2] = jnp.where(left, pltpu.roll(one, 2 * WIDTH, axis), two)
    second = [None] * 4
    for b in (0, 2):
        one, two = first[b], first[b + 1]
        second[b] = jnp.where(low, one, pltpu.roll(two, WIDTH, axis))
        second[b + 1] = jnp.where(low, pltpu.roll(one, LANES - WIDTH, axis), two)
    return second


def pick_lanes(tiles, which):
    axis = len(tiles[0].shape) - 1
    group = lax.broadcasted_iota(jnp.int32, tiles[0].shape, axis) // WIDTH
    result = None
    for g, tile in enumerate(tiles):
        distance = (g - which) * WIDTH % LANES
        moved = pltpu.roll(tile, distance, axis) if distance else tile
        result = moved if result is None else jnp.where(group == g, moved, result)
    return result


def cut_kernel(which, in_ref, out_ref):
    for part in range(2):
        tiles = [in_ref[part, g] for g in range(GROUPS)]
        if len(which) == 1:
            out_ref[0, part] = pick_lanes(tiles, which[0])
        else:
            tiles = swap_lanes(tiles)
            for index, q in enumerate(which):
                out_ref[index, part] = tiles[q]


def cut_columns(density, which, partner):
    rows = density.shape[2]
    step = min(rows, 128)
    return pl.pallas_call(
        functools.partial(cut_kernel, which),
        grid=(rows // step,),
        in_specs=[
            pl.BlockSpec(
                (2, GROUPS, step, LANES), lambda i: (0, 0, i, lax.axis_index("narrow") ^ partner)
            )
        ],
        out_specs=pl.BlockSpec((len(which), 2, step, LANES), lambda i: (0, 0, i, 0)),
        out_shape=jax.ShapeDtypeStruct((len(which), 2, rows, LANES), jnp.float32),
        compiler_params=params(),
        cost_estimate=pl.CostEstimate(
            flops=8 * rows * LANES * len(which),
            bytes_accessed=40 * rows * LANES,
            transcendentals=0,
        ),
        name="cut",
    )(density)


def place_kernel(order, *refs):
    inputs, out_ref = refs[:-1], refs[-1]
    device = lax.axis_index("narrow")
    for k in range(GROUPS):
        lanes = pl.ds(pl.multiple_of((device ^ k) * LANES, LANES), LANES)
        for part in range(2):
            tiles = [
                jnp.zeros(out_ref.shape[2:3] + (LANES,), jnp.float32)
                if spot is None
                else inputs[spot[0] * GROUPS + k][spot[1], part]
                for spot in order
            ]
            for g, value in enumerate(swap_lanes(tiles)):
                out_ref[part, g, :, lanes] = value


def add_kernel(which, *refs):
    inputs, so_far_ref, out_ref = refs[:4], refs[4], refs[5]
    device = lax.axis_index("narrow")
    group = lax.broadcasted_iota(jnp.int32, (out_ref.shape[2], LANES), 1) // WIDTH
    for k in range(GROUPS):
        lanes = pl.ds(pl.multiple_of((device ^ k) * LANES, LANES), LANES)
        for part in range(2):
            tile = inputs[k][0, part]
            for g in range(GROUPS):
                distance = (which - g) * WIDTH % LANES
                moved = pltpu.roll(tile, distance, 1) if distance else tile
                value = jnp.where(group == which, moved, so_far_ref[part, g, :, lanes])
                out_ref[part, g, :, lanes] = value


def place_columns(chunks, plan):
    specs, operands, order = [], [], [None] * GROUPS
    for which, chunk in zip(plan, chunks):
        if chunk is None:
            continue
        rows = chunk[0].shape[2]
        step = min(rows, 128)
        for index, q in enumerate(which):
            order[q] = (len(operands) // GROUPS, index)
        specs += [pl.BlockSpec((len(which), 2, step, LANES), lambda i: (0, 0, i, 0))] * GROUPS
        operands += list(chunk)
    shape = (2, GROUPS, rows, GROUPS * LANES)
    return pl.pallas_call(
        functools.partial(place_kernel, order),
        grid=(rows // step,),
        out_shape=jax.ShapeDtypeStruct(shape, jnp.float32),
        in_specs=specs,
        out_specs=pl.BlockSpec((2, GROUPS, step, GROUPS * LANES), lambda i: (0, 0, i, 0)),
        compiler_params=params(),
        cost_estimate=pl.CostEstimate(
            flops=64 * rows * LANES, bytes_accessed=128 * rows * LANES, transcendentals=0
        ),
        name="place",
    )(*operands)


def add_columns(chunk, which, so_far):
    rows = chunk[0].shape[2]
    step = min(rows, ADD_STEP)
    block = pl.BlockSpec((2, GROUPS, step, GROUPS * LANES), lambda i: (0, 0, i, 0))
    return pl.pallas_call(
        functools.partial(add_kernel, which),
        grid=(rows // step,),
        out_shape=jax.ShapeDtypeStruct(so_far.shape, jnp.float32),
        in_specs=[pl.BlockSpec((1, 2, step, LANES), lambda i: (0, 0, i, 0))] * GROUPS + [block],
        out_specs=block,
        input_output_aliases={GROUPS: 0},
        compiler_params=params(),
        cost_estimate=pl.CostEstimate(
            flops=64 * rows * LANES, bytes_accessed=128 * rows * LANES, transcendentals=0
        ),
        name="add",
    )(*chunk, so_far)


def fetch(sources, held, semaphores):
    copies = [
        pltpu.make_async_copy(source, there, semaphores.at[i])
        for i, (source, there) in enumerate(zip(sources, held))
    ]

    @pl.when(pl.program_id(0) == 0)
    def start():
        for copy in copies:
            copy.start()

    def wait(*which):
        @pl.when(pl.program_id(0) == 0)
        def finish_copies():
            for i in which:
                copies[i].wait()

    return wait


def lines_forward_kernel(rows, slot_ref, *refs):
    sources, inputs = refs[:4], refs[4:8]
    out_ref, first, second, head_ref, mix_ref, matrix_ref, turn_ref, semaphores = refs[8:]
    tile = 8
    wait = fetch(sources, (head_ref, mix_ref, matrix_ref, turn_ref), semaphores)
    wait(0)

    def step(index, carry):
        place = pl.ds(pl.multiple_of(index * tile, tile), tile)
        x = [(ref[0, 0, place, :], ref[0, 1, place, :]) for ref in inputs]
        even = [c_add(x[0], x[2]), c_add(x[1], x[3])]
        odd = [c_sub(x[0], x[2]), c_sub(x[1], x[3])]
        turned = (odd[1][1], -odd[1][0])
        values = [
            c_add(even[0], even[1]),
            c_sub(even[0], even[1]),
            c_add(odd[0], turned),
            c_sub(odd[0], turned),
        ]
        for k in range(4):
            twiddle = (head_ref[k, 0, place, :], head_ref[k, 1, place, :])
            real_part, imag_part = c_mul(values[k], twiddle)
            first[slot_ref[k], place, :LANES] = real_part
            first[slot_ref[k], place, LANES:] = imag_part
        return carry

    lax.fori_loop(0, rows // tile, step, 0)
    wait(1, 2, 3)
    dot = functools.partial(jnp.dot, preferred_element_type=jnp.float32)
    for k in range(4):
        value = first[k]
        high = value.astype(jnp.bfloat16)
        low = (value - high.astype(jnp.float32)).astype(jnp.bfloat16)
        value = dot(high, mix_ref[...]) + dot(low, mix_ref[...])
        real_part, imag_part = c_mul(
            (value[:, :LANES], value[:, LANES:]), (turn_ref[0], turn_ref[1])
        )
        second[:rows, k * LANES : (k + 1) * LANES] = real_part
        second[rows:, k * LANES : (k + 1) * LANES] = imag_part
    for side in range(2):
        lanes = slice(2 * side * LANES, 2 * (side + 1) * LANES)
        value = dot3(matrix_ref[0], matrix_ref[1], second[:, lanes], True)
        for k in range(2):
            for part in range(2):
                piece = value[part * rows : (part + 1) * rows, k * LANES : (k + 1) * LANES]
                out_ref[:, 0, part, 2 * side + k] = piece.reshape(rows // tile, tile, LANES)


def line_specs():
    return [pl.BlockSpec(memory_space=pltpu.SMEM)] + [pl.BlockSpec(memory_space=pl.ANY)] * 4


def line_scratch(rows, tables):
    return (
        [
            pltpu.VMEM((4, rows, 2 * LANES), jnp.float32),
            pltpu.VMEM((2 * rows, 4 * LANES), jnp.float32),
        ]
        + [pltpu.VMEM(table.shape, table.dtype) for table in tables]
        + [pltpu.SemaphoreType.DMA((len(tables),))]
    )


def lines_forward(pieces, slots, head, tables):
    count, _, rows, _ = pieces[0].shape
    places = rows // 8
    return pl.pallas_call(
        functools.partial(lines_forward_kernel, rows),
        grid=(count,),
        out_shape=jax.ShapeDtypeStruct((places, count, 2, 4, 8, LANES), jnp.float32),
        in_specs=line_specs()
        + [pl.BlockSpec((1, 2, rows, LANES), lambda i: (i, 0, 0, 0))] * 4,
        out_specs=pl.BlockSpec((places, 1, 2, 4, 8, LANES), lambda i: (0, i, 0, 0, 0, 0)),
        scratch_shapes=line_scratch(rows, (head, *tables)),
        compiler_params=params(),
        cost_estimate=pl.CostEstimate(
            flops=LINE_WEIGHT * rows * rows * LANES * count,
            bytes_accessed=64 * rows * LANES * count,
            transcendentals=0,
        ),
        name="lines_forward",
    )(slots, head, *tables, *pieces)


def lines_inverse_kernel(rows, slot_ref, *refs):
    sources, in_ref, outputs = refs[:4], refs[4], refs[5:9]
    first, second, head_ref, mix_ref, matrix_ref, turn_ref, semaphores = refs[9:]
    tile = 8
    wait = fetch(sources, (head_ref, mix_ref, matrix_ref, turn_ref), semaphores)
    for k in range(4):
        for part in range(2):
            piece = in_ref[:, 0, part, k].reshape(rows, LANES)
            second[part * rows : (part + 1) * rows, k * LANES : (k + 1) * LANES] = piece
    dot = functools.partial(jnp.dot, preferred_element_type=jnp.float32)
    wait(2)
    for side in range(2):
        lanes = slice(2 * side * LANES, 2 * (side + 1) * LANES)
        second[:, lanes] = dot3(matrix_ref[0], matrix_ref[1], second[:, lanes], True)
    wait(0, 1, 3)
    for k in range(4):
        lanes = slice(k * LANES, (k + 1) * LANES)
        real_part, imag_part = c_mul(
            (second[:rows, lanes], second[rows:, lanes]), (turn_ref[0], -turn_ref[1])
        )
        value = jnp.concatenate([real_part, imag_part], axis=1)
        high = value.astype(jnp.bfloat16)
        low = (value - high.astype(jnp.float32)).astype(jnp.bfloat16)
        first[k] = dot(high, mix_ref[...]) + dot(low, mix_ref[...])

    def step(index, carry):
        place = pl.ds(pl.multiple_of(index * tile, tile), tile)
        values = []
        for k in range(4):
            value = (first[slot_ref[k], place, :LANES], first[slot_ref[k], place, LANES:])
            values.append(c_mul(value, (head_ref[k, 0, place, :], -head_ref[k, 1, place, :])))
        even = [c_add(values[0], values[1]), c_sub(values[0], values[1])]
        differ = c_sub(values[2], values[3])
        odd = [c_add(values[2], values[3]), (-differ[1], differ[0])]
        for k in range(2):
            for side, value in enumerate((c_add(even[k], odd[k]), c_sub(even[k], odd[k]))):
                outputs[k + 2 * side][0, 0, place, :] = value[0]
                outputs[k + 2 * side][0, 1, place, :] = value[1]
        return carry

    lax.fori_loop(0, rows // tile, step, 0)


def lines_inverse(blocks, slots, head, tables):
    places, count = blocks.shape[:2]
    rows = places * 8
    return pl.pallas_call(
        functools.partial(lines_inverse_kernel, rows),
        grid=(count,),
        out_shape=[jax.ShapeDtypeStruct((count, 2, rows, LANES), jnp.float32)] * 4,
        in_specs=line_specs()
        + [pl.BlockSpec((places, 1, 2, 4, 8, LANES), lambda i: (0, i, 0, 0, 0, 0))],
        out_specs=[pl.BlockSpec((1, 2, rows, LANES), lambda i: (i, 0, 0, 0))] * 4,
        scratch_shapes=line_scratch(rows, (head, *tables)),
        compiler_params=params(),
        cost_estimate=pl.CostEstimate(
            flops=BACK_WEIGHT * rows * rows * LANES * count,
            bytes_accessed=64 * rows * LANES * count,
            transcendentals=0,
        ),
        name="lines_inverse",
    )(slots, head, *tables, blocks)


def row_filter_kernel(plan, slots, forward_ref, inverse_ref, turn_ref, green_ref, *refs):
    inputs, outputs = refs[: len(plan)], refs[len(plan) : 2 * len(plan)]
    x, held = refs[-2:]
    chunks = 4
    inner = slots * chunks
    modes = inner * GROUPS
    rows = 8
    where = {q: (c, index) for c, which in enumerate(plan) for index, q in enumerate(which)}

    for q in range(GROUPS):
        c, index = where[q]
        columns = []
        for n in range(chunks):
            values = [
                (inputs[c][n * slots + k, index, 0, 0], inputs[c][n * slots + k, index, 1, 0])
                for k in range(slots)
            ]
            values = small_dft(values, -1)
            columns.append([c_const(values[a], a * n, inner, -1) for a in range(slots)])
        for a in range(slots):
            values = small_dft([columns[n][a] for n in range(chunks)], -1)
            for b in range(chunks):
                mode = a + slots * b
                x[q, mode, 0], x[q, mode, 1] = c_const(values[b], q * mode, modes, -1)

    def before(mode, carry):
        values = [(x[q, mode, 0], x[q, mode, 1]) for q in range(GROUPS)]
        values = small_dft(values, -1)
        for e in range(GROUPS):
            where_to = mode + inner * e
            twiddle = (turn_ref[0, pl.ds(where_to, 1), :], turn_ref[1, pl.ds(where_to, 1), :])
            held[where_to, :, :LANES], held[where_to, :, LANES:] = c_mul(values[e], twiddle)
        return carry

    lax.fori_loop(0, inner, before, 0, unroll=16)

    group = 256 // rows

    def middle(index, carry):
        mode = pl.multiple_of(index * group, group)
        value = held[pl.ds(mode, group)].reshape(group * rows, 2 * LANES)
        value = dot3(forward_ref[0], forward_ref[1], value, False)
        green = green_ref[pl.ds(mode, group)].reshape(group * rows, LANES)
        value = value * jnp.concatenate([green, green], axis=1)
        value = dot3(inverse_ref[0], inverse_ref[1], value, False)
        held[pl.ds(mode, group)] = value.reshape(group, rows, 2 * LANES)
        return carry

    lax.fori_loop(0, modes // group, middle, 0, unroll=MIDDLE_UNROLL)

    def after_(mode, carry):
        values = []
        for e in range(GROUPS):
            where_from = mode + inner * e
            twiddle = (turn_ref[0, pl.ds(where_from, 1), :], -turn_ref[1, pl.ds(where_from, 1), :])
            values.append(c_mul((held[where_from, :, :LANES], held[where_from, :, LANES:]), twiddle))
        values = small_dft(values, 1)
        for q in range(GROUPS):
            x[q, mode, 0], x[q, mode, 1] = values[q]
        return carry

    lax.fori_loop(0, inner, after_, 0, unroll=16)

    for q in range(GROUPS):
        c, index = where[q]
        columns = []
        for a in range(slots):
            values = []
            for b in range(chunks):
                mode = a + slots * b
                values.append(c_const((x[q, mode, 0], x[q, mode, 1]), q * mode, modes, 1))
            columns.append(small_dft(values, 1))
        for n in range(chunks):
            values = [c_const(columns[a][n], a * n, inner, 1) for a in range(slots)]
            values = small_dft(values, 1)
            for k in range(slots):
                outputs[c][n * slots + k, index, 0, 0] = values[k][0]
                outputs[c][n * slots + k, index, 1, 0] = values[k][1]


def group_matrix(orient):
    index = np.arange(WIDTH)
    small = np.exp(orient * 2j * np.pi * (np.outer(index, index) % WIDTH) / WIDTH)
    whole = np.kron(np.eye(GROUPS), small)
    return np.stack(split_bf16(np.block([[whole.real, whole.imag], [-whole.imag, whole.real]])))


def row_filter(blocks, plan, turns, green, slots):
    sources = blocks[0].shape[0]
    modes = sources * GROUPS
    forward = jnp.asarray(group_matrix(-1))
    inverse = jnp.asarray(group_matrix(1))
    specs = [
        pl.BlockSpec((sources, len(which), 2, 1, 8, LANES), lambda i: (0, 0, 0, i, 0, 0))
        for which in plan
    ]
    return pl.pallas_call(
        functools.partial(row_filter_kernel, plan, slots),
        grid=(4,),
        out_shape=[jax.ShapeDtypeStruct(block.shape, jnp.float32) for block in blocks],
        in_specs=[
            whole_spec(forward.shape),
            whole_spec(inverse.shape),
            whole_spec(turns.shape),
            pl.BlockSpec((modes, 8, LANES), lambda i: (0, i, 0)),
        ]
        + specs,
        out_specs=specs,
        scratch_shapes=[
            pltpu.VMEM((GROUPS, sources, 2, 8, LANES), jnp.float32),
            pltpu.VMEM((modes, 8, 2 * LANES), jnp.float32),
        ],
        compiler_params=params(),
        cost_estimate=pl.CostEstimate(
            flops=96 * LANES * LANES * modes * 32,
            bytes_accessed=20 * modes * 32 * LANES,
            transcendentals=0,
        ),
        name="row_filter",
    )(forward, inverse, turns, green, *blocks)


def four_plane(density, plane_wave):
    narrow, wide = lax.axis_size("narrow"), lax.axis_size("wide")
    device, place = lax.axis_index("narrow"), lax.axis_index("wide")
    z_local, x_local = density.shape[1:]
    total_z, total_x = z_local * narrow, x_local * wide
    rows = z_local // GROUPS
    modes = narrow * wide * GROUPS
    partners = np.arange(4)

    own = np.arange(4)
    slots = np.stack([0 * own, 2 + 0 * own, 1 + 2 * (own % 2), 3 - 2 * (own % 2)], axis=1)
    sign_low, sign_high = 1.0 - 2.0 * (own % 2), 1.0 - 2.0 * (own // 2)
    phase = np.stack(
        [
            np.ones(4),
            sign_low,
            sign_high * np.where(own % 2 == 0, 1, 1j),
            sign_high * np.where(own % 2 == 0, 1, -1j),
        ],
        axis=1,
    )
    group = np.repeat(np.arange(GROUPS), WIDTH)
    depth = group[None, :] * rows + np.arange(rows)[:, None]
    angle = 2.0 * np.pi * (slots[:, :, None, None] * depth % total_z) / total_z
    head = phase[:, :, None, None] * np.exp(-1j * angle)
    head = pick(np.stack([head.real, head.imag], axis=2).astype(np.float32), device)
    slots = pick(slots.astype(np.int32), device)
    turns = np.moveaxis(turn(group[None, :] * np.arange(rows)[:, None], GROUPS * rows), 2, 0)
    four = np.exp(-2j * np.pi * (np.outer(partners, partners) % 4) / 4)
    mixing = np.round(np.kron(four, np.eye(WIDTH)))
    ahead = np.block([[mixing.real, mixing.imag], [-mixing.imag, mixing.real]])
    backward = np.block([[mixing.real, -mixing.imag], [mixing.imag, mixing.real]])
    way = lax.optimization_barrier(jnp.arange(2, dtype=jnp.int32))
    tables = [
        pick(np.stack([one, two]), way[0])
        for one, two in (
            (ahead.astype(jnp.bfloat16), backward.astype(jnp.bfloat16)),
            (dft_matrix(rows, -1, True), dft_matrix(rows, 1, True)),
            (turns, turns),
        )
    ]
    tables_back = (
        jnp.asarray(backward.astype(jnp.bfloat16)),
        jnp.asarray(dft_matrix(rows, 1, True)),
        jnp.asarray(turns),
    )
    cell = np.tile(np.arange(WIDTH), GROUPS)
    x_turns = turn(np.arange(modes)[:, None] * cell[None, :], total_x)
    x_turns = jnp.asarray(np.moveaxis(x_turns, 2, 0))
    residue = np.arange(4)[:, None, None] + 16 * np.arange(8)[:, None] + 4 * group
    wave_z = jnp.asarray(residue.reshape(32, LANES).astype(np.int32))
    wave_z = wave_z + 16 * 8 * (device * wide + place)
    wave_x = np.arange(modes)[:, None, None] + modes * cell
    signed_x = jnp.asarray(np.where(wave_x < total_x // 2, wave_x, wave_x - total_x).astype(np.int32))
    green = green_of(plane_wave, wave_z[None], signed_x, total_z, total_x)

    source = density.reshape(2, GROUPS, rows, x_local)

    def send(pieces):
        moved = {k: swap(pieces[k], "narrow", k) for k in (1, 2, 3)}
        return [pieces[0], moved[1], moved[2], moved[3]]

    def trade_all(blocks):
        return lax.all_to_all(blocks, ("narrow", "wide"), 0, 0, tiled=True)

    arrived, got, made = [], None, []
    for c, which in enumerate(PLAN):
        wanted = after(source, made[c - 2]) if c >= 2 else source
        pieces = [cut_columns(wanted, which, k) for k in range(4)]
        got = send(pieces if got is None else after(pieces, got))
        made.append(lines_forward(got, slots, head, tables))
        arrived.append(trade_all(made[c]))

    filtered = row_filter(arrived, PLAN, x_turns, green, wide)

    back, blocks, made = [None] * len(PLAN), None, []
    for c in reversed(range(len(PLAN))):
        wanted = filtered[c] if blocks is None else after(filtered[c], blocks)
        if len(made) >= 2:
            wanted = after(wanted, made[-2])
        blocks = trade_all(wanted)
        made.append(lines_inverse(blocks, slots, head, tables_back))
        back[c] = send(made[-1] if c + 1 == len(PLAN) else after(made[-1], back[c + 1]))
    if len(PLAN[0]) > 1:
        return place_columns(back, PLAN).reshape(density.shape)
    so_far = place_columns([None] + back[1:], PLAN)
    return add_columns(back[0], PLAN[0][0], so_far).reshape(density.shape)


def plane(density, plane_wave):
    narrow, wide = lax.axis_size("narrow"), lax.axis_size("wide")
    bits = narrow.bit_length() - 1
    device, place = lax.axis_index("narrow"), lax.axis_index("wide")
    z_local, x_local = density.shape[1:]
    total_z, total_x = z_local * narrow, x_local * wide
    rows = z_local // wide
    chunks = x_local // LANES
    modes = wide * chunks
    four = narrow == 4
    low_wave = device if four else reversed_index(device, bits)
    parts = 2 if four else 1
    half = z_local // parts

    waves = [d if four else int(format(d, "b").zfill(bits)[::-1], 2) for d in range(narrow)]
    waves = np.array(waves)
    block = waves[:, None] + narrow * np.arange(wide)
    turns = turn(np.arange(rows) * block[..., None], total_z)
    turns = pick(np.moveaxis(turns, 3, 2), device)
    turns = jnp.broadcast_to(turns[..., None], (wide, 2, rows, LANES))
    head = np.arange(wide) * waves[:, None]
    inner = pick(turn(-head, narrow * wide), device)
    if four:
        give, keep = narrow_terms(1, narrow * wide)
        outer = np.repeat(keep, wide // 2, axis=1) + head[..., None]
        outer = pick(turn(outer, narrow * wide).reshape(narrow, wide, 6), device)
        give = pick(turn(give, narrow * wide).reshape(narrow, 2, 4), device)
        give_back, keep = narrow_terms(-1, narrow * wide)
        give_back = pick(turn(give_back, narrow * wide).reshape(narrow, 2, 4), device)
        last = pick(turn(keep, narrow * wide).reshape(narrow, 2, 6), device)
    else:
        outer = pick(turn(head, narrow * wide), device)
        last = jnp.array([[1.0, 0.0]], jnp.float32)
    x_turns = turn(np.arange(modes)[:, None] * np.arange(LANES)[None, :], total_x)
    x_turns = jnp.asarray(np.moveaxis(x_turns, 2, 0))
    line = jnp.arange(rows, dtype=jnp.int32)
    wave_z = low_wave + narrow * (place + wide * line)
    green = green_values(plane_wave, wave_z, modes, total_z, total_x)

    def part_spec(part, chunk):
        def make(steps):
            first = part * steps
            return pl.BlockSpec((2, half // steps, LANES), lambda i: (0, first + i, chunk))

        return make

    def own_spec(steps):
        return pl.BlockSpec((2, half // steps, LANES), lambda i: (0, i, 0))

    def cut(c, source):
        columns = slice(c * LANES, (c + 1) * LANES)
        return [source[:, p * half : (p + 1) * half, columns] for p in range(parts)]

    def first_swap(pieces):
        return [swap(piece, "narrow", first) for piece, first in zip(pieces, FIRSTS)]

    def second_swap(pieces):
        return [swap(piece, "narrow", 3 - first) for piece, first in zip(pieces, FIRSTS)]

    arrived, pieces = [], [cut(0, density)]
    rest = after(density, pieces[0])
    pieces += [cut(c, rest) for c in range(1, chunks)]
    partner = received = sent = None
    for c in range(chunks):
        if four:
            if c == 0:
                partner = first_swap(pieces[0])
            else:
                partner = first_swap(after(pieces[c], received))
            ready = after(partner, sent) if c else partner
            mixed = mix(
                [[(density, part_spec(p, c)), (ready[p], own_spec)] for p in range(parts)], give, half
            )
            received = second_swap(mixed)
            terms = [
                [
                    (density, part_spec(p, c)(1)),
                    (partner[p], own_spec(1)),
                    (received[p], own_spec(1)),
                ]
                for p in range(parts)
            ]
        else:
            terms = [[(butterfly_forward(piece, device, bits), own_spec(1))] for piece in pieces[c]]
        sent = z_forward(terms, outer, turns, wide, rows)
        arrived.append(trade(sent))

    filtered = x_filter(arrived, x_turns, green)

    result, done = None, []
    for c in range(chunks):
        blocks = after(filtered[c], done[c - 2]) if four and c >= 2 else filtered[c]
        pieces = z_inverse(trade(blocks), inner, turns, parts)
        if four:
            partner = first_swap(pieces)
            ready = after(partner, received) if c else partner
            mixed = mix(
                [[(pieces[p], own_spec), (ready[p], own_spec)] for p in range(parts)], give_back, half
            )
            done.append(mixed)
            received = second_swap(mixed)
            pieces = [[pieces[p], partner[p], received[p]] for p in range(parts)]
        else:
            pieces = [[butterfly_inverse(piece, device, bits)] for piece in pieces]
        result = finish(pieces, last, c, chunks, result)
    return result.reshape(density.shape)


def shards(density, plane_wave):
    sizes = lax.axis_size("narrow"), lax.axis_size("wide")
    one = four_plane if fits(*sizes, *density.shape[2:]) else plane
    planes = [one(density[:, y], plane_wave[y]) for y in range(density.shape[1])]
    return jnp.stack(planes, axis=1)


def solution(mesh):
    in_specs = (P(None, None, "narrow", "wide"), P())
    out_specs = P(None, None, "narrow", "wide")
    return jax.shard_map(shards, mesh=mesh, in_specs=in_specs, out_specs=out_specs, check_vma=False)
```
